128 devices in a mesh: blk: 64 (over x, y, z_lo, core), rep: 2 (over z_hi).
Axes of the slice: x: 4, y: 4, z: 4 (z_hi: 2, z_lo: 2; z = z_hi * 2 + z_lo), core: 2. Of those that a mesh axis runs over, the one named last changes fastest.
Arguments:
- query_in: bfloat16 [32768, 1024], P(('blk', 'rep')), may hold values from -12 to 12
- doc_in: bfloat16 [32768, 1024], P(('blk', 'rep')), may hold values from -12 to 12
- cluster: int32 [32768], P(('blk', 'rep')), may hold values from 0 to 127, never falling along the last dimension, each value on 1 to 384 neighbouring positions
- gain: float32 [1024], replicated, may hold values from 0.5 to 1.5
- w_in: bfloat16 [1024, 4096], P(None, 'rep'), may hold values from -0.1875 to 0.1875
- w_out: bfloat16 [4096, 1024], P('rep'), may hold values from -0.09375 to 0.09375
Outputs:
- loss: float32 [], replicated
- grad_down: float32 [4096, 1024], P('rep', 'blk')
- grad_gain: float32 [1024], replicated
- grad_query_in: bfloat16 [32768, 1024], P(('blk', 'rep'))
- grad_doc_in: bfloat16 [32768, 1024], P(('blk', 'rep'))
The draws below stay inside these ranges and needn't reach their ends.
Inputs may be any that keep to these rules, and one draw needn't show every extreme that they name: Never falls along the pairs; each cluster holds 1 to 384 consecutive pairs, one exactly 384.
All inputs are finite; a program needn't handle non-finite values.
Results may differ from the reference program's by a relative error of at most 0.015.
Values may be sent and summed in bfloat16 or wider, within the bound.
A program may use at most 128 MiB of HBM per device.

```python
import math
import jax
import jax.numpy as jnp
import numpy as np
from jax import lax

D = 1024
FF = 4096
PAIR_DEV = 256
BAND = 2
PAIRS = 32768
CLUSTERS = 128
CMOST = 384
N_BLK = 64
N_REP = 2


def doc_values(key, low, high, lean):
    base_draw = jax.random.normal(key, (PAIRS, D), jnp.float32)
    log_scale = jax.random.uniform(jax.random.fold_in(key, 12), (PAIRS, 1), jnp.float32, math.log(low), math.log(high))
    drawn = base_draw * jnp.exp(log_scale)
    row_ids = jnp.arange(PAIRS)[:, None]
    shift_rows = PAIR_DEV * N_REP + 1
    twin_rows = jnp.roll(drawn, shift_rows, axis=0)
    marked = ((row_ids - shift_rows) % 64 == 0) & (lean > 0.0)
    return jnp.clip(jnp.where(marked, twin_rows, drawn), -12.0, 12.0)


def draw_doc_in(key, part):
    return doc_values(key, 1.0, 1.0, 0.0).astype(jnp.bfloat16)


def draw_query_in(key, part):
    own_key = jax.random.fold_in(key, 3)
    return jnp.clip(jax.random.normal(own_key, (PAIRS, D), jnp.float32), -12.0, 12.0).astype(jnp.bfloat16)


def block_scale(key, shape, pieces, low, largest):
    factor_of = 1.0
    for position, parts in pieces:
        steps = jax.random.uniform(jax.random.fold_in(jax.random.fold_in(key, 6), position), (parts,), jnp.float32, low / len(pieces), largest / len(pieces))
        factor_of = factor_of * jnp.repeat(jnp.exp(steps), shape[position] // parts).reshape((-1,) + (1,) * (len(shape) - 1 - position))
    return factor_of


def split_up(count, total, reach, skew):
    loads = [(1 << 20) // math.isqrt(rank ** skew) + 1 for rank in range(2, count + 1)]
    rest, holding = total - reach - (count - 1), [1] * (count - 1)
    while rest > 0:
        movable = [i for i in range(count - 1) if holding[i] < reach]
        pool, budget = sum([loads[i] for i in movable]), rest
        for i in movable:
            extra = min(reach - holding[i], max(1, budget * loads[i] // pool), rest)
            holding[i] = holding[i] + extra
            rest = rest - extra
    return np.array([reach] + holding)


def ragged_sizes(stream_key, amount, total, reach, skew):
    if amount == 2:
        one = jax.random.randint(stream_key, (), max(1, total - reach), min(reach, total - 1) + 1)
        return jnp.stack([one, total - one])
    sizes = jnp.asarray(split_up(amount, total, reach, skew), jnp.int32)
    twos = (amount - 1) // 2
    donor, receiver = sizes[1:1 + 2 * twos:2], sizes[2:2 + 2 * twos:2]
    margin = jnp.minimum(donor - 1, reach - receiver)
    shifted = jax.random.randint(jax.random.fold_in(stream_key, 1), (twos,), 0, 1 << 20) % (margin + 1)
    sizes = sizes.at[1:1 + 2 * twos:2].set(donor - shifted).at[2:2 + 2 * twos:2].set(receiver + shifted)
    return sizes[jax.random.permutation(jax.random.fold_in(stream_key, 2), amount)]


def normal_values(key, shape, scale, bound, shards=(), held_as=jnp.bfloat16):
    values = jax.random.normal(key, shape, jnp.float32) * scale
    if len(shards) > 0:
        values = block_scale(key, shape, shards, -0.22, 0.18) * values
    return jnp.clip(values, min=-bound, max=bound).astype(held_as)


def setup_inputs(seed: int = 0) -> dict:
    streams_of = jax.random.split(jax.random.key(seed), 7)
    return {
        "query_in": draw_query_in(jax.random.fold_in(streams_of[6], 71), 0),
        "doc_in": draw_doc_in(jax.random.fold_in(streams_of[6], 71), 0),
        "cluster": jnp.searchsorted(jnp.cumsum(ragged_sizes(streams_of[2], CLUSTERS, PAIRS, CMOST, 0)), jnp.arange(PAIRS), side="right").astype(jnp.int32),
        "gain": jnp.clip(1.0 + 0.1 * jax.random.normal(streams_of[3], (D,), jnp.float32), 0.5, 1.5),
        "w_in": normal_values(streams_of[4], (D, FF), D ** -0.5, 0.1875, ((1, 2),)),
        "w_out": normal_values(streams_of[5], (FF, D), FF ** -0.5, 0.09375, ((0, 2),)),
    }


epsilon = 1e-06

def forward_rows(rows, gain, w_in, w_out):
    values = rows.astype(jnp.float32)
    inv_rms = lax.rsqrt(lax.optimization_barrier(jnp.mean(values * values, axis=-1, keepdims=True)) + epsilon)
    unit_rows = values * inv_rms
    normed = (unit_rows * gain).astype(jnp.bfloat16)
    pre_act = jnp.dot(normed, w_in, preferred_element_type=jnp.float32)
    hidden = jax.nn.gelu(pre_act, approximate=True).astype(jnp.bfloat16)
    mixed_out = jnp.dot(hidden, w_out, preferred_element_type=jnp.float32)
    embedded = (values + mixed_out).astype(jnp.bfloat16)
    return (embedded, values, inv_rms, unit_rows, pre_act, hidden)

def backward_rows(rows, upstream, gain, w_in, w_out):
    embedded, values, inv_rms, unit_rows, pre_act, hidden = forward_rows(rows, gain, w_in, w_out)
    g_act = lax.dot_general(upstream, w_out, (((1,), (1,)), ((), ())), preferred_element_type=jnp.float32)
    g_pre = jax.vjp(lambda p: jax.nn.gelu(p, approximate=True), pre_act)[1](g_act)[0].astype(jnp.bfloat16)
    g_norm = lax.dot_general(g_pre, w_in, (((1,), (1,)), ((), ())), preferred_element_type=jnp.float32)
    gain_term = lax.optimization_barrier(jnp.sum(g_norm * unit_rows, axis=0))
    d_unit = g_norm * gain
    d_values = inv_rms * (d_unit - unit_rows * lax.optimization_barrier(jnp.mean(d_unit * unit_rows, axis=-1, keepdims=True)))
    grad_rows = (upstream.astype(jnp.float32) + d_values).astype(jnp.bfloat16)
    down_term = lax.dot_general(hidden, upstream, (((0,), (0,)), ((), ())), preferred_element_type=jnp.float32)
    return (grad_rows, down_term, gain_term)

def shard_scores(query_emb, band_docs, query_cluster, band_cluster, positive):
    inv_root = 1.0 / math.sqrt(query_emb.shape[1])
    scores = lax.dot_general(query_emb, band_docs, (((1,), (1,)), ((), ())), preferred_element_type=jnp.float32) * inv_root
    columns = jnp.arange(band_docs.shape[0], dtype=jnp.int32)[None, :]
    is_positive = columns == positive[:, None]
    allowed = (band_cluster[None, :] != query_cluster[:, None]) | is_positive
    masked = jnp.where(allowed, scores, -jnp.inf)
    row_max = lax.optimization_barrier(jnp.max(masked, axis=1, keepdims=True))
    log_total = row_max + jnp.log(lax.optimization_barrier(jnp.sum(jnp.exp(masked - row_max), axis=1, keepdims=True)))
    positive_score = lax.optimization_barrier(jnp.sum(jnp.where(is_positive, scores, 0.0), axis=1))
    loss_part = jnp.sum(log_total[:, 0] - positive_score)
    weights = (jnp.exp(masked - log_total) - is_positive.astype(jnp.float32)).astype(jnp.bfloat16)
    return (weights, loss_part)

def reference(query_in, doc_in, cluster, gain, w_in, w_out):
    shard_rows = PAIR_DEV * N_REP
    inv_root = 1.0 / math.sqrt(D)

    def embed_rows(row_block):
        return forward_rows(row_block, gain, w_in, w_out)[0]
    query_blocks = query_in.reshape(N_BLK, shard_rows, D)
    doc_blocks = doc_in.reshape(N_BLK, shard_rows, D)
    query_emb = lax.map(embed_rows, query_blocks)
    doc_emb = lax.map(embed_rows, doc_blocks)
    groups = cluster.reshape(N_BLK, shard_rows)
    offsets = jnp.arange(-BAND, BAND + 1, dtype=jnp.int32)
    positive = BAND * shard_rows + jnp.arange(shard_rows, dtype=jnp.int32)

    def weights_of(b):
        band_index = (b + offsets) % N_BLK
        band_docs = doc_emb[band_index].reshape(-1, D)
        band_cluster = groups[band_index].reshape(-1)
        weights, loss_part = shard_scores(query_emb[b], band_docs, groups[b], band_cluster, positive)
        return (weights, loss_part, band_docs)

    def query_side(b):
        weights, loss_part, band_docs = weights_of(b)
        query_grad = (jnp.dot(weights, band_docs, preferred_element_type=jnp.float32) * inv_root).astype(jnp.bfloat16)
        return (query_grad, loss_part)
    shard_ids = jnp.arange(N_BLK, dtype=jnp.int32)
    query_grad, losses = lax.map(query_side, shard_ids)

    def doc_side(c):
        summed = jnp.zeros((shard_rows, D), jnp.float32)
        for m in range(2 * BAND + 1):
            b = (c - (m - BAND)) % N_BLK
            weights = weights_of(b)[0]
            column_block = weights[:, m * shard_rows:(m + 1) * shard_rows]
            queries = query_emb[b]
            for r in range(N_REP):
                part_bf = (lax.dot_general(column_block[r * PAIR_DEV:(r + 1) * PAIR_DEV], queries[r * PAIR_DEV:(r + 1) * PAIR_DEV], (((0,), (0,)), ((), ())), preferred_element_type=jnp.float32) * inv_root).astype(jnp.bfloat16)
                summed = summed + lax.optimization_barrier(part_bf).astype(jnp.float32)
        return summed.astype(jnp.bfloat16)
    doc_grad = lax.map(doc_side, shard_ids)
    rows_all = jnp.concatenate([query_blocks, doc_blocks], axis=0)
    upstream_all = jnp.concatenate([query_grad, doc_grad], axis=0)

    def layer_step(carry, items):
        grad_rows, down_term, gain_term = backward_rows(items[0], items[1], gain, w_in, w_out)
        return ((carry[0] + down_term, carry[1] + gain_term), grad_rows)
    start = (jnp.zeros((FF, D), jnp.float32), jnp.zeros((D,), jnp.float32))
    (grad_down, grad_gain), grad_rows = lax.scan(layer_step, start, (rows_all, upstream_all))
    grad_query_in = grad_rows[:N_BLK].reshape(PAIRS, D)
    grad_doc_in = grad_rows[N_BLK:].reshape(PAIRS, D)
    loss = jnp.sum(losses) / PAIRS
    return (loss, grad_down, grad_gain, grad_query_in, grad_doc_in)
```

```python
import math

import jax
import jax.numpy as jnp
from jax import lax
from jax.experimental import pallas as pl
from jax.experimental.pallas import tpu as pltpu
from jax.sharding import PartitionSpec as P

MESH = pl.DeviceIdType.MESH
MIB = 2**20
NX, NY, NZ, NC = 4, 4, 2, 2
NBLK = NX * NY * NZ * NC
RING = NX
EPSILON = 1e-06
SLOTS = 10
OWN = 4


def coords():
    b = lax.axis_index("blk")
    r = lax.axis_index("rep")
    return b // (NY * NZ * NC), (b // (NZ * NC)) % NY, (b // NC) % NZ, b % NC, r


def device(x, y, zl, c, r):
    return {"blk": ((x * NY + y) * NZ + zl) * NC + c, "rep": r}


def wrap(v, n):
    return lax.rem(v + n, n)


def greet(peers):
    barrier = pltpu.get_barrier_semaphore()
    for peer in peers:
        pl.semaphore_signal(barrier, inc=1, device_id=peer, device_id_type=MESH)
    pl.semaphore_wait(barrier, len(peers))


def remote(src, dst, send, recv, peer):
    return pltpu.make_async_remote_copy(
        src_ref=src,
        dst_ref=dst,
        send_sem=send,
        recv_sem=recv,
        device_id=peer,
        device_id_type=MESH,
    )


WBLK = 256
W_CHUNKS = 8


def weight_view(in_ref, out_ref, block, chunk):
    if chunk < W_CHUNKS // 2:
        rows = in_ref.shape[0] // (W_CHUNKS // 2)
        return in_ref.at[
            pl.ds(chunk * rows, rows), pl.ds(pl.multiple_of(block * WBLK, WBLK), WBLK)
        ]
    rows = WBLK // (W_CHUNKS // 2)
    first = block * WBLK + (chunk - W_CHUNKS // 2) * rows
    return out_ref.at[pl.ds(pl.multiple_of(first, rows), rows)]


def weights_kernel(win, wout, oin, oout, send, recv):
    x, y, zl, c, r = coords()
    cross = device(x, y, 1 - zl, c, 1 - r)
    near = device(x, y, 1 - zl, c, r)
    ahead = device(wrap(x + 1, NX), y, zl, c, r)
    behind = device(wrap(x - 1, NX), y, zl, c, r)
    sibling = device(x, y, zl, 1 - c, r)
    greet([cross, near, ahead, behind, sibling])
    color = lax.rem(x + 2 * zl, 4)

    def block_of(shift):
        return 2 * lax.rem(color + shift, 4) + c

    def copy(flow, block, chunk, peer, source=None):
        src = weight_view(*(source or (oin, oout)), block, chunk)
        dst = weight_view(oin, oout, block, chunk)
        return remote(src, dst, send.at[flow, chunk], recv.at[flow, chunk], peer)

    started = []

    def start(*args):
        op = copy(*args)
        op.start()
        started.append(op)

    for chunk in range(W_CHUNKS):
        start(0, block_of(2), chunk, cross, (win, wout))
    mine = block_of(0)
    for chunk in range(W_CHUNKS):
        copy(0, mine, chunk, cross).wait_recv()
        start(1, mine, chunk, ahead)
        start(2, mine, chunk, behind)
        start(3, mine, chunk, near)
        start(4, mine, chunk, sibling)
        if chunk:
            pass_on(copy, start, block_of, chunk - 1, (behind, ahead, near), sibling)
    pass_on(copy, start, block_of, W_CHUNKS - 1, (behind, ahead, near), sibling)
    for chunk in range(W_CHUNKS):
        for k in range(4):
            other = 2 * lax.rem(color + k, 4) + (1 - c)
            copy(4 + k, other, chunk, sibling).wait_recv()
    for op in started:
        op.wait_send()


def pass_on(copy, start, block_of, chunk, peers, sibling):
    for flow, shift, k in ((1, 3, 3), (2, 1, 1), (3, 2, 2)):
        block = block_of(shift)
        copy(flow, block, chunk, peers[flow - 1]).wait_recv()
        start(4 + k, block, chunk, sibling)


def gather_weights(w_in, w_out):
    return pl.pallas_call(
        weights_kernel,
        out_shape=(
            jax.ShapeDtypeStruct(w_in.shape, w_in.dtype),
            jax.ShapeDtypeStruct(w_out.shape, w_out.dtype),
        ),
        in_specs=[pl.BlockSpec(memory_space=pl.ANY)] * 2,
        out_specs=[pl.BlockSpec(memory_space=pl.ANY)] * 2,
        scratch_shapes=[pltpu.SemaphoreType.DMA((8, W_CHUNKS))] * 2,
        compiler_params=pltpu.CompilerParams(collective_id=0, has_side_effects=True),
        name="gather_weights",
    )(w_in, w_out)


B_CHUNKS = 5


def band_kernel(docs, tags, queries, gd, gx, gq, send, recv, local):
    x, y, zl, c, r = coords()
    b = lax.axis_index("blk")
    cross = device(x, y, 1 - zl, c, 1 - r)
    near = device(x, y, 1 - zl, c, r)
    sibling = device(x, y, zl, 1 - c, r)
    step = NZ * NC * (1 - 2 * zl)
    onward = {"blk": wrap(b + step, NBLK), "rep": r}
    source = {"blk": wrap(b - step, NBLK), "rep": r}
    greet([cross, near, sibling, onward, source])

    rows = docs.shape[0]
    half = rows // 2
    tag_rows = tags.shape[0]

    def view(slot, chunk):
        if chunk == 2:
            return gx.at[pl.ds(pl.multiple_of(slot * tag_rows, tag_rows), tag_rows)]
        ref = gd if chunk < 2 else gq
        first = slot * rows + (chunk % 3) * half
        return ref.at[pl.ds(pl.multiple_of(first, half), half)]

    def own(chunk):
        if chunk == 2:
            return tags
        ref = docs if chunk < 2 else queries
        return ref.at[pl.ds((chunk % 3) * half, half)]

    z_slot = 8 - 8 * zl
    far_slot = 8 * zl
    started = []

    def make(flow, chunk, src, dst_slot, peer):
        return remote(
            src, view(dst_slot, chunk), send.at[flow, chunk], recv.at[flow, chunk], peer
        )

    def start(*args):
        op = make(*args)
        op.start()
        started.append(op)

    def arrived(flow, chunk, slot):
        make(flow, chunk, view(slot, chunk), slot, near).wait_recv()

    def band_to_sibling(chunk):
        return [
            make(7 + k, chunk, view(8 - 8 * c + k, chunk), 6 - 4 * c + k, sibling)
            for k in range(2)
        ]

    order = (0, 1, 2, 3, 4)
    theirs = 8 * zl
    keep = []
    for chunk in order:
        start(0, chunk, own(chunk), theirs, near)
        start(1, chunk, own(chunk), theirs + 1, cross)
        start(5, chunk, own(chunk), 2 + 4 * c, sibling)
        op = pltpu.make_async_copy(own(chunk), view(OWN, chunk), local.at[chunk])
        op.start()
        keep.append(op)
    for place, chunk in enumerate(order):
        arrived(0, chunk, z_slot)
        start(3, chunk, view(z_slot, chunk), far_slot, onward)
        if place % 2 == 0:
            start(2, chunk, view(z_slot, chunk), OWN + 1, cross)
        arrived(1, chunk, z_slot + 1)
        start(4, chunk, view(z_slot + 1, chunk), far_slot + 1, onward)
        if place % 2 == 1:
            start(2, chunk, view(z_slot + 1, chunk), OWN + 1, near)

        @pl.when(c == zl)
        def _():
            for op in band_to_sibling(chunk):
                op.start()

    for chunk in order:
        arrived(2, chunk, OWN + 1)
        start(6, chunk, view(OWN + 1, chunk), 3 + 4 * c, sibling)
        arrived(3, chunk, far_slot)
        arrived(4, chunk, far_slot + 1)

        @pl.when(c != zl)
        def _():
            for op in band_to_sibling(chunk):
                op.start()

    for chunk in order:
        arrived(5, chunk, 6 - 4 * c)
        arrived(6, chunk, 7 - 4 * c)
        for op in band_to_sibling(chunk):
            op.wait_send()
        arrived(7, chunk, 2 + 4 * c)
        arrived(8, chunk, 3 + 4 * c)
        keep[chunk].wait()
    for op in started:
        op.wait_send()


def gather_band(docs, tags, queries):
    return pl.pallas_call(
        band_kernel,
        out_shape=[
            jax.ShapeDtypeStruct((SLOTS * v.shape[0], v.shape[1]), v.dtype)
            for v in (docs, tags, queries)
        ],
        in_specs=[pl.BlockSpec(memory_space=pl.ANY)] * 3,
        out_specs=[pl.BlockSpec(memory_space=pl.ANY)] * 3,
        scratch_shapes=[
            pltpu.SemaphoreType.DMA((9, B_CHUNKS)),
            pltpu.SemaphoreType.DMA((9, B_CHUNKS)),
            pltpu.SemaphoreType.DMA((B_CHUNKS,)),
        ],
        compiler_params=pltpu.CompilerParams(collective_id=1, has_side_effects=True),
        name="gather_band",
    )(docs, tags, queries)


def totals_kernel(mine, out, send, recv):
    b = lax.axis_index("blk")
    r = lax.axis_index("rep")
    peers = []
    for offset in range(-2, 3):
        for other in range(2):
            if offset or other:
                rep = 1 - r if other else r
                peers.append((offset, other, {"blk": wrap(b + offset, NBLK), "rep": rep}))
    greet([peer for _, _, peer in peers])
    ops = []
    for i, (offset, other, peer) in enumerate(peers):
        slot = (2 - offset) * 2 + other
        op = remote(mine, out.at[slot], send.at[i], recv.at[slot], peer)
        op.start()
        ops.append(op)
    out[OWN] = mine[...]
    for slot in range(SLOTS):
        if slot != OWN:
            remote(mine, out.at[slot], send.at[0], recv.at[slot], peers[0][2]).wait_recv()
    for op in ops:
        op.wait_send()


def exchange_totals(log_total):
    rows = log_total.shape[0]
    tile = jnp.pad(log_total.reshape(rows // 128, 128), ((0, 8 - rows // 128), (0, 0)))
    out = pl.pallas_call(
        totals_kernel,
        out_shape=jax.ShapeDtypeStruct((SLOTS, 8, 128), jnp.float32),
        in_specs=[pl.BlockSpec(memory_space=pltpu.VMEM)],
        out_specs=pl.BlockSpec(memory_space=pltpu.VMEM),
        scratch_shapes=[
            pltpu.SemaphoreType.DMA((SLOTS,)),
            pltpu.SemaphoreType.DMA((SLOTS,)),
        ],
        compiler_params=pltpu.CompilerParams(collective_id=2, has_side_effects=True),
        name="exchange_totals",
    )(tile)
    return out[:, : rows // 128].reshape(SLOTS * rows)


GROUP = 16


def reduce_kernel(own, oth, small, out, total, r1, a1, r2, a2, r3, a3, r4, s_buf, sems):
    x, y, zl, c, r = coords()
    hid = own.shape[-1]
    mid = hid // 2
    sibling = device(x, y, zl, 1 - c, r)
    xs = [device(wrap(x + k, NX), y, zl, c, r) for k in range(1, RING)]
    ys = [device(x, wrap(y + k, NY), zl, c, r) for k in range(1, RING)]
    zs = [device(x, y, 1 - zl, c, r), device(x, y, zl, c, 1 - r), device(x, y, 1 - zl, c, 1 - r)]
    greet([sibling] + xs + ys + zs)
    state = {"n": 0}
    ops = []

    def send(src, dst, peer):
        n = state["n"]
        state["n"] = n + 1
        op = remote(src, dst, sems.at[0, n], sems.at[1, n], peer)
        op.start()
        ops.append(op)
        return op

    s_buf[12] = small[...]

    wait1 = [
        send(own.at[:, 1 - c], r1.at[0], sibling),
        send(oth.at[:, 1 - c], r1.at[1], sibling),
        send(s_buf.at[12], s_buf.at[13], sibling),
    ]
    for op in wait1:
        op.wait_recv()
    s_buf[x] = s_buf[12] + s_buf[13]
    for h, ref in enumerate((own, oth)):

        def add1(g, _):
            a1[h, g] = (
                ref[g, c].astype(jnp.float32) + r1[h, g].astype(jnp.float32)
            ).astype(jnp.bfloat16)
            return 0

        lax.fori_loop(0, NX * NY * NZ, add1, 0)

    wait2 = []
    for k in range(1, RING):
        slot = RING - 1 - k
        tx = wrap(x + k, NX)
        ty = wrap(y + k, NY)
        for h in range(2):
            wait2.append(
                send(
                    a1.at[h, pl.ds(tx * NY * NZ, NY * NZ), :, pl.ds(0, mid)],
                    r2.at[0, slot, h],
                    xs[k - 1],
                )
            )
            for xx in range(NX):
                wait2.append(
                    send(
                        a1.at[h, pl.ds((xx * NY + ty) * NZ, NZ), :, pl.ds(mid, mid)],
                        r2.at[1, slot, h, pl.ds(xx * NZ, NZ)],
                        ys[k - 1],
                    )
                )
        wait2.append(send(s_buf.at[x], s_buf.at[x], xs[k - 1]))
    for op in wait2:
        op.wait_recv()
    s_buf[4 + y] = ((s_buf[0] + s_buf[1]) + s_buf[2]) + s_buf[3]
    for h in range(2):

        def add2(g, _):
            first = a1[h, x * NY * NZ + g, :, pl.ds(0, mid)].astype(jnp.float32)
            second = a1[h, (g // NZ * NY + y) * NZ + g % NZ, :, pl.ds(mid, mid)].astype(
                jnp.float32
            )
            for k in range(RING - 1):
                first += r2[0, k, h, g].astype(jnp.float32)
                second += r2[1, k, h, g].astype(jnp.float32)
            a2[0, h, g] = first.astype(jnp.bfloat16)
            a2[1, h, g] = second.astype(jnp.bfloat16)
            return 0

        lax.fori_loop(0, NY * NZ, add2, 0)

    wait3 = []
    for k in range(1, RING):
        slot = RING - 1 - k
        tx = wrap(x + k, NX)
        ty = wrap(y + k, NY)
        wait3.append(send(a2.at[0, :, pl.ds(ty * NZ, NZ)], r3.at[0, slot], ys[k - 1]))
        wait3.append(send(a2.at[1, :, pl.ds(tx * NZ, NZ)], r3.at[1, slot], xs[k - 1]))
        wait3.append(send(s_buf.at[4 + y], s_buf.at[4 + y], ys[k - 1]))
    for op in wait3:
        op.wait_recv()
    s_buf[8 + 2 * r + zl] = ((s_buf[4] + s_buf[5]) + s_buf[6]) + s_buf[7]
    for part in range(2):
        at = (y, x)[part]
        for h in range(2):
            for z in range(NZ):
                tot = a2[part, h, at * NZ + z].astype(jnp.float32)
                for k in range(RING - 1):
                    tot += r3[part, k, h, z].astype(jnp.float32)
                a3[h, z, :, part * mid : (part + 1) * mid] = tot.astype(jnp.bfloat16)

    mine = s_buf.at[8 + 2 * r + zl]
    wait4 = [
        send(a3.at[0, 1 - zl], r4.at[0], zs[0]),
        send(a3.at[1, zl], r4.at[1], zs[1]),
        send(a3.at[1, 1 - zl], r4.at[2], zs[2]),
    ] + [send(mine, mine, peer) for peer in zs]
    for op in wait4:
        op.wait_recv()
    out[...] = (
        (a3[0, zl].astype(jnp.float32) + r4[0].astype(jnp.float32))
        + (r4[1].astype(jnp.float32) + r4[2].astype(jnp.float32))
    )
    total[...] = (s_buf[8] + s_buf[9]) + (s_buf[10] + s_buf[11])
    for op in ops:
        op.wait_send()


def reduce_all(own, oth, small):
    hid = own.shape[1]
    groups = NX * NY * NZ
    shape = (groups, NC, GROUP, hid)
    n_copies = 3 + 3 * (2 + 2 * NX + 1) + 9 + 6
    bf = jnp.bfloat16
    return pl.pallas_call(
        reduce_kernel,
        out_shape=(
            jax.ShapeDtypeStruct((GROUP, hid), jnp.float32),
            jax.ShapeDtypeStruct(small.shape, jnp.float32),
        ),
        in_specs=[pl.BlockSpec(memory_space=pltpu.VMEM)] * 3,
        out_specs=[pl.BlockSpec(memory_space=pltpu.VMEM)] * 2,
        scratch_shapes=[
            pltpu.VMEM((2, groups, GROUP, hid), bf),
            pltpu.VMEM((2, groups, GROUP, hid), bf),
            pltpu.VMEM((2, RING - 1, 2, NY * NZ, GROUP, hid // 2), bf),
            pltpu.VMEM((2, 2, NY * NZ, GROUP, hid // 2), bf),
            pltpu.VMEM((2, RING - 1, 2, NZ, GROUP, hid // 2), bf),
            pltpu.VMEM((2, NZ, GROUP, hid), bf),
            pltpu.VMEM((3, GROUP, hid), bf),
            pltpu.VMEM((14,) + small.shape, jnp.float32),
            pltpu.SemaphoreType.DMA((2, n_copies)),
        ],
        compiler_params=pltpu.CompilerParams(
            collective_id=3, has_side_effects=True, vmem_limit_bytes=56 * MIB
        ),
        name="reduce_all",
    )(own.reshape(shape), oth.reshape(shape), small)


def dot(a, b, dims):
    return lax.dot_general(a, b, (dims, ((), ())), preferred_element_type=jnp.float32)


def gelu_and_slope(p):
    hidden, back = jax.vjp(lambda v: jax.nn.gelu(v, approximate=True), p)
    return hidden, back


def on_device(query_in, doc_in, cluster, gain, w_in, w_out):
    rows, width = query_in.shape
    inv_root = 1.0 / math.sqrt(width)
    o_in, o_out = gather_weights(w_in, w_out)

    rows_in = jnp.concatenate([query_in, doc_in], axis=0)
    values = rows_in.astype(jnp.float32)
    inv_rms = lax.rsqrt(jnp.mean(values * values, axis=-1, keepdims=True) + EPSILON)
    unit_rows = values * inv_rms
    normed = (unit_rows * gain).astype(jnp.bfloat16)
    pre = [jnp.dot(normed, w, preferred_element_type=jnp.float32) for w in (w_in, o_in)]
    hidden = [jax.nn.gelu(p, approximate=True).astype(jnp.bfloat16) for p in pre]
    mixed = jnp.dot(hidden[0], w_out, preferred_element_type=jnp.float32) + jnp.dot(
        hidden[1], o_out, preferred_element_type=jnp.float32
    )
    embedded = (values + mixed).astype(jnp.bfloat16)
    queries, docs = embedded[:rows], embedded[rows:]

    tags = jnp.broadcast_to(cluster.astype(jnp.bfloat16)[None, :], (16, rows))
    band_docs, band_tags, band_queries = gather_band(docs, tags, queries)
    band_cluster = band_tags.reshape(SLOTS, 16, rows)[:, 0].astype(jnp.int32).reshape(-1)

    columns = jnp.arange(SLOTS * rows, dtype=jnp.int32)[None, :]
    is_positive = columns == (OWN * rows + jnp.arange(rows, dtype=jnp.int32))[:, None]
    allowed = (band_cluster[None, :] != cluster[:, None]) | is_positive
    positive_value = is_positive.astype(jnp.float32)

    scores = dot(queries, band_docs, ((1,), (1,))) * inv_root
    masked = jnp.where(allowed, scores, -jnp.inf)
    row_max = jnp.max(masked, axis=1, keepdims=True)
    log_total = row_max + jnp.log(jnp.sum(jnp.exp(masked - row_max), axis=1, keepdims=True))
    positive_score = jnp.sum(jnp.where(is_positive, scores, 0.0), axis=1)
    loss_part = jnp.sum(log_total[:, 0] - positive_score)
    weights = (jnp.exp(masked - log_total) - positive_value).astype(jnp.bfloat16)

    band_totals = exchange_totals(log_total[:, 0])
    back_scores = dot(docs, band_queries, ((1,), (1,))) * inv_root
    back_masked = jnp.where(allowed, back_scores, -jnp.inf)
    back_weights = (jnp.exp(back_masked - band_totals[None, :]) - positive_value).astype(
        jnp.bfloat16
    )
    query_grad = (dot(weights, band_docs, ((1,), (0,))) * inv_root).astype(jnp.bfloat16)
    doc_grad = (dot(back_weights, band_queries, ((1,), (0,))) * inv_root).astype(jnp.bfloat16)
    upstream = jnp.concatenate([query_grad, doc_grad], axis=0)

    g_norm = jnp.zeros((2 * rows, width), jnp.float32)
    downs = []
    for p, h, up, down in zip(pre, hidden, (w_in, o_in), (w_out, o_out)):
        g_act = dot(upstream, down, ((1,), (1,)))
        g_pre = jax.vjp(lambda v: jax.nn.gelu(v, approximate=True), p)[1](g_act)[0]
        g_norm = g_norm + dot(g_pre.astype(jnp.bfloat16), up, ((1,), (1,)))
        downs.append(dot(upstream, h, ((0,), (0,))).astype(jnp.bfloat16))
    gain_term = jnp.sum(g_norm * unit_rows, axis=0)
    d_unit = g_norm * gain
    d_values = inv_rms * (d_unit - unit_rows * jnp.mean(d_unit * unit_rows, axis=-1, keepdims=True))
    grad_rows = (upstream.astype(jnp.float32) + d_values).astype(jnp.bfloat16)

    small = jnp.concatenate(
        [gain_term.reshape(width // 128, 128), jnp.broadcast_to(loss_part, (8, 128))], axis=0
    )
    down_t, total = reduce_all(downs[0], downs[1], small)
    loss = total[width // 128, 0] / (rows * 2 * NBLK)
    gain_total = total[: width // 128].reshape(width)
    return (loss, down_t.T, gain_total, grad_rows[:rows], grad_rows[rows:])


def solution(mesh):
    in_specs = (
        P(("blk", "rep"), None),
        P(("blk", "rep"), None),
        P(("blk", "rep")),
        P(),
        P(None, "rep"),
        P("rep", None),
    )
    out_specs = (P(), P("rep", "blk"), P(), P(("blk", "rep"), None), P(("blk", "rep"), None))
    return jax.shard_map(
        on_device, mesh=mesh, in_specs=in_specs, out_specs=out_specs, check_vma=False
    )
```

```python
import math

import jax
import jax.numpy as jnp
from jax import lax
from jax.experimental import pallas as pl
from jax.experimental.pallas import tpu as pltpu
from jax.sharding import PartitionSpec as P

MESH = pl.DeviceIdType.MESH
MIB = 2**20
NX, NY, NZ, NC = 4, 4, 2, 2
NBLK = NX * NY * NZ * NC
RING = NX
EPSILON = 1e-06
SLOTS = 10
OWN = 4


def coords():
    b = lax.axis_index("blk")
    r = lax.axis_index("rep")
    return b // (NY * NZ * NC), (b // (NZ * NC)) % NY, (b // NC) % NZ, b % NC, r


def device(x, y, zl, c, r):
    return {"blk": ((x * NY + y) * NZ + zl) * NC + c, "rep": r}


def wrap(v, n):
    return lax.rem(v + n, n)


def greet(peers):
    barrier = pltpu.get_barrier_semaphore()
    for peer in peers:
        pl.semaphore_signal(barrier, inc=1, device_id=peer, device_id_type=MESH)
    pl.semaphore_wait(barrier, len(peers))


def remote(src, dst, send, recv, peer):
    return pltpu.make_async_remote_copy(
        src_ref=src,
        dst_ref=dst,
        send_sem=send,
        recv_sem=recv,
        device_id=peer,
        device_id_type=MESH,
    )


WBLK = 256
W_CHUNKS = 8


def weight_view(in_ref, out_ref, block, chunk):
    if chunk < W_CHUNKS // 2:
        rows = in_ref.shape[0] // (W_CHUNKS // 2)
        return in_ref.at[
            pl.ds(chunk * rows, rows), pl.ds(pl.multiple_of(block * WBLK, WBLK), WBLK)
        ]
    rows = WBLK // (W_CHUNKS // 2)
    first = block * WBLK + (chunk - W_CHUNKS // 2) * rows
    return out_ref.at[pl.ds(pl.multiple_of(first, rows), rows)]


def weights_kernel(win, wout, oin, oout, send, recv):
    x, y, zl, c, r = coords()
    cross = device(x, y, 1 - zl, c, 1 - r)
    near = device(x, y, 1 - zl, c, r)
    ahead = device(wrap(x + 1, NX), y, zl, c, r)
    behind = device(wrap(x - 1, NX), y, zl, c, r)
    sibling = device(x, y, zl, 1 - c, r)
    greet([cross, near, ahead, behind, sibling])
    color = lax.rem(x + 2 * zl, 4)

    def block_of(shift):
        return 2 * lax.rem(color + shift, 4) + c

    def copy(flow, block, chunk, peer, source=None):
        src = weight_view(*(source or (oin, oout)), block, chunk)
        dst = weight_view(oin, oout, block, chunk)
        return remote(src, dst, send.at[flow, chunk], recv.at[flow, chunk], peer)

    started = []

    def start(*args):
        op = copy(*args)
        op.start()
        started.append(op)

    for chunk in range(W_CHUNKS):
        start(0, block_of(2), chunk, cross, (win, wout))
    mine = block_of(0)
    for chunk in range(W_CHUNKS):
        copy(0, mine, chunk, cross).wait_recv()
        start(1, mine, chunk, ahead)
        start(2, mine, chunk, behind)
        start(3, mine, chunk, near)
        start(4, mine, chunk, sibling)
        if chunk:
            pass_on(copy, start, block_of, chunk - 1, (behind, ahead, near), sibling)
    pass_on(copy, start, block_of, W_CHUNKS - 1, (behind, ahead, near), sibling)
    for chunk in range(W_CHUNKS):
        for k in range(4):
            other = 2 * lax.rem(color + k, 4) + (1 - c)
            copy(4 + k, other, chunk, sibling).wait_recv()
    for op in started:
        op.wait_send()


def pass_on(copy, start, block_of, chunk, peers, sibling):
    for flow, shift, k in ((1, 3, 3), (2, 1, 1), (3, 2, 2)):
        block = block_of(shift)
        copy(flow, block, chunk, peers[flow - 1]).wait_recv()
        start(4 + k, block, chunk, sibling)


def gather_weights(w_in, w_out):
    return pl.pallas_call(
        weights_kernel,
        out_shape=(
            jax.ShapeDtypeStruct(w_in.shape, w_in.dtype),
            jax.ShapeDtypeStruct(w_out.shape, w_out.dtype),
        ),
        in_specs=[pl.BlockSpec(memory_space=pl.ANY)] * 2,
        out_specs=[pl.BlockSpec(memory_space=pl.ANY)] * 2,
        scratch_shapes=[pltpu.SemaphoreType.DMA((8, W_CHUNKS))] * 2,
        compiler_params=pltpu.CompilerParams(collective_id=0, has_side_effects=True),
        name="gather_weights",
    )(w_in, w_out)


B_CHUNKS = 5


def band_kernel(docs, tags, queries, gd, gx, gq, send, recv, local):
    x, y, zl, c, r = coords()
    b = lax.axis_index("blk")
    cross = device(x, y, 1 - zl, c, 1 - r)
    near = device(x, y, 1 - zl, c, r)
    sibling = device(x, y, zl, 1 - c, r)
    step = NZ * NC * (1 - 2 * zl)
    onward = {"blk": wrap(b + step, NBLK), "rep": r}
    source = {"blk": wrap(b - step, NBLK), "rep": r}
    greet([cross, near, sibling, onward, source])

    rows = docs.shape[0]
    half = rows // 2
    tag_rows = tags.shape[0]

    def view(slot, chunk):
        if chunk == 2:
            return gx.at[pl.ds(pl.multiple_of(slot * tag_rows, tag_rows), tag_rows)]
        ref = gd if chunk < 2 else gq
        first = slot * rows + (chunk % 3) * half
        return ref.at[pl.ds(pl.multiple_of(first, half), half)]

    def own(chunk):
        if chunk == 2:
            return tags
        ref = docs if chunk < 2 else queries
        return ref.at[pl.ds((chunk % 3) * half, half)]

    z_slot = 8 - 8 * zl
    far_slot = 8 * zl
    started = []

    def make(flow, chunk, src, dst_slot, peer):
        return remote(
            src, view(dst_slot, chunk), send.at[flow, chunk], recv.at[flow, chunk], peer
        )

    def start(*args):
        op = make(*args)
        op.start()
        started.append(op)

    def arrived(flow, chunk, slot):
        make(flow, chunk, view(slot, chunk), slot, near).wait_recv()

    def band_to_sibling(chunk):
        return [
            make(7 + k, chunk, view(8 - 8 * c + k, chunk), 6 - 4 * c + k, sibling)
            for k in range(2)
        ]

    order = (0, 1, 2, 3, 4)
    theirs = 8 * zl
    keep = []
    for chunk in order:
        start(0, chunk, own(chunk), theirs, near)
        start(1, chunk, own(chunk), theirs + 1, cross)
        start(5, chunk, own(chunk), 2 + 4 * c, sibling)
        op = pltpu.make_async_copy(own(chunk), view(OWN, chunk), local.at[chunk])
        op.start()
        keep.append(op)
    for place, chunk in enumerate(order):
        arrived(0, chunk, z_slot)
        start(3, chunk, view(z_slot, chunk), far_slot, onward)
        if place % 2 == 0:
            start(2, chunk, view(z_slot, chunk), OWN + 1, cross)
        arrived(1, chunk, z_slot + 1)
        start(4, chunk, view(z_slot + 1, chunk), far_slot + 1, onward)
        if place % 2 == 1:
            start(2, chunk, view(z_slot + 1, chunk), OWN + 1, near)

        @pl.when(c == zl)
        def _():
            for op in band_to_sibling(chunk):
                op.start()

    for chunk in order:
        arrived(2, chunk, OWN + 1)
        start(6, chunk, view(OWN + 1, chunk), 3 + 4 * c, sibling)
        arrived(3, chunk, far_slot)
        arrived(4, chunk, far_slot + 1)

        @pl.when(c != zl)
        def _():
            for op in band_to_sibling(chunk):
                op.start()

    for chunk in order:
        arrived(5, chunk, 6 - 4 * c)
        arrived(6, chunk, 7 - 4 * c)
        for op in band_to_sibling(chunk):
            op.wait_send()
        arrived(7, chunk, 2 + 4 * c)
        arrived(8, chunk, 3 + 4 * c)
        keep[chunk].wait()
    for op in started:
        op.wait_send()


def gather_band(docs, tags, queries):
    return pl.pallas_call(
        band_kernel,
        out_shape=[
            jax.ShapeDtypeStruct((SLOTS * v.shape[0], v.shape[1]), v.dtype)
            for v in (docs, tags, queries)
        ],
        in_specs=[pl.BlockSpec(memory_space=pl.ANY)] * 3,
        out_specs=[pl.BlockSpec(memory_space=pl.ANY)] * 3,
        scratch_shapes=[
            pltpu.SemaphoreType.DMA((9, B_CHUNKS)),
            pltpu.SemaphoreType.DMA((9, B_CHUNKS)),
            pltpu.SemaphoreType.DMA((B_CHUNKS,)),
        ],
        compiler_params=pltpu.CompilerParams(collective_id=1, has_side_effects=True),
        name="gather_band",
    )(docs, tags, queries)


def totals_kernel(mine, out, send, recv):
    b = lax.axis_index("blk")
    r = lax.axis_index("rep")
    peers = []
    for offset in range(-2, 3):
        for other in range(2):
            if offset or other:
                rep = 1 - r if other else r
                peers.append((offset, other, {"blk": wrap(b + offset, NBLK), "rep": rep}))
    greet([peer for _, _, peer in peers])
    ops = []
    for i, (offset, other, peer) in enumerate(peers):
        slot = (2 - offset) * 2 + other
        op = remote(mine, out.at[slot], send.at[i], recv.at[slot], peer)
        op.start()
        ops.append(op)
    out[OWN] = mine[...]
    for slot in range(SLOTS):
        if slot != OWN:
            remote(mine, out.at[slot], send.at[0], recv.at[slot], peers[0][2]).wait_recv()
    for op in ops:
        op.wait_send()


def exchange_totals(log_total):
    rows = log_total.shape[0]
    tile = jnp.pad(log_total.reshape(rows // 128, 128), ((0, 8 - rows // 128), (0, 0)))
    out = pl.pallas_call(
        totals_kernel,
        out_shape=jax.ShapeDtypeStruct((SLOTS, 8, 128), jnp.float32),
        in_specs=[pl.BlockSpec(memory_space=pltpu.VMEM)],
        out_specs=pl.BlockSpec(memory_space=pltpu.VMEM),
        scratch_shapes=[
            pltpu.SemaphoreType.DMA((SLOTS,)),
            pltpu.SemaphoreType.DMA((SLOTS,)),
        ],
        compiler_params=pltpu.CompilerParams(collective_id=2, has_side_effects=True),
        name="exchange_totals",
    )(tile)
    return out[:, : rows // 128].reshape(SLOTS * rows)


GROUP = 16
CHUNKS = 4


def nt(a, b):
    return lax.dot_general(a, b, (((1,), (1,)), ((), ())), preferred_element_type=jnp.float32)


def nn(a, b):
    return lax.dot_general(a, b, (((1,), (0,)), ((), ())), preferred_element_type=jnp.float32)


def backward_kernel(
    rows_ref,
    up_ref,
    upt_ref,
    gain_ref,
    loss_ref,
    hid_hbm,
    slope_hbm,
    win_hbm,
    oin_hbm,
    wout_hbm,
    oout_hbm,
    out,
    total,
    grads,
    hid,
    slope,
    win,
    wout,
    s1,
    r1,
    a1,
    r2,
    a2,
    r3,
    a3,
    r4,
    acc,
    s_buf,
    local,
    sems,
):
    x, y, zl, c, r = coords()
    width = up_ref.shape[1]
    half = win_hbm.shape[1]
    cols = 2 * half // CHUNKS
    sibling = device(x, y, zl, 1 - c, r)
    xs = [device(wrap(x + k, NX), y, zl, c, r) for k in range(1, RING)]
    ys = [device(x, wrap(y + k, NY), zl, c, r) for k in range(1, RING)]
    zs = [device(x, y, 1 - zl, c, r), device(x, y, zl, c, 1 - r), device(x, y, 1 - zl, c, 1 - r)]

    loads = []

    def load(src, dst):
        op = pltpu.make_async_copy(src, dst, local.at[len(loads)])
        op.start()
        loads.append(op)

    for j in range(CHUNKS):
        part = pl.ds(j * cols, cols)
        load(hid_hbm.at[:, part], hid.at[j])
    for j in range(CHUNKS):
        part = pl.ds(j * cols, cols)
        load(slope_hbm.at[:, part], slope.at[j])
    for k, (inner, outer) in enumerate(((win_hbm, wout_hbm), (oin_hbm, oout_hbm))):
        load(inner, win.at[k])
        load(outer, wout.at[k])

    greet([sibling] + xs + ys + zs)
    state = {"n": 0}
    ops = []

    def send(src, dst, peer):
        n = state["n"]
        state["n"] = n + 1
        op = remote(src, dst, sems.at[0, n], sems.at[1, n], peer)
        op.start()
        ops.append(op)
        return op

    wait1 = []
    for j in range(CHUNKS):
        loads[j].wait()
        s1[j] = nn(upt_ref[1 - c], hid[j]).astype(jnp.bfloat16)
        wait1.append(send(s1.at[j], r1.at[j], sibling))

    wait2 = []
    for j in range(CHUNKS):
        mine = nn(upt_ref[c], hid[j])
        wait1[j].wait_recv()
        mine = mine + r1[j].astype(jnp.float32)
        a1[j] = mine.astype(jnp.bfloat16).reshape(NX, NY, NZ, GROUP, cols)
        waits = []
        for k in range(1, RING):
            slot = RING - 1 - k
            if j % 2 == 0:
                waits.append(send(a1.at[j, wrap(x + k, NX)], r2.at[j, slot], xs[k - 1]))
            else:
                waits.append(send(a1.at[j, :, wrap(y + k, NY)], r2.at[j, slot], ys[k - 1]))
        wait2.append(waits)

    per_half = CHUNKS // 2
    for j in range(CHUNKS):
        loads[CHUNKS + j].wait()
    for k in range(2):
        loads[2 * CHUNKS + 2 * k].wait()
        loads[2 * CHUNKS + 2 * k + 1].wait()
    tile = 512
    for j in range(CHUNKS):
        k = j // per_half

        def tile_step(t, _, j=j, k=k):
            first = pl.multiple_of(t * tile, tile)
            there = pl.multiple_of((j % per_half) * cols + t * tile, tile)
            g_act = nt(up_ref[...], wout[k, pl.ds(there, tile), :])
            g_pre = (g_act * slope[j, :, pl.ds(first, tile)].astype(jnp.float32)).astype(
                jnp.bfloat16
            )
            step = nt(g_pre, win[k, :, pl.ds(there, tile)])
            if j == 0:
                before = jnp.where(t == 0, 0.0, acc[...])
            else:
                before = acc[...]
            acc[...] = before + step
            return 0

        if j == 0:
            acc[...] = jnp.zeros_like(acc)
        lax.fori_loop(0, cols // tile, tile_step, 0)

    values = rows_ref[...].astype(jnp.float32)
    inv_rms = lax.rsqrt(jnp.mean(values * values, axis=1, keepdims=True) + EPSILON)
    unit_rows = values * inv_rms
    g_norm = acc[...]
    weighted = g_norm * unit_rows
    gain_term = jnp.sum(weighted, axis=0, keepdims=True)
    gain = gain_ref[...]
    mean = jnp.mean(weighted * gain, axis=1, keepdims=True)
    d_values = inv_rms * (g_norm * gain - unit_rows * mean)
    grads[...] = (up_ref[...].astype(jnp.float32) + d_values).astype(jnp.bfloat16)

    row = lax.broadcasted_iota(jnp.int32, (8, width), 0)
    s_buf[12] = jnp.where(
        row == 0,
        jnp.broadcast_to(gain_term, (8, width)),
        jnp.broadcast_to(loss_ref[0:1, 0:1], (8, width)),
    )
    small = send(s_buf.at[12], s_buf.at[13], sibling)
    small.wait_recv()
    s_buf[x] = s_buf[12] + s_buf[13]
    small = [send(s_buf.at[x], s_buf.at[x], peer) for peer in xs]

    wait3 = []
    for j in range(CHUNKS):
        for op in wait2[j]:
            op.wait_recv()
        tot = (a1[j, x] if j % 2 == 0 else a1[j, :, y]).astype(jnp.float32)
        for k in range(RING - 1):
            tot = tot + r2[j, k].astype(jnp.float32)
        a2[j] = tot.astype(jnp.bfloat16)
        waits = []
        for k in range(1, RING):
            slot = RING - 1 - k
            if j % 2 == 0:
                waits.append(send(a2.at[j, wrap(y + k, NY)], r3.at[j, slot], ys[k - 1]))
            else:
                waits.append(send(a2.at[j, wrap(x + k, NX)], r3.at[j, slot], xs[k - 1]))
        wait3.append(waits)
        if j == 1:
            for op in small:
                op.wait_recv()
            s_buf[4 + y] = ((s_buf[0] + s_buf[1]) + s_buf[2]) + s_buf[3]
            small = [send(s_buf.at[4 + y], s_buf.at[4 + y], peer) for peer in ys]

    for op in small:
        op.wait_recv()
    here = s_buf.at[8 + 2 * r + zl]
    here[...] = ((s_buf[4] + s_buf[5]) + s_buf[6]) + s_buf[7]
    small = [send(here, here, peer) for peer in zs]

    wait4 = []
    for j in range(CHUNKS):
        for op in wait3[j]:
            op.wait_recv()
        tot = (a2[j, y] if j % 2 == 0 else a2[j, x]).astype(jnp.float32)
        for k in range(RING - 1):
            tot = tot + r3[j, k].astype(jnp.float32)
        a3[j] = tot.astype(jnp.bfloat16)
        if j < per_half:
            wait4.append([send(a3.at[j, 1 - zl], r4.at[0, j], zs[0])])
        else:
            i = j - per_half
            wait4[i].append(send(a3.at[j, zl], r4.at[1, i], zs[1]))
            wait4[i].append(send(a3.at[j, 1 - zl], r4.at[2, i], zs[2]))
    for i in range(per_half):
        for op in wait4[i]:
            op.wait_recv()
        out[:, i * cols : (i + 1) * cols] = (
            a3[i, zl].astype(jnp.float32) + r4[0, i].astype(jnp.float32)
        ) + (r4[1, i].astype(jnp.float32) + r4[2, i].astype(jnp.float32))
    for op in small:
        op.wait_recv()
    total[...] = (s_buf[8] + s_buf[9]) + (s_buf[10] + s_buf[11])
    for op in ops:
        op.wait_send()


def backward(rows_in, upstream, gain, loss_part, hidden, slope, w_in, o_in, w_out, o_out):
    rows, width = rows_in.shape
    half = w_in.shape[1]
    cols = 2 * half // CHUNKS
    groups = NX * NY * NZ
    bf, f32 = jnp.bfloat16, jnp.float32
    upt = upstream.T.reshape(groups, NC, GROUP, rows).transpose(1, 0, 2, 3)
    upt = upt.reshape(NC, groups * GROUP, rows)
    vmem = pl.BlockSpec(memory_space=pltpu.VMEM)
    hbm = pl.BlockSpec(memory_space=pl.ANY)
    return pl.pallas_call(
        backward_kernel,
        out_shape=(
            jax.ShapeDtypeStruct((GROUP, half), f32),
            jax.ShapeDtypeStruct((8, width), f32),
            jax.ShapeDtypeStruct((rows, width), bf),
        ),
        in_specs=[vmem] * 5 + [hbm] * 6,
        out_specs=[vmem] * 3,
        scratch_shapes=[
            pltpu.VMEM((CHUNKS, rows, cols), bf),
            pltpu.VMEM((CHUNKS, rows, cols), bf),
            pltpu.VMEM((2,) + w_in.shape, bf),
            pltpu.VMEM((2,) + w_out.shape, bf),
            pltpu.VMEM((CHUNKS, groups * GROUP, cols), bf),
            pltpu.VMEM((CHUNKS, groups * GROUP, cols), bf),
            pltpu.VMEM((CHUNKS, NX, NY, NZ, GROUP, cols), bf),
            pltpu.VMEM((CHUNKS, RING - 1, RING, NZ, GROUP, cols), bf),
            pltpu.VMEM((CHUNKS, RING, NZ, GROUP, cols), bf),
            pltpu.VMEM((CHUNKS, RING - 1, NZ, GROUP, cols), bf),
            pltpu.VMEM((CHUNKS, NZ, GROUP, cols), bf),
            pltpu.VMEM((3, CHUNKS // 2, GROUP, cols), bf),
            pltpu.VMEM((rows, width), f32),
            pltpu.VMEM((14, 8, width), f32),
            pltpu.SemaphoreType.DMA((2 * CHUNKS + 4,)),
            pltpu.SemaphoreType.DMA((2, 7 * CHUNKS + 16)),
        ],
        compiler_params=pltpu.CompilerParams(
            collective_id=3, has_side_effects=True, vmem_limit_bytes=60 * MIB
        ),
        name="backward",
    )(
        rows_in,
        upstream,
        upt,
        gain.reshape(1, width),
        jnp.broadcast_to(loss_part, (8, 128)),
        hidden,
        slope,
        w_in,
        o_in,
        w_out,
        o_out,
    )


def dot(a, b, dims):
    return lax.dot_general(a, b, (dims, ((), ())), preferred_element_type=jnp.float32)


def gelu_slope(p):
    k = math.sqrt(2.0 / math.pi)
    t = jnp.tanh(k * (p + 0.044715 * (p * p * p)))
    return 0.5 * (1.0 + t) + 0.5 * p * (1.0 - t * t) * (k * (1.0 + 3 * 0.044715 * (p * p)))


def on_device(query_in, doc_in, cluster, gain, w_in, w_out):
    rows, width = query_in.shape
    inv_root = 1.0 / math.sqrt(width)
    o_in, o_out = gather_weights(w_in, w_out)

    rows_in = jnp.concatenate([query_in, doc_in], axis=0)
    values = rows_in.astype(jnp.float32)
    inv_rms = lax.rsqrt(jnp.mean(values * values, axis=-1, keepdims=True) + EPSILON)
    unit_rows = values * inv_rms
    normed = (unit_rows * gain).astype(jnp.bfloat16)
    pre = [jnp.dot(normed, w, preferred_element_type=jnp.float32) for w in (w_in, o_in)]
    hidden = [jax.nn.gelu(p, approximate=True).astype(jnp.bfloat16) for p in pre]
    mixed = jnp.dot(hidden[0], w_out, preferred_element_type=jnp.float32) + jnp.dot(
        hidden[1], o_out, preferred_element_type=jnp.float32
    )
    embedded = (values + mixed).astype(jnp.bfloat16)
    queries, docs = embedded[:rows], embedded[rows:]

    tags = jnp.broadcast_to(cluster.astype(jnp.bfloat16)[None, :], (16, rows))
    band_docs, band_tags, band_queries = gather_band(docs, tags, queries)
    band_cluster = band_tags.reshape(SLOTS, 16, rows)[:, 0].astype(jnp.int32).reshape(-1)

    columns = jnp.arange(SLOTS * rows, dtype=jnp.int32)[None, :]
    is_positive = columns == (OWN * rows + jnp.arange(rows, dtype=jnp.int32))[:, None]
    allowed = (band_cluster[None, :] != cluster[:, None]) | is_positive
    positive_value = is_positive.astype(jnp.float32)

    scores = dot(queries, band_docs, ((1,), (1,))) * inv_root
    masked = jnp.where(allowed, scores, -jnp.inf)
    row_max = jnp.max(masked, axis=1, keepdims=True)
    log_total = row_max + jnp.log(jnp.sum(jnp.exp(masked - row_max), axis=1, keepdims=True))
    positive_score = jnp.sum(jnp.where(is_positive, scores, 0.0), axis=1)
    loss_part = jnp.sum(log_total[:, 0] - positive_score)
    weights = (jnp.exp(masked - log_total) - positive_value).astype(jnp.bfloat16)

    band_totals = exchange_totals(log_total[:, 0])
    back_scores = dot(docs, band_queries, ((1,), (1,))) * inv_root
    back_masked = jnp.where(allowed, back_scores, -jnp.inf)
    back_weights = (jnp.exp(back_masked - band_totals[None, :]) - positive_value).astype(
        jnp.bfloat16
    )
    query_grad = (dot(weights, band_docs, ((1,), (0,))) * inv_root).astype(jnp.bfloat16)
    doc_grad = (dot(back_weights, band_queries, ((1,), (0,))) * inv_root).astype(jnp.bfloat16)
    upstream = jnp.concatenate([query_grad, doc_grad], axis=0)

    hidden_all = jnp.concatenate(hidden, axis=1)
    slope_all = jnp.concatenate([gelu_slope(p).astype(jnp.bfloat16) for p in pre], axis=1)
    down_t, total, grad_rows = backward(
        rows_in, upstream, gain, loss_part, hidden_all, slope_all, w_in, o_in, w_out, o_out
    )
    loss = total[1, 0] / (rows * 2 * NBLK)
    return (loss, down_t.T, total[0], grad_rows[:rows], grad_rows[rows:])


def solution(mesh):
    in_specs = (
        P(("blk", "rep"), None),
        P(("blk", "rep"), None),
        P(("blk", "rep")),
        P(),
        P(None, "rep"),
        P("rep", None),
    )
    out_specs = (P(), P("rep", "blk"), P(), P(("blk", "rep"), None), P(("blk", "rep"), None))
    return jax.shard_map(
        on_device, mesh=mesh, in_specs=in_specs, out_specs=out_specs, check_vma=False
    )
```

```python
import math

import jax
import jax.numpy as jnp
from jax import lax
from jax.experimental import pallas as pl
from jax.experimental.pallas import tpu as pltpu
from jax.sharding import PartitionSpec as P

MESH = pl.DeviceIdType.MESH
MIB = 2**20
NX, NY, NZ, NC = 4, 4, 2, 2
NBLK = NX * NY * NZ * NC
RING = NX
EPSILON = 1e-06
SLOTS = 10
OWN = 4


def coords():
    b = lax.axis_index("blk")
    r = lax.axis_index("rep")
    return b // (NY * NZ * NC), (b // (NZ * NC)) % NY, (b // NC) % NZ, b % NC, r


def device(x, y, zl, c, r):
    return {"blk": ((x * NY + y) * NZ + zl) * NC + c, "rep": r}


def wrap(v, n):
    return lax.rem(v + n, n)


def greet(peers):
    barrier = pltpu.get_barrier_semaphore()
    for peer in peers:
        pl.semaphore_signal(barrier, inc=1, device_id=peer, device_id_type=MESH)
    pl.semaphore_wait(barrier, len(peers))


def remote(src, dst, send, recv, peer):
    return pltpu.make_async_remote_copy(
        src_ref=src,
        dst_ref=dst,
        send_sem=send,
        recv_sem=recv,
        device_id=peer,
        device_id_type=MESH,
    )


WBLK = 256
W_CHUNKS = 8
STRIP = 64


def nt(a, b):
    return lax.dot_general(a, b, (((1,), (1,)), ((), ())), preferred_element_type=jnp.float32)


def nn(a, b):
    return lax.dot_general(a, b, (((1,), (0,)), ((), ())), preferred_element_type=jnp.float32)


def gelu_both(p):
    k = math.sqrt(2.0 / math.pi)
    square = p * p
    t = jnp.tanh(p * (k + (k * 0.044715) * square))
    up = 0.5 + 0.5 * t
    slope = up + (0.5 * p) * ((1.0 - t * t) * (k + (3 * k * 0.044715) * square))
    return p * up, slope


def weight_view(in_ref, out_ref, block, chunk):
    if chunk < W_CHUNKS // 2:
        rows = in_ref.shape[0] // (W_CHUNKS // 2)
        return in_ref.at[
            pl.ds(chunk * rows, rows), pl.ds(pl.multiple_of(block * WBLK, WBLK), WBLK)
        ]
    rows = WBLK // (W_CHUNKS // 2)
    first = block * WBLK + (chunk - W_CHUNKS // 2) * rows
    return out_ref.at[pl.ds(pl.multiple_of(first, rows), rows)]


def forward_kernel(
    q_in,
    d_in,
    gain_ref,
    win_hbm,
    wout_hbm,
    q_emb,
    d_emb,
    hid_hbm,
    slope_hbm,
    oin_hbm,
    oout_hbm,
    win,
    wout,
    oin,
    oout,
    normed,
    hid,
    slope,
    pre,
    acc,
    local,
    stores,
    send,
    recv,
):
    x, y, zl, c, r = coords()
    cross = device(x, y, 1 - zl, c, 1 - r)
    near = device(x, y, 1 - zl, c, r)
    ahead = device(wrap(x + 1, NX), y, zl, c, r)
    behind = device(wrap(x - 1, NX), y, zl, c, r)
    sibling = device(x, y, zl, 1 - c, r)
    half = win_hbm.shape[1]
    rows = q_in.shape[0]
    load_in = pltpu.make_async_copy(win_hbm, win, local.at[0])
    load_out = pltpu.make_async_copy(wout_hbm, wout, local.at[1])
    load_in.start()
    load_out.start()
    greet([cross, near, ahead, behind, sibling])
    color = lax.rem(x + 2 * zl, 4)
    started = []

    def color_at(shift):
        return lax.rem(color + shift, 4)

    def block_of(shift):
        return 2 * color_at(shift) + c

    def copy(flow, block, chunk, peer, source=None):
        src = weight_view(*(source or (oin, oout)), block, chunk)
        dst = weight_view(oin, oout, block, chunk)
        return remote(src, dst, send.at[flow, chunk], recv.at[flow, chunk], peer)

    def start(*args):
        op = copy(*args)
        op.start()
        started.append(op)

    def first_hop(chunk):
        mine = block_of(0)
        copy(0, mine, chunk, cross).wait_recv()
        start(1, mine, chunk, ahead)
        start(2, mine, chunk, behind)
        start(3, mine, chunk, near)
        start(4, mine, chunk, sibling)

    def second_hop(chunk):
        for flow, shift in ((1, 3), (2, 1), (3, 2)):
            block = block_of(shift)
            copy(flow, block, chunk, near).wait_recv()
            start(4 + shift, block, chunk, sibling)

    def from_sibling(shift, chunks):
        block = 2 * color_at(shift) + (1 - c)
        for chunk in chunks:
            copy(4 + shift, block, chunk, sibling).wait_recv()

    stored = []

    def store(src, dst):
        op = pltpu.make_async_copy(src, dst, stores.at[len(stored)])
        op.start()
        stored.append(op)

    tile = 2 * WBLK

    def activate(block):
        def strip(i, _):
            at = pl.ds(pl.multiple_of(i * STRIP, STRIP), STRIP)
            h, s = gelu_both(pre[at, :])
            hid[block, at, :] = h.astype(jnp.bfloat16)
            slope[block, at, :] = s.astype(jnp.bfloat16)
            return 0

        lax.fori_loop(0, 2 * rows // STRIP, strip, 0)
        there = (block // 2, slice(None), pl.ds(pl.multiple_of((block % 2) * tile, tile), tile))
        store(hid.at[block], hid_hbm.at[there])
        store(slope.at[block], slope_hbm.at[there])

    def up_own(t):
        pre[...] = nn(normed[...], win[:, t * tile : (t + 1) * tile])
        activate(t)

    def down_own(t):
        step = nn(hid[t], wout[t * tile : (t + 1) * tile, :])
        acc[...] = step if t == 0 else acc[...] + step

    def up_other(shift):
        from_sibling(shift, range(W_CHUNKS // 2))
        at = pl.ds(pl.multiple_of(color_at(shift) * tile, tile), tile)
        pre[...] = nn(normed[...], oin[:, at])
        activate(half // tile + color_at(shift))
        store(oin.at[:, at], oin_hbm.at[:, at])

    def down_other(shift):
        from_sibling(shift, range(W_CHUNKS // 2, W_CHUNKS))
        at = pl.ds(pl.multiple_of(color_at(shift) * tile, tile), tile)
        acc[...] += nn(hid[half // tile + color_at(shift)], oout[at, :])
        store(oout.at[at, :], oout_hbm.at[at, :])

    for chunk in range(W_CHUNKS):
        start(0, block_of(2), chunk, cross, (win_hbm, wout_hbm))
    for k, ref in enumerate((q_in, d_in)):
        values = ref[...].astype(jnp.float32)
        inv_rms = lax.rsqrt(jnp.mean(values * values, axis=1, keepdims=True) + EPSILON)
        normed[k * rows : (k + 1) * rows, :] = ((values * inv_rms) * gain_ref[...]).astype(
            jnp.bfloat16
        )
    load_in.wait()
    up_own(0)
    first_hop(0)
    up_own(1)
    first_hop(1)
    second_hop(0)
    up_own(2)
    first_hop(2)
    second_hop(1)
    up_own(3)
    first_hop(3)
    second_hop(2)
    load_out.wait()
    down_own(0)
    down_own(1)
    first_hop(4)
    second_hop(3)
    up_other(0)
    first_hop(5)
    second_hop(4)
    up_other(1)
    first_hop(6)
    second_hop(5)
    up_other(2)
    first_hop(7)
    second_hop(6)
    up_other(3)
    second_hop(7)
    down_own(2)
    down_own(3)
    for shift in (0, 3, 1, 2):
        down_other(shift)
    for k, (ref, emb) in enumerate(((q_in, q_emb), (d_in, d_emb))):
        emb[...] = (ref[...].astype(jnp.float32) + acc[k * rows : (k + 1) * rows, :]).astype(
            jnp.bfloat16
        )
    for op in started:
        op.wait_send()
    for op in stored:
        op.wait()


def forward(q_in, d_in, gain, w_in, w_out):
    rows, width = q_in.shape
    half = w_in.shape[1]
    bf, f32 = jnp.bfloat16, jnp.float32
    tile = 2 * WBLK
    vmem = pl.BlockSpec(memory_space=pltpu.VMEM)
    hbm = pl.BlockSpec(memory_space=pl.ANY)
    per_chunk = jax.ShapeDtypeStruct((CHUNKS, 2 * rows, 2 * half // CHUNKS), bf)
    return pl.pallas_call(
        forward_kernel,
        out_shape=(
            jax.ShapeDtypeStruct(q_in.shape, bf),
            jax.ShapeDtypeStruct(d_in.shape, bf),
            per_chunk,
            per_chunk,
            jax.ShapeDtypeStruct(w_in.shape, bf),
            jax.ShapeDtypeStruct(w_out.shape, bf),
        ),
        in_specs=[vmem] * 3 + [hbm] * 2,
        out_specs=[vmem] * 2 + [hbm] * 4,
        scratch_shapes=[
            pltpu.VMEM(w_in.shape, bf),
            pltpu.VMEM(w_out.shape, bf),
            pltpu.VMEM(w_in.shape, bf),
            pltpu.VMEM(w_out.shape, bf),
            pltpu.VMEM((2 * rows, width), bf),
            pltpu.VMEM((2 * half // tile, 2 * rows, tile), bf),
            pltpu.VMEM((2 * half // tile, 2 * rows, tile), bf),
            pltpu.VMEM((2 * rows, tile), f32),
            pltpu.VMEM((2 * rows, width), f32),
            pltpu.SemaphoreType.DMA((2,)),
            pltpu.SemaphoreType.DMA((2 * 2 * half // tile + 8,)),
            pltpu.SemaphoreType.DMA((8, W_CHUNKS)),
            pltpu.SemaphoreType.DMA((8, W_CHUNKS)),
        ],
        compiler_params=pltpu.CompilerParams(
            collective_id=0, has_side_effects=True, vmem_limit_bytes=56 * MIB
        ),
        name="forward",
    )(q_in, d_in, gain.reshape(1, width), w_in, w_out)


PIECES = (
    (0, 0, 64, 0, 0),
    (1, 0, 16, 0, 0),
    (0, 64, 64, 1, 0),
    (0, 128, 80, 0, 0),
    (0, 208, 48, 1, 1),
    (2, 0, 64, 0, 0),
    (2, 64, 64, 1, 0),
    (2, 128, 80, 0, 0),
    (2, 208, 48, 1, 1),
)
DOC_PIECES = (0, 1, 2, 3, 4)
QUERY_PIECES = (5, 6, 7, 8)
DETOUR_ROWS = 48


def band_kernel(
    docs, tags, queries, column_tag, up, loss, gd, gx, gq, transit, s, w, lt, mine, acc, send, recv, tsem
):
    x, y, zl, c, r = coords()
    b = lax.axis_index("blk")
    rows, width = docs.shape
    inv_root = 1.0 / math.sqrt(width)
    cross = device(x, y, 1 - zl, c, 1 - r)
    near = device(x, y, 1 - zl, c, r)
    sibling = device(x, y, zl, 1 - c, r)
    step = NZ * NC * (1 - 2 * zl)
    onward = {"blk": wrap(b + step, NBLK), "rep": r}
    source = {"blk": wrap(b - step, NBLK), "rep": r}
    peers = []
    for offset in range(-2, 3):
        for other in range(2):
            if offset or other:
                rep = 1 - r if other else r
                peers.append((offset, other, {"blk": wrap(b + offset, NBLK), "rep": rep}))
    greet([peer for _, _, peer in peers] + [onward, source])

    def view(slot, p):
        kind, first, count = PIECES[p][:3]
        return (gd, gx, gq)[kind].at[slot, pl.ds(first, count)]

    def own(p):
        kind, first, count = PIECES[p][:3]
        return (docs, tags, queries)[kind].at[pl.ds(first, count)]

    z_slot = 8 - 8 * zl
    far_slot = 8 * zl
    theirs = 8 * zl
    started = []

    def make(flow, p, src, dst, peer):
        return remote(src, dst, send.at[flow, p], recv.at[flow, p], peer)

    def start(*args):
        op = make(*args)
        op.start()
        started.append(op)

    def arrived(flow, p, slot):
        make(flow, p, view(slot, p), view(slot, p), near).wait_recv()

    def band_to_sibling(p):
        return [
            make(7 + k, p, view(8 - 8 * c + k, p), view(6 - 4 * c + k, p), sibling)
            for k in range(2)
        ]

    def through(p):
        return transit.at[p // 5]

    def send_own(p):
        start(0, p, own(p), view(theirs, p), near)
        start(1, p, own(p), view(theirs + 1, p), cross)
        if PIECES[p][4]:
            start(9, p, own(p), through(p), source)
        start(5, p, own(p), view(2 + 4 * c, p), sibling)

    def from_z(p):
        by_near, detour = PIECES[p][3:]
        arrived(0, p, z_slot)
        if not detour:
            start(3, p, view(z_slot, p), view(far_slot, p), onward)
        if not by_near:
            start(2, p, view(z_slot, p), view(OWN + 1, p), cross)
        arrived(1, p, z_slot + 1)
        if not detour:
            start(4, p, view(z_slot + 1, p), view(far_slot + 1, p), onward)
        if by_near:
            start(2, p, view(z_slot + 1, p), view(OWN + 1, p), near)

        @pl.when(c == zl)
        def _():
            for op in band_to_sibling(p):
                op.start()

    def from_transit(p):
        if PIECES[p][4]:
            make(9, p, own(p), through(p), source).wait_recv()
            start(10, p, through(p), view(8 - 8 * zl, p), near)
            start(11, p, through(p), view(8 - 8 * zl + 1, p), cross)

    def from_rep(p):
        arrived(2, p, OWN + 1)
        start(6, p, view(OWN + 1, p), view(3 + 4 * c, p), sibling)

    def from_far(p):
        detour = PIECES[p][4]
        arrived(10 if detour else 3, p, far_slot)
        arrived(11 if detour else 4, p, far_slot + 1)

        @pl.when(c != zl)
        def _():
            for op in band_to_sibling(p):
                op.start()

    def from_sibling(p):
        arrived(5, p, 6 - 4 * c)
        arrived(6, p, 7 - 4 * c)

    def band_from_sibling(p):
        arrived(7, p, 2 + 4 * c)
        arrived(8, p, 3 + 4 * c)

    row = lax.broadcasted_iota(jnp.int32, (rows, rows), 0)
    col = lax.broadcasted_iota(jnp.int32, (rows, rows), 1)
    diagonal = row == col

    def masked(a, g, slot):
        scores = nt(a[...], g[slot]) * inv_root
        tag_row = gx[slot].astype(jnp.float32)[0:1, :]
        allowed = tag_row != column_tag[...]
        if isinstance(slot, int) and slot == OWN:
            allowed = allowed | diagonal
        return scores, jnp.where(allowed, scores, -jnp.inf)

    def score(slot):
        s[slot] = masked(queries, gd, slot)[1]

    def backward_of(slot):
        m = masked(docs, gq, slot)[1]
        wt = jnp.exp(m - lt[slot, 0:1, :])
        if isinstance(slot, int) and slot == OWN:
            wt = wt - diagonal.astype(jnp.float32)
        acc[...] += nn(wt.astype(jnp.bfloat16), gq[slot])

    for p in DOC_PIECES:
        send_own(p)
    gd[OWN] = docs[...]
    gq[OWN] = queries[...]
    gx[OWN] = tags[...]
    for p in DOC_PIECES:
        from_z(p)
    for p in QUERY_PIECES:
        send_own(p)
    for p in DOC_PIECES:
        from_transit(p)
    score(OWN)
    positive = jnp.sum(jnp.where(diagonal, s[OWN], 0.0), axis=1, keepdims=True)
    score(z_slot)
    score(z_slot + 1)
    for p in DOC_PIECES:
        from_rep(p)
    for p in DOC_PIECES[:3]:
        from_far(p)
    from_z(QUERY_PIECES[0])
    for p in DOC_PIECES[3:]:
        from_far(p)
    for p in DOC_PIECES:
        from_sibling(p)
    from_z(QUERY_PIECES[1])
    score(OWN + 1)
    score(6 - 4 * c)
    score(7 - 4 * c)
    score(far_slot)
    score(far_slot + 1)
    from_z(QUERY_PIECES[2])
    for p in DOC_PIECES:
        band_from_sibling(p)
    score(2 + 4 * c)
    score(3 + 4 * c)
    top = s[0]
    for slot in range(1, SLOTS):
        top = jnp.maximum(top, s[slot])
    row_max = jnp.max(top, axis=1, keepdims=True)
    total = jnp.exp(s[0] - row_max)
    for slot in range(1, SLOTS):
        total = total + jnp.exp(s[slot] - row_max)
    log_total = row_max + jnp.log(jnp.sum(total, axis=1, keepdims=True))
    loss[...] = jnp.broadcast_to(
        jnp.sum(log_total - positive, axis=0, keepdims=True), loss.shape
    )
    mine[...] = jnp.transpose(jnp.broadcast_to(log_total, (rows, 128)))[0:8, :]
    lt[OWN] = mine[...]
    tops = []
    for i, (offset, other, peer) in enumerate(peers):
        slot = (2 - offset) * 2 + other
        op = remote(mine, lt.at[slot], tsem.at[0, i], tsem.at[1, slot], peer)
        op.start()
        tops.append(op)
    from_z(QUERY_PIECES[3])
    for p in QUERY_PIECES:
        from_transit(p)
    for slot in range(SLOTS):
        wt = jnp.exp(s[slot] - log_total)
        if slot == OWN:
            wt = wt - diagonal.astype(jnp.float32)
        w[:, slot * rows : (slot + 1) * rows] = wt.astype(jnp.bfloat16)
    query_grad = nn(w[...], gd[...].reshape(SLOTS * rows, width))
    up[0:rows, :] = (query_grad * inv_root).astype(jnp.bfloat16)

    for slot in range(SLOTS):
        if slot != OWN:
            remote(mine, lt.at[slot], tsem.at[0, 0], tsem.at[1, slot], near).wait_recv()
    for p in QUERY_PIECES:
        from_rep(p)
    acc[...] = jnp.zeros_like(acc)
    backward_of(OWN)
    backward_of(z_slot)
    backward_of(z_slot + 1)
    backward_of(OWN + 1)
    for p in QUERY_PIECES:
        from_sibling(p)
    backward_of(6 - 4 * c)
    backward_of(7 - 4 * c)
    for p in QUERY_PIECES:
        from_far(p)
    backward_of(far_slot)
    backward_of(far_slot + 1)
    for p in QUERY_PIECES:
        band_from_sibling(p)
    backward_of(2 + 4 * c)
    backward_of(3 + 4 * c)
    up[rows : 2 * rows, :] = (acc[...] * inv_root).astype(jnp.bfloat16)

    for p in range(len(PIECES)):
        for op in band_to_sibling(p):
            op.wait_send()
    for op in started + tops:
        op.wait_send()


def band(docs, tags, queries, column_tag):
    rows, width = docs.shape
    bf, f32 = jnp.bfloat16, jnp.float32
    vmem = pl.BlockSpec(memory_space=pltpu.VMEM)
    return pl.pallas_call(
        band_kernel,
        out_shape=(
            jax.ShapeDtypeStruct((2 * rows, width), bf),
            jax.ShapeDtypeStruct((8, 128), f32),
        ),
        in_specs=[vmem] * 4,
        out_specs=[vmem] * 2,
        scratch_shapes=[
            pltpu.VMEM((SLOTS, rows, width), bf),
            pltpu.VMEM((SLOTS,) + tags.shape, bf),
            pltpu.VMEM((SLOTS, rows, width), bf),
            pltpu.VMEM((2, DETOUR_ROWS, width), bf),
            pltpu.VMEM((SLOTS, rows, rows), f32),
            pltpu.VMEM((rows, SLOTS * rows), bf),
            pltpu.VMEM((SLOTS, 8, rows), f32),
            pltpu.VMEM((8, rows), f32),
            pltpu.VMEM((rows, width), f32),
            pltpu.SemaphoreType.DMA((12, len(PIECES))),
            pltpu.SemaphoreType.DMA((12, len(PIECES))),
            pltpu.SemaphoreType.DMA((2, SLOTS)),
        ],
        compiler_params=pltpu.CompilerParams(
            collective_id=1, has_side_effects=True, vmem_limit_bytes=48 * MIB
        ),
        name="band",
    )(docs, tags, queries, column_tag)


GROUP = 16
CHUNKS = 4


def backward_kernel(
    rows_ref,
    up_ref,
    upt_ref,
    gain_ref,
    loss_ref,
    hid_hbm,
    slope_hbm,
    win_hbm,
    oin_hbm,
    wout_hbm,
    oout_hbm,
    out,
    total,
    grads,
    hid,
    slope,
    win,
    wout,
    s1,
    r1,
    a1,
    r2,
    a2,
    r3,
    a3,
    r4,
    acc,
    s_buf,
    local,
    sems,
):
    x, y, zl, c, r = coords()
    width = up_ref.shape[1]
    half = win_hbm.shape[1]
    cols = 2 * half // CHUNKS
    sibling = device(x, y, zl, 1 - c, r)
    xs = [device(wrap(x + k, NX), y, zl, c, r) for k in range(1, RING)]
    ys = [device(x, wrap(y + k, NY), zl, c, r) for k in range(1, RING)]
    zs = [device(x, y, 1 - zl, c, r), device(x, y, zl, c, 1 - r), device(x, y, 1 - zl, c, 1 - r)]

    loads = []

    def load(src, dst):
        op = pltpu.make_async_copy(src, dst, local.at[len(loads)])
        op.start()
        loads.append(op)

    for j in range(CHUNKS):
        load(hid_hbm.at[j], hid.at[j])
    for j in range(CHUNKS):
        load(slope_hbm.at[j], slope.at[j])
    for k, (inner, outer) in enumerate(((win_hbm, wout_hbm), (oin_hbm, oout_hbm))):
        load(inner, win.at[k])
        load(outer, wout.at[k])

    greet([sibling] + xs + ys + zs)
    state = {"n": 0}
    ops = []

    def send(src, dst, peer):
        n = state["n"]
        state["n"] = n + 1
        op = remote(src, dst, sems.at[0, n], sems.at[1, n], peer)
        op.start()
        ops.append(op)
        return op

    wait1 = []
    for j in range(CHUNKS):
        loads[j].wait()
        s1[j] = nn(upt_ref[1 - c], hid[j]).astype(jnp.bfloat16)
        wait1.append(send(s1.at[j], r1.at[j], sibling))

    wait2 = []
    for j in range(CHUNKS):
        mine = nn(upt_ref[c], hid[j])
        wait1[j].wait_recv()
        mine = mine + r1[j].astype(jnp.float32)
        a1[j] = mine.astype(jnp.bfloat16).reshape(NX, NY, NZ, GROUP, cols)
        waits = []
        for k in range(1, RING):
            slot = RING - 1 - k
            if j % 2 == 0:
                waits.append(send(a1.at[j, wrap(x + k, NX)], r2.at[j, slot], xs[k - 1]))
            else:
                waits.append(send(a1.at[j, :, wrap(y + k, NY)], r2.at[j, slot], ys[k - 1]))
        wait2.append(waits)

    per_half = CHUNKS // 2
    for j in range(CHUNKS):
        loads[CHUNKS + j].wait()
    for k in range(2):
        loads[2 * CHUNKS + 2 * k].wait()
        loads[2 * CHUNKS + 2 * k + 1].wait()
    tile = 512
    for j in range(CHUNKS):
        k = j // per_half

        def tile_step(t, _, j=j, k=k):
            first = pl.multiple_of(t * tile, tile)
            there = pl.multiple_of((j % per_half) * cols + t * tile, tile)
            g_act = nt(up_ref[...], wout[k, pl.ds(there, tile), :])
            g_pre = (g_act * slope[j, :, pl.ds(first, tile)].astype(jnp.float32)).astype(
                jnp.bfloat16
            )
            step = nt(g_pre, win[k, :, pl.ds(there, tile)])
            if j == 0:
                before = jnp.where(t == 0, 0.0, acc[...])
            else:
                before = acc[...]
            acc[...] = before + step
            return 0

        if j == 0:
            acc[...] = jnp.zeros_like(acc)
        lax.fori_loop(0, cols // tile, tile_step, 0)

    values = rows_ref[...].astype(jnp.float32)
    inv_rms = lax.rsqrt(jnp.mean(values * values, axis=1, keepdims=True) + EPSILON)
    unit_rows = values * inv_rms
    g_norm = acc[...]
    weighted = g_norm * unit_rows
    gain_term = jnp.sum(weighted, axis=0, keepdims=True)
    gain = gain_ref[...]
    mean = jnp.mean(weighted * gain, axis=1, keepdims=True)
    d_values = inv_rms * (g_norm * gain - unit_rows * mean)
    grads[...] = (up_ref[...].astype(jnp.float32) + d_values).astype(jnp.bfloat16)

    row = lax.broadcasted_iota(jnp.int32, (8, width), 0)
    s_buf[12] = jnp.where(
        row == 0,
        jnp.broadcast_to(gain_term, (8, width)),
        jnp.broadcast_to(loss_ref[0:1, 0:1], (8, width)),
    )
    small = send(s_buf.at[12], s_buf.at[13], sibling)
    small.wait_recv()
    s_buf[x] = s_buf[12] + s_buf[13]
    small = [send(s_buf.at[x], s_buf.at[x], peer) for peer in xs]

    wait3 = []
    for j in range(CHUNKS):
        for op in wait2[j]:
            op.wait_recv()
        tot = (a1[j, x] if j % 2 == 0 else a1[j, :, y]).astype(jnp.float32)
        for k in range(RING - 1):
            tot = tot + r2[j, k].astype(jnp.float32)
        a2[j] = tot.astype(jnp.bfloat16)
        waits = []
        for k in range(1, RING):
            slot = RING - 1 - k
            if j % 2 == 0:
                waits.append(send(a2.at[j, wrap(y + k, NY)], r3.at[j, slot], ys[k - 1]))
            else:
                waits.append(send(a2.at[j, wrap(x + k, NX)], r3.at[j, slot], xs[k - 1]))
        wait3.append(waits)
        if j == 1:
            for op in small:
                op.wait_recv()
            s_buf[4 + y] = ((s_buf[0] + s_buf[1]) + s_buf[2]) + s_buf[3]
            small = [send(s_buf.at[4 + y], s_buf.at[4 + y], peer) for peer in ys]

    for op in small:
        op.wait_recv()
    here = s_buf.at[8 + 2 * r + zl]
    here[...] = ((s_buf[4] + s_buf[5]) + s_buf[6]) + s_buf[7]
    small = [send(here, here, peer) for peer in zs]

    wait4 = []
    for j in range(CHUNKS):
        for op in wait3[j]:
            op.wait_recv()
        tot = (a2[j, y] if j % 2 == 0 else a2[j, x]).astype(jnp.float32)
        for k in range(RING - 1):
            tot = tot + r3[j, k].astype(jnp.float32)
        a3[j] = tot.astype(jnp.bfloat16)
        if j < per_half:
            wait4.append([send(a3.at[j, 1 - zl], r4.at[0, j], zs[0])])
        else:
            i = j - per_half
            wait4[i].append(send(a3.at[j, zl], r4.at[1, i], zs[1]))
            wait4[i].append(send(a3.at[j, 1 - zl], r4.at[2, i], zs[2]))
    for i in range(per_half):
        for op in wait4[i]:
            op.wait_recv()
        out[:, i * cols : (i + 1) * cols] = (
            a3[i, zl].astype(jnp.float32) + r4[0, i].astype(jnp.float32)
        ) + (r4[1, i].astype(jnp.float32) + r4[2, i].astype(jnp.float32))
    for op in small:
        op.wait_recv()
    total[...] = (s_buf[8] + s_buf[9]) + (s_buf[10] + s_buf[11])
    for op in ops:
        op.wait_send()


def backward(rows_in, upstream, gain, loss_part, hidden, slope, w_in, o_in, w_out, o_out):
    rows, width = rows_in.shape
    half = w_in.shape[1]
    cols = 2 * half // CHUNKS
    groups = NX * NY * NZ
    bf, f32 = jnp.bfloat16, jnp.float32
    upt = upstream.T.reshape(groups, NC, GROUP, rows).transpose(1, 0, 2, 3)
    upt = upt.reshape(NC, groups * GROUP, rows)
    vmem = pl.BlockSpec(memory_space=pltpu.VMEM)
    hbm = pl.BlockSpec(memory_space=pl.ANY)
    return pl.pallas_call(
        backward_kernel,
        out_shape=(
            jax.ShapeDtypeStruct((GROUP, half), f32),
            jax.ShapeDtypeStruct((8, width), f32),
            jax.ShapeDtypeStruct((rows, width), bf),
        ),
        in_specs=[vmem] * 5 + [hbm] * 6,
        out_specs=[vmem] * 3,
        scratch_shapes=[
            pltpu.VMEM((CHUNKS, rows, cols), bf),
            pltpu.VMEM((CHUNKS, rows, cols), bf),
            pltpu.VMEM((2,) + w_in.shape, bf),
            pltpu.VMEM((2,) + w_out.shape, bf),
            pltpu.VMEM((CHUNKS, groups * GROUP, cols), bf),
            pltpu.VMEM((CHUNKS, groups * GROUP, cols), bf),
            pltpu.VMEM((CHUNKS, NX, NY, NZ, GROUP, cols), bf),
            pltpu.VMEM((CHUNKS, RING - 1, RING, NZ, GROUP, cols), bf),
            pltpu.VMEM((CHUNKS, RING, NZ, GROUP, cols), bf),
            pltpu.VMEM((CHUNKS, RING - 1, NZ, GROUP, cols), bf),
            pltpu.VMEM((CHUNKS, NZ, GROUP, cols), bf),
            pltpu.VMEM((3, CHUNKS // 2, GROUP, cols), bf),
            pltpu.VMEM((rows, width), f32),
            pltpu.VMEM((14, 8, width), f32),
            pltpu.SemaphoreType.DMA((2 * CHUNKS + 4,)),
            pltpu.SemaphoreType.DMA((2, 7 * CHUNKS + 16)),
        ],
        compiler_params=pltpu.CompilerParams(
            collective_id=3, has_side_effects=True, vmem_limit_bytes=60 * MIB
        ),
        name="backward",
    )(
        rows_in,
        upstream,
        upt,
        gain.reshape(1, width),
        loss_part,
        hidden,
        slope,
        w_in,
        o_in,
        w_out,
        o_out,
    )


def on_device(query_in, doc_in, cluster, gain, w_in, w_out):
    rows, width = query_in.shape
    queries, docs, hidden, slope, o_in, o_out = forward(query_in, doc_in, gain, w_in, w_out)

    tags = jnp.broadcast_to(cluster.astype(jnp.bfloat16)[None, :], (16, rows))
    column_tag = cluster.astype(jnp.float32)[:, None]
    upstream, loss_part = band(docs, tags, queries, column_tag)

    rows_in = jnp.concatenate([query_in, doc_in], axis=0)
    down_t, total, grad_rows = backward(
        rows_in, upstream, gain, loss_part, hidden, slope, w_in, o_in, w_out, o_out
    )
    loss = total[1, 0] / (rows * 2 * NBLK)
    return (loss, down_t.T, total[0], grad_rows[:rows], grad_rows[rows:])


def solution(mesh):
    in_specs = (
        P(("blk", "rep"), None),
        P(("blk", "rep"), None),
        P(("blk", "rep")),
        P(),
        P(None, "rep"),
        P("rep", None),
    )
    out_specs = (P(), P("rep", "blk"), P(), P(("blk", "rep"), None), P(("blk", "rep"), None))
    return jax.shard_map(
        on_device, mesh=mesh, in_specs=in_specs, out_specs=out_specs, check_vma=False
    )
```

```python
import math

import jax
import jax.numpy as jnp
from jax import lax
from jax.experimental import pallas as pl
from jax.experimental.pallas import tpu as pltpu
from jax.sharding import PartitionSpec as P

MESH = pl.DeviceIdType.MESH
MIB = 2**20
NX, NY, NZ, NC = 4, 4, 2, 2
NBLK = NX * NY * NZ * NC
RING = NX
EPSILON = 1e-06
SLOTS = 10
OWN = 4
GROUP = 16


def coords():
    b = lax.axis_index("blk")
    r = lax.axis_index("rep")
    return b // (NY * NZ * NC), (b // (NZ * NC)) % NY, (b // NC) % NZ, b % NC, r


def device(x, y, zl, c, r):
    return {"blk": ((x * NY + y) * NZ + zl) * NC + c, "rep": r}


def wrap(v, n):
    return lax.rem(v + n, n)


def greet(peers):
    barrier = pltpu.get_barrier_semaphore()
    for peer in peers:
        pl.semaphore_signal(barrier, inc=1, device_id=peer, device_id_type=MESH)
    pl.semaphore_wait(barrier, len(peers))


def remote(src, dst, send, recv, peer):
    return pltpu.make_async_remote_copy(
        src_ref=src,
        dst_ref=dst,
        send_sem=send,
        recv_sem=recv,
        device_id=peer,
        device_id_type=MESH,
    )


WBLK = 256
W_CHUNKS = 8
STRIP = 64


def nt(a, b):
    return lax.dot_general(a, b, (((1,), (1,)), ((), ())), preferred_element_type=jnp.float32)


def nn(a, b):
    return lax.dot_general(a, b, (((1,), (0,)), ((), ())), preferred_element_type=jnp.float32)


def gelu_both(p):
    k = math.sqrt(2.0 / math.pi)
    square = p * p
    t = jnp.tanh(p * (k + (k * 0.044715) * square))
    up = 0.5 + 0.5 * t
    slope = up + (0.5 * p) * ((1.0 - t * t) * (k + (3 * k * 0.044715) * square))
    return p * up, slope


def weight_view(in_ref, out_ref, block, chunk):
    if chunk < W_CHUNKS // 2:
        rows = in_ref.shape[0] // (W_CHUNKS // 2)
        return in_ref.at[
            pl.ds(chunk * rows, rows), pl.ds(pl.multiple_of(block * WBLK, WBLK), WBLK)
        ]
    rows = WBLK // (W_CHUNKS // 2)
    first = block * WBLK + (chunk - W_CHUNKS // 2) * rows
    return out_ref.at[pl.ds(pl.multiple_of(first, rows), rows)]


def forward_kernel(
    q_in,
    d_in,
    gain_ref,
    win_hbm,
    wout_hbm,
    q_emb,
    d_emb,
    hid_hbm,
    slope_hbm,
    oin_hbm,
    oout_hbm,
    win,
    wout,
    oin,
    oout,
    normed,
    hid,
    slope,
    pre,
    acc,
    local,
    stores,
    send,
    recv,
):
    x, y, zl, c, r = coords()
    cross = device(x, y, 1 - zl, c, 1 - r)
    near = device(x, y, 1 - zl, c, r)
    ahead = device(wrap(x + 1, NX), y, zl, c, r)
    behind = device(wrap(x - 1, NX), y, zl, c, r)
    sibling = device(x, y, zl, 1 - c, r)
    half = win_hbm.shape[1]
    rows = q_in.shape[0]
    load_in = pltpu.make_async_copy(win_hbm, win, local.at[0])
    load_out = pltpu.make_async_copy(wout_hbm, wout, local.at[1])
    load_in.start()
    load_out.start()
    greet([cross, near, ahead, behind, sibling])
    color = lax.rem(x + 2 * zl, 4)
    started = []

    def color_at(shift):
        return lax.rem(color + shift, 4)

    def block_of(shift):
        return 2 * color_at(shift) + c

    def copy(flow, block, chunk, peer, source=None):
        src = weight_view(*(source or (oin, oout)), block, chunk)
        dst = weight_view(oin, oout, block, chunk)
        return remote(src, dst, send.at[flow, chunk], recv.at[flow, chunk], peer)

    def start(*args):
        op = copy(*args)
        op.start()
        started.append(op)

    def first_hop(chunk):
        mine = block_of(0)
        copy(0, mine, chunk, cross).wait_recv()
        start(1, mine, chunk, ahead)
        start(2, mine, chunk, behind)
        start(3, mine, chunk, near)
        start(4, mine, chunk, sibling)

    def second_hop(chunk):
        for flow, shift in ((1, 3), (2, 1), (3, 2)):
            block = block_of(shift)
            copy(flow, block, chunk, near).wait_recv()
            start(4 + shift, block, chunk, sibling)

    def from_sibling(shift, chunks):
        block = 2 * color_at(shift) + (1 - c)
        for chunk in chunks:
            copy(4 + shift, block, chunk, sibling).wait_recv()

    stored = []

    def store(src, dst):
        op = pltpu.make_async_copy(src, dst, stores.at[len(stored)])
        op.start()
        stored.append(op)

    tile = 2 * WBLK

    def activate(block):
        def strip(i, _):
            at = pl.ds(pl.multiple_of(i * STRIP, STRIP), STRIP)
            h, s = gelu_both(pre[at, :])
            hid[block, at, :] = h.astype(jnp.bfloat16)
            slope[block, at, :] = s.astype(jnp.bfloat16)
            return 0

        lax.fori_loop(0, 2 * rows // STRIP, strip, 0)
        there = (block // 2, slice(None), pl.ds(pl.multiple_of((block % 2) * tile, tile), tile))
        store(hid.at[block], hid_hbm.at[there])
        store(slope.at[block], slope_hbm.at[there])

    def up_own(t):
        pre[...] = nn(normed[...], win[:, t * tile : (t + 1) * tile])
        activate(t)

    def down_own(t):
        step = nn(hid[t], wout[t * tile : (t + 1) * tile, :])
        acc[...] = step if t == 0 else acc[...] + step

    def up_other(shift):
        from_sibling(shift, range(W_CHUNKS // 2))
        at = pl.ds(pl.multiple_of(color_at(shift) * tile, tile), tile)
        pre[...] = nn(normed[...], oin[:, at])
        activate(half // tile + color_at(shift))
        store(oin.at[:, at], oin_hbm.at[:, at])

    def down_other(shift):
        from_sibling(shift, range(W_CHUNKS // 2, W_CHUNKS))
        at = pl.ds(pl.multiple_of(color_at(shift) * tile, tile), tile)
        acc[...] += nn(hid[half // tile + color_at(shift)], oout[at, :])
        store(oout.at[at, :], oout_hbm.at[at, :])

    for chunk in range(W_CHUNKS):
        start(0, block_of(2), chunk, cross, (win_hbm, wout_hbm))
    for k, ref in enumerate((q_in, d_in)):
        values = ref[...].astype(jnp.float32)
        inv_rms = lax.rsqrt(jnp.mean(values * values, axis=1, keepdims=True) + EPSILON)
        normed[k * rows : (k + 1) * rows, :] = ((values * inv_rms) * gain_ref[...]).astype(
            jnp.bfloat16
        )
    load_in.wait()
    up_own(0)
    first_hop(0)
    up_own(1)
    first_hop(1)
    second_hop(0)
    up_own(2)
    first_hop(2)
    second_hop(1)
    up_own(3)
    first_hop(3)
    second_hop(2)
    load_out.wait()
    down_own(0)
    down_own(1)
    first_hop(4)
    second_hop(3)
    up_other(0)
    first_hop(5)
    second_hop(4)
    up_other(1)
    first_hop(6)
    second_hop(5)
    up_other(2)
    first_hop(7)
    second_hop(6)
    up_other(3)
    second_hop(7)
    down_own(2)
    down_own(3)
    for shift in (0, 3, 1, 2):
        down_other(shift)
    for k, (ref, emb) in enumerate(((q_in, q_emb), (d_in, d_emb))):
        emb[...] = (ref[...].astype(jnp.float32) + acc[k * rows : (k + 1) * rows, :]).astype(
            jnp.bfloat16
        )
    for op in started:
        op.wait_send()
    for op in stored:
        op.wait()


def forward(q_in, d_in, gain, w_in, w_out):
    rows, width = q_in.shape
    half = w_in.shape[1]
    bf, f32 = jnp.bfloat16, jnp.float32
    tile = 2 * WBLK
    vmem = pl.BlockSpec(memory_space=pltpu.VMEM)
    hbm = pl.BlockSpec(memory_space=pl.ANY)
    per_chunk = jax.ShapeDtypeStruct((CHUNKS, 2 * rows, 2 * half // CHUNKS), bf)
    return pl.pallas_call(
        forward_kernel,
        out_shape=(
            jax.ShapeDtypeStruct(q_in.shape, bf),
            jax.ShapeDtypeStruct(d_in.shape, bf),
            per_chunk,
            per_chunk,
            jax.ShapeDtypeStruct(w_in.shape, bf),
            jax.ShapeDtypeStruct(w_out.shape, bf),
        ),
        in_specs=[vmem] * 3 + [hbm] * 2,
        out_specs=[vmem] * 2 + [hbm] * 4,
        scratch_shapes=[
            pltpu.VMEM(w_in.shape, bf),
            pltpu.VMEM(w_out.shape, bf),
            pltpu.VMEM(w_in.shape, bf),
            pltpu.VMEM(w_out.shape, bf),
            pltpu.VMEM((2 * rows, width), bf),
            pltpu.VMEM((2 * half // tile, 2 * rows, tile), bf),
            pltpu.VMEM((2 * half // tile, 2 * rows, tile), bf),
            pltpu.VMEM((2 * rows, tile), f32),
            pltpu.VMEM((2 * rows, width), f32),
            pltpu.SemaphoreType.DMA((2,)),
            pltpu.SemaphoreType.DMA((2 * 2 * half // tile + 8,)),
            pltpu.SemaphoreType.DMA((8, W_CHUNKS)),
            pltpu.SemaphoreType.DMA((8, W_CHUNKS)),
        ],
        compiler_params=pltpu.CompilerParams(
            collective_id=0, has_side_effects=True, vmem_limit_bytes=56 * MIB
        ),
        name="forward",
    )(q_in, d_in, gain.reshape(1, width), w_in, w_out)


PIECES = (
    (0, 0, 64, 0, 0),
    (1, 0, 16, 0, 0),
    (0, 64, 64, 1, 0),
    (0, 128, 80, 0, 0),
    (0, 208, 48, 1, 1),
    (2, 0, 64, 0, 0),
    (2, 64, 64, 1, 0),
    (2, 128, 80, 0, 0),
    (2, 208, 48, 1, 1),
)
DOC_PIECES = (0, 1, 2, 3, 4)
QUERY_PIECES = (5, 6, 7, 8)
DETOUR_ROWS = 48


def band_kernel(
    docs,
    tags,
    queries,
    column_tag,
    up,
    upt,
    loss,
    gd,
    gx,
    gq,
    transit,
    s,
    w,
    lt,
    mine,
    acc,
    up_v,
    upt_v,
    local,
    send,
    recv,
    tsem,
):
    x, y, zl, c, r = coords()
    b = lax.axis_index("blk")
    rows, width = docs.shape
    inv_root = 1.0 / math.sqrt(width)
    cross = device(x, y, 1 - zl, c, 1 - r)
    near = device(x, y, 1 - zl, c, r)
    sibling = device(x, y, zl, 1 - c, r)
    step = NZ * NC * (1 - 2 * zl)
    onward = {"blk": wrap(b + step, NBLK), "rep": r}
    source = {"blk": wrap(b - step, NBLK), "rep": r}
    peers = []
    for offset in range(-2, 3):
        for other in range(2):
            if offset or other:
                rep = 1 - r if other else r
                peers.append((offset, other, {"blk": wrap(b + offset, NBLK), "rep": rep}))
    own_docs = pltpu.make_async_copy(docs, gd.at[OWN], local.at[0])
    own_queries = pltpu.make_async_copy(queries, gq.at[OWN], local.at[1])
    own_docs.start()
    own_queries.start()
    greet([peer for _, _, peer in peers] + [onward, source])

    def view(slot, p):
        kind, first, count = PIECES[p][:3]
        return (gd, gx, gq)[kind].at[slot, pl.ds(first, count)]

    def own(p):
        kind, first, count = PIECES[p][:3]
        return (docs, tags, queries)[kind].at[pl.ds(first, count)]

    z_slot = 8 - 8 * zl
    far_slot = 8 * zl
    theirs = 8 * zl
    started = []

    def make(flow, p, src, dst, peer):
        return remote(src, dst, send.at[flow, p], recv.at[flow, p], peer)

    def start(*args):
        op = make(*args)
        op.start()
        started.append(op)

    def arrived(flow, p, slot):
        make(flow, p, view(slot, p), view(slot, p), near).wait_recv()

    def band_to_sibling(p):
        return [
            make(7 + k, p, view(8 - 8 * c + k, p), view(6 - 4 * c + k, p), sibling)
            for k in range(2)
        ]

    def through(p):
        return transit.at[p // 5]

    def send_own(p):
        start(0, p, own(p), view(theirs, p), near)
        start(1, p, own(p), view(theirs + 1, p), cross)
        if PIECES[p][4]:
            start(9, p, own(p), through(p), source)
        start(5, p, own(p), view(2 + 4 * c, p), sibling)

    def from_z(p):
        by_near, detour = PIECES[p][3:]
        arrived(0, p, z_slot)
        if not detour:
            start(3, p, view(z_slot, p), view(far_slot, p), onward)
        if not by_near:
            start(2, p, view(z_slot, p), view(OWN + 1, p), cross)
        arrived(1, p, z_slot + 1)
        if not detour:
            start(4, p, view(z_slot + 1, p), view(far_slot + 1, p), onward)
        if by_near:
            start(2, p, view(z_slot + 1, p), view(OWN + 1, p), near)

        @pl.when(c == zl)
        def _():
            for op in band_to_sibling(p):
                op.start()

    def from_transit(p):
        if PIECES[p][4]:
            make(9, p, own(p), through(p), source).wait_recv()
            start(10, p, through(p), view(8 - 8 * zl, p), near)
            start(11, p, through(p), view(8 - 8 * zl + 1, p), cross)

    def from_rep(p):
        arrived(2, p, OWN + 1)
        start(6, p, view(OWN + 1, p), view(3 + 4 * c, p), sibling)

    def from_far(p):
        detour = PIECES[p][4]
        arrived(10 if detour else 3, p, far_slot)
        arrived(11 if detour else 4, p, far_slot + 1)

        @pl.when(c != zl)
        def _():
            for op in band_to_sibling(p):
                op.start()

    def from_sibling(p):
        arrived(5, p, 6 - 4 * c)
        arrived(6, p, 7 - 4 * c)

    def band_from_sibling(p):
        arrived(7, p, 2 + 4 * c)
        arrived(8, p, 3 + 4 * c)

    def hand_out(k, value):
        up_v[k] = value
        turned = jnp.transpose(value).reshape(width // (NC * GROUP), NC, GROUP, rows)
        for core in range(NC):
            upt_v[k, core] = turned[:, core].reshape(width // NC, rows)
        ops = [
            pltpu.make_async_copy(up_v.at[k], up.at[pl.ds(k * rows, rows)], local.at[2 + 2 * k]),
            pltpu.make_async_copy(upt_v.at[k], upt.at[k], local.at[3 + 2 * k]),
        ]
        for op in ops:
            op.start()
        return ops

    row = lax.broadcasted_iota(jnp.int32, (rows, rows), 0)
    col = lax.broadcasted_iota(jnp.int32, (rows, rows), 1)
    diagonal = row == col

    def masked(a, g, slot):
        scores = nt(a[OWN], g[slot]) * inv_root
        tag_row = gx[slot].astype(jnp.float32)[0:1, :]
        allowed = tag_row != column_tag[...]
        if isinstance(slot, int) and slot == OWN:
            allowed = allowed | diagonal
        return scores, jnp.where(allowed, scores, -jnp.inf)

    def score(slot):
        s[slot] = masked(gq, gd, slot)[1]

    def backward_of(slot):
        m = masked(gd, gq, slot)[1]
        wt = jnp.exp(m - lt[slot, 0:1, :])
        if isinstance(slot, int) and slot == OWN:
            wt = wt - diagonal.astype(jnp.float32)
        acc[...] += nn(wt.astype(jnp.bfloat16), gq[slot])

    for p in DOC_PIECES:
        send_own(p)
    gx[OWN] = tags[...]
    own_docs.wait()
    own_queries.wait()
    for p in DOC_PIECES:
        from_z(p)
    for p in QUERY_PIECES:
        send_own(p)
    for p in DOC_PIECES:
        from_transit(p)
    score(OWN)
    positive = jnp.sum(jnp.where(diagonal, s[OWN], 0.0), axis=1, keepdims=True)
    score(z_slot)
    score(z_slot + 1)
    for p in DOC_PIECES:
        from_rep(p)
    for p in DOC_PIECES[:3]:
        from_far(p)
    from_z(QUERY_PIECES[0])
    for p in DOC_PIECES[3:]:
        from_far(p)
    for p in DOC_PIECES:
        from_sibling(p)
    from_z(QUERY_PIECES[1])
    score(OWN + 1)
    score(6 - 4 * c)
    score(7 - 4 * c)
    score(far_slot)
    score(far_slot + 1)
    from_z(QUERY_PIECES[2])
    for p in DOC_PIECES:
        band_from_sibling(p)
    score(2 + 4 * c)
    score(3 + 4 * c)
    top = s[0]
    for slot in range(1, SLOTS):
        top = jnp.maximum(top, s[slot])
    row_max = jnp.max(top, axis=1, keepdims=True)
    total = jnp.exp(s[0] - row_max)
    for slot in range(1, SLOTS):
        total = total + jnp.exp(s[slot] - row_max)
    log_total = row_max + jnp.log(jnp.sum(total, axis=1, keepdims=True))
    loss[...] = jnp.broadcast_to(
        jnp.sum(log_total - positive, axis=0, keepdims=True), loss.shape
    )
    mine[...] = jnp.transpose(jnp.broadcast_to(log_total, (rows, 128)))[0:8, :]
    lt[OWN] = mine[...]
    tops = []
    for i, (offset, other, peer) in enumerate(peers):
        slot = (2 - offset) * 2 + other
        op = remote(mine, lt.at[slot], tsem.at[0, i], tsem.at[1, slot], peer)
        op.start()
        tops.append(op)
    from_z(QUERY_PIECES[3])
    for p in QUERY_PIECES:
        from_transit(p)
    for slot in range(SLOTS):
        wt = jnp.exp(s[slot] - log_total)
        if slot == OWN:
            wt = wt - diagonal.astype(jnp.float32)
        w[:, slot * rows : (slot + 1) * rows] = wt.astype(jnp.bfloat16)
    query_grad = nn(w[...], gd[...].reshape(SLOTS * rows, width))
    outs = hand_out(0, (query_grad * inv_root).astype(jnp.bfloat16))

    for slot in range(SLOTS):
        if slot != OWN:
            remote(mine, lt.at[slot], tsem.at[0, 0], tsem.at[1, slot], near).wait_recv()
    for p in QUERY_PIECES:
        from_rep(p)
    acc[...] = jnp.zeros_like(acc)
    backward_of(OWN)
    backward_of(z_slot)
    backward_of(z_slot + 1)
    backward_of(OWN + 1)
    for p in QUERY_PIECES:
        from_sibling(p)
    backward_of(6 - 4 * c)
    backward_of(7 - 4 * c)
    for p in QUERY_PIECES:
        from_far(p)
    backward_of(far_slot)
    backward_of(far_slot + 1)
    for p in QUERY_PIECES:
        band_from_sibling(p)
    backward_of(2 + 4 * c)
    backward_of(3 + 4 * c)
    outs += hand_out(1, (acc[...] * inv_root).astype(jnp.bfloat16))

    for p in range(len(PIECES)):
        for op in band_to_sibling(p):
            op.wait_send()
    for op in started + tops:
        op.wait_send()
    for op in outs:
        op.wait()


def band(docs, tags, queries, column_tag):
    rows, width = docs.shape
    bf, f32 = jnp.bfloat16, jnp.float32
    vmem = pl.BlockSpec(memory_space=pltpu.VMEM)
    hbm = pl.BlockSpec(memory_space=pl.ANY)
    return pl.pallas_call(
        band_kernel,
        out_shape=(
            jax.ShapeDtypeStruct((2 * rows, width), bf),
            jax.ShapeDtypeStruct((2, NC, width // NC, rows), bf),
            jax.ShapeDtypeStruct((8, 128), f32),
        ),
        in_specs=[hbm, vmem, hbm, vmem],
        out_specs=[hbm, hbm, vmem],
        scratch_shapes=[
            pltpu.VMEM((SLOTS, rows, width), bf),
            pltpu.VMEM((SLOTS,) + tags.shape, bf),
            pltpu.VMEM((SLOTS, rows, width), bf),
            pltpu.VMEM((2, DETOUR_ROWS, width), bf),
            pltpu.VMEM((SLOTS, rows, rows), f32),
            pltpu.VMEM((rows, SLOTS * rows), bf),
            pltpu.VMEM((SLOTS, 8, rows), f32),
            pltpu.VMEM((8, rows), f32),
            pltpu.VMEM((rows, width), f32),
            pltpu.VMEM((2, rows, width), bf),
            pltpu.VMEM((2, NC, width // NC, rows), bf),
            pltpu.SemaphoreType.DMA((6,)),
            pltpu.SemaphoreType.DMA((12, len(PIECES))),
            pltpu.SemaphoreType.DMA((12, len(PIECES))),
            pltpu.SemaphoreType.DMA((2, SLOTS)),
        ],
        compiler_params=pltpu.CompilerParams(
            collective_id=1, has_side_effects=True, vmem_limit_bytes=60 * MIB
        ),
        name="band",
    )(docs, tags, queries, column_tag)


CHUNKS = 4


def backward_kernel(
    q_hbm,
    d_hbm,
    up_hbm,
    upt_hbm,
    gain_ref,
    loss_ref,
    hid_hbm,
    slope_hbm,
    win_hbm,
    oin_hbm,
    wout_hbm,
    oout_hbm,
    out,
    total,
    grads,
    in_v,
    up_ref,
    upt_ref,
    hid,
    slope,
    win,
    wout,
    s1,
    r1,
    a1,
    r2,
    a2,
    r3,
    a3,
    r4,
    acc,
    s_buf,
    local,
    sems,
):
    x, y, zl, c, r = coords()
    rows, width = q_hbm.shape
    half = win_hbm.shape[1]
    cols = 2 * half // CHUNKS
    sibling = device(x, y, zl, 1 - c, r)
    xs = [device(wrap(x + k, NX), y, zl, c, r) for k in range(1, RING)]
    ys = [device(x, wrap(y + k, NY), zl, c, r) for k in range(1, RING)]
    zs = [device(x, y, 1 - zl, c, r), device(x, y, zl, c, 1 - r), device(x, y, 1 - zl, c, 1 - r)]

    loads = []
    n_loads = [0]

    def load(src, dst):
        nonlocal loads
        op = pltpu.make_async_copy(src, dst, local.at[n_loads[0]])
        op.start()
        n_loads[0] += 1
        loads.append(op)
        return op

    first_loads = [load(upt_hbm.at[k], upt_ref.at[k]) for k in range(2)]
    loads = []
    for j in range(CHUNKS):
        load(hid_hbm.at[j], hid.at[j])
    for j in range(CHUNKS):
        load(slope_hbm.at[j], slope.at[j])
    for k, (inner, outer) in enumerate(((win_hbm, wout_hbm), (oin_hbm, oout_hbm))):
        load(inner, win.at[k])
        load(outer, wout.at[k])
    late_loads = [
        load(up_hbm, up_ref),
        load(q_hbm, in_v.at[pl.ds(0, rows)]),
        load(d_hbm, in_v.at[pl.ds(rows, rows)]),
    ]

    greet([sibling] + xs + ys + zs)
    state = {"n": 0}
    ops = []

    def send(src, dst, peer):
        n = state["n"]
        state["n"] = n + 1
        op = remote(src, dst, sems.at[0, n], sems.at[1, n], peer)
        op.start()
        ops.append(op)
        return op

    def down_part(core, j):
        return nn(upt_ref[0, core], hid[j, 0:rows, :]) + nn(upt_ref[1, core], hid[j, rows:, :])

    wait1 = []
    for j in range(CHUNKS):
        loads[j].wait()
        if j == 0:
            for op in first_loads:
                op.wait()
        s1[j] = down_part(1 - c, j).astype(jnp.bfloat16)
        wait1.append(send(s1.at[j], r1.at[j], sibling))

    wait2 = []
    for j in range(CHUNKS):
        mine = down_part(c, j)
        wait1[j].wait_recv()
        mine = mine + r1[j].astype(jnp.float32)
        a1[j] = mine.astype(jnp.bfloat16).reshape(NX, NY, NZ, GROUP, cols)
        waits = []
        for k in range(1, RING):
            slot = RING - 1 - k
            if j % 2 == 0:
                waits.append(send(a1.at[j, wrap(x + k, NX)], r2.at[j, slot], xs[k - 1]))
            else:
                waits.append(send(a1.at[j, :, wrap(y + k, NY)], r2.at[j, slot], ys[k - 1]))
        wait2.append(waits)

    per_half = CHUNKS // 2
    for j in range(CHUNKS):
        loads[CHUNKS + j].wait()
    for k in range(2):
        loads[2 * CHUNKS + 2 * k].wait()
        loads[2 * CHUNKS + 2 * k + 1].wait()
    for op in late_loads:
        op.wait()
    tile = 512
    for j in range(CHUNKS):
        k = j // per_half

        def tile_step(t, _, j=j, k=k):
            first = pl.multiple_of(t * tile, tile)
            there = pl.multiple_of((j % per_half) * cols + t * tile, tile)
            g_act = nt(up_ref[...], wout[k, pl.ds(there, tile), :])
            g_pre = (g_act * slope[j, :, pl.ds(first, tile)].astype(jnp.float32)).astype(
                jnp.bfloat16
            )
            step = nt(g_pre, win[k, :, pl.ds(there, tile)])
            if j == 0:
                before = jnp.where(t == 0, 0.0, acc[...])
            else:
                before = acc[...]
            acc[...] = before + step
            return 0

        if j == 0:
            acc[...] = jnp.zeros_like(acc)
        lax.fori_loop(0, cols // tile, tile_step, 0)

    values = in_v[...].astype(jnp.float32)
    inv_rms = lax.rsqrt(jnp.mean(values * values, axis=1, keepdims=True) + EPSILON)
    unit_rows = values * inv_rms
    g_norm = acc[...]
    weighted = g_norm * unit_rows
    gain_term = jnp.sum(weighted, axis=0, keepdims=True)
    gain = gain_ref[...]
    mean = jnp.mean(weighted * gain, axis=1, keepdims=True)
    d_values = inv_rms * (g_norm * gain - unit_rows * mean)
    grads[...] = (up_ref[...].astype(jnp.float32) + d_values).astype(jnp.bfloat16)

    row = lax.broadcasted_iota(jnp.int32, (8, width), 0)
    s_buf[12] = jnp.where(
        row == 0,
        jnp.broadcast_to(gain_term, (8, width)),
        jnp.broadcast_to(loss_ref[0:1, 0:1], (8, width)),
    )
    small = send(s_buf.at[12], s_buf.at[13], sibling)
    small.wait_recv()
    s_buf[x] = s_buf[12] + s_buf[13]
    small = [send(s_buf.at[x], s_buf.at[x], peer) for peer in xs]

    wait3 = []
    for j in range(CHUNKS):
        for op in wait2[j]:
            op.wait_recv()
        tot = (a1[j, x] if j % 2 == 0 else a1[j, :, y]).astype(jnp.float32)
        for k in range(RING - 1):
            tot = tot + r2[j, k].astype(jnp.float32)
        a2[j] = tot.astype(jnp.bfloat16)
        waits = []
        for k in range(1, RING):
            slot = RING - 1 - k
            if j % 2 == 0:
                waits.append(send(a2.at[j, wrap(y + k, NY)], r3.at[j, slot], ys[k - 1]))
            else:
                waits.append(send(a2.at[j, wrap(x + k, NX)], r3.at[j, slot], xs[k - 1]))
        wait3.append(waits)
        if j == 1:
            for op in small:
                op.wait_recv()
            s_buf[4 + y] = ((s_buf[0] + s_buf[1]) + s_buf[2]) + s_buf[3]
            small = [send(s_buf.at[4 + y], s_buf.at[4 + y], peer) for peer in ys]

    for op in small:
        op.wait_recv()
    here = s_buf.at[8 + 2 * r + zl]
    here[...] = ((s_buf[4] + s_buf[5]) + s_buf[6]) + s_buf[7]
    small = [send(here, here, peer) for peer in zs]

    wait4 = []
    for j in range(CHUNKS):
        for op in wait3[j]:
            op.wait_recv()
        tot = (a2[j, y] if j % 2 == 0 else a2[j, x]).astype(jnp.float32)
        for k in range(RING - 1):
            tot = tot + r3[j, k].astype(jnp.float32)
        a3[j] = tot.astype(jnp.bfloat16)
        if j < per_half:
            wait4.append([send(a3.at[j, 1 - zl], r4.at[0, j], zs[0])])
        else:
            i = j - per_half
            wait4[i].append(send(a3.at[j, zl], r4.at[1, i], zs[1]))
            wait4[i].append(send(a3.at[j, 1 - zl], r4.at[2, i], zs[2]))
    for i in range(per_half):
        for op in wait4[i]:
            op.wait_recv()
        out[:, i * cols : (i + 1) * cols] = (
            a3[i, zl].astype(jnp.float32) + r4[0, i].astype(jnp.float32)
        ) + (r4[1, i].astype(jnp.float32) + r4[2, i].astype(jnp.float32))
    for op in small:
        op.wait_recv()
    total[...] = (s_buf[8] + s_buf[9]) + (s_buf[10] + s_buf[11])
    for op in ops:
        op.wait_send()


def backward(q_in, d_in, up, upt, gain, loss_part, hidden, slope, w_in, o_in, w_out, o_out):
    rows, width = 2 * q_in.shape[0], q_in.shape[1]
    half = w_in.shape[1]
    cols = 2 * half // CHUNKS
    groups = NX * NY * NZ
    bf, f32 = jnp.bfloat16, jnp.float32
    vmem = pl.BlockSpec(memory_space=pltpu.VMEM)
    hbm = pl.BlockSpec(memory_space=pl.ANY)
    return pl.pallas_call(
        backward_kernel,
        out_shape=(
            jax.ShapeDtypeStruct((GROUP, half), f32),
            jax.ShapeDtypeStruct((8, width), f32),
            jax.ShapeDtypeStruct((rows, width), bf),
        ),
        in_specs=[hbm] * 4 + [vmem] * 2 + [hbm] * 6,
        out_specs=[vmem] * 3,
        scratch_shapes=[
            pltpu.VMEM((rows, width), bf),
            pltpu.VMEM((rows, width), bf),
            pltpu.VMEM(upt.shape, bf),
            pltpu.VMEM((CHUNKS, rows, cols), bf),
            pltpu.VMEM((CHUNKS, rows, cols), bf),
            pltpu.VMEM((2,) + w_in.shape, bf),
            pltpu.VMEM((2,) + w_out.shape, bf),
            pltpu.VMEM((CHUNKS, groups * GROUP, cols), bf),
            pltpu.VMEM((CHUNKS, groups * GROUP, cols), bf),
            pltpu.VMEM((CHUNKS, NX, NY, NZ, GROUP, cols), bf),
            pltpu.VMEM((CHUNKS, RING - 1, RING, NZ, GROUP, cols), bf),
            pltpu.VMEM((CHUNKS, RING, NZ, GROUP, cols), bf),
            pltpu.VMEM((CHUNKS, RING - 1, NZ, GROUP, cols), bf),
            pltpu.VMEM((CHUNKS, NZ, GROUP, cols), bf),
            pltpu.VMEM((3, CHUNKS // 2, GROUP, cols), bf),
            pltpu.VMEM((rows, width), f32),
            pltpu.VMEM((14, 8, width), f32),
            pltpu.SemaphoreType.DMA((2 * CHUNKS + 9,)),
            pltpu.SemaphoreType.DMA((2, 7 * CHUNKS + 16)),
        ],
        compiler_params=pltpu.CompilerParams(
            collective_id=3, has_side_effects=True, vmem_limit_bytes=60 * MIB
        ),
        name="backward",
    )(
        q_in,
        d_in,
        up,
        upt,
        gain.reshape(1, width),
        loss_part,
        hidden,
        slope,
        w_in,
        o_in,
        w_out,
        o_out,
    )


def finish_kernel(down, total, grads, down_out, gain_out, loss_out, q_out, d_out):
    rows = q_out.shape[0]
    down_out[...] = down[...]
    gain_out[...] = total[0:1, :]
    loss_out[...] = total[1:2, 0:1] * (1.0 / (rows * 2 * NBLK))
    q_out[...] = grads[0:rows, :]
    d_out[...] = grads[rows : 2 * rows, :]


def finish(down, total, grads):
    rows, width = grads.shape[0] // 2, grads.shape[1]
    f32 = jnp.float32
    row_grads = jax.ShapeDtypeStruct((rows, width), grads.dtype)
    return pl.pallas_call(
        finish_kernel,
        out_shape=(
            jax.ShapeDtypeStruct(down.shape, f32),
            jax.ShapeDtypeStruct((1, width), f32),
            jax.ShapeDtypeStruct((1, 1), f32),
            row_grads,
            row_grads,
        ),
        name="finish",
    )(down, total, grads)


def on_device(query_in, doc_in, cluster, gain, w_in, w_out):
    rows, width = query_in.shape
    queries, docs, hidden, slope, o_in, o_out = forward(query_in, doc_in, gain, w_in, w_out)

    tags = jnp.broadcast_to(cluster.astype(jnp.bfloat16)[None, :], (16, rows))
    column_tag = cluster.astype(jnp.float32)[:, None]
    up, upt, loss_part = band(docs, tags, queries, column_tag)
    sums = backward(
        query_in, doc_in, up, upt, gain, loss_part, hidden, slope, w_in, o_in, w_out, o_out
    )
    down_t, gain_total, loss, q_grads, d_grads = finish(*sums)
    return (loss.reshape(()), down_t.T, gain_total.reshape(width), q_grads, d_grads)


def solution(mesh):
    in_specs = (
        P(("blk", "rep"), None),
        P(("blk", "rep"), None),
        P(("blk", "rep")),
        P(),
        P(None, "rep"),
        P("rep", None),
    )
    out_specs = (P(), P("rep", "blk"), P(), P(("blk", "rep"), None), P(("blk", "rep"), None))
    return jax.shard_map(
        on_device, mesh=mesh, in_specs=in_specs, out_specs=out_specs, check_vma=False
    )
```

```python
import math

import jax
import jax.numpy as jnp
from jax import lax
from jax.experimental import pallas as pl
from jax.experimental.pallas import tpu as pltpu
from jax.sharding import PartitionSpec as P

MESH = pl.DeviceIdType.MESH
MIB = 2**20
NX, NY, NZ, NC = 4, 4, 2, 2
NBLK = NX * NY * NZ * NC
RING = NX
EPSILON = 1e-06
SLOTS = 10
OWN = 4
GROUP = 16


def coords():
    b = lax.axis_index("blk")
    r = lax.axis_index("rep")
    return b // (NY * NZ * NC), (b // (NZ * NC)) % NY, (b // NC) % NZ, b % NC, r


def device(x, y, zl, c, r):
    return {"blk": ((x * NY + y) * NZ + zl) * NC + c, "rep": r}


def wrap(v, n):
    return lax.rem(v + n, n)


def greet(peers):
    barrier = pltpu.get_barrier_semaphore()
    for peer in peers:
        pl.semaphore_signal(barrier, inc=1, device_id=peer, device_id_type=MESH)
    pl.semaphore_wait(barrier, len(peers))


def remote(src, dst, send, recv, peer):
    return pltpu.make_async_remote_copy(
        src_ref=src,
        dst_ref=dst,
        send_sem=send,
        recv_sem=recv,
        device_id=peer,
        device_id_type=MESH,
    )


WBLK = 256
W_CHUNKS = 8
STRIP = 64


def nt(a, b):
    return lax.dot_general(a, b, (((1,), (1,)), ((), ())), preferred_element_type=jnp.float32)


def nn(a, b):
    return lax.dot_general(a, b, (((1,), (0,)), ((), ())), preferred_element_type=jnp.float32)


def gelu_both(p):
    k = math.sqrt(2.0 / math.pi)
    square = p * p
    t = jnp.tanh(p * (k + (k * 0.044715) * square))
    up = 0.5 + 0.5 * t
    slope = up + (0.5 * p) * ((1.0 - t * t) * (k + (3 * k * 0.044715) * square))
    return p * up, slope


def weight_view(in_ref, out_ref, block, chunk):
    if chunk < W_CHUNKS // 2:
        rows = in_ref.shape[0] // (W_CHUNKS // 2)
        return in_ref.at[
            pl.ds(chunk * rows, rows), pl.ds(pl.multiple_of(block * WBLK, WBLK), WBLK)
        ]
    rows = WBLK // (W_CHUNKS // 2)
    first = block * WBLK + (chunk - W_CHUNKS // 2) * rows
    return out_ref.at[pl.ds(pl.multiple_of(first, rows), rows)]


def forward_kernel(
    q_in,
    d_in,
    gain_ref,
    win_hbm,
    wout_hbm,
    q_emb,
    d_emb,
    hid_hbm,
    slope_hbm,
    oin_hbm,
    oout_hbm,
    win,
    wout,
    oin,
    oout,
    normed,
    hid,
    slope,
    pre,
    acc,
    local,
    stores,
    send,
    recv,
):
    x, y, zl, c, r = coords()
    cross = device(x, y, 1 - zl, c, 1 - r)
    near = device(x, y, 1 - zl, c, r)
    ahead = device(wrap(x + 1, NX), y, zl, c, r)
    behind = device(wrap(x - 1, NX), y, zl, c, r)
    sibling = device(x, y, zl, 1 - c, r)
    half = win_hbm.shape[1]
    rows = q_in.shape[0]
    load_in = pltpu.make_async_copy(win_hbm, win, local.at[0])
    load_out = pltpu.make_async_copy(wout_hbm, wout, local.at[1])
    load_in.start()
    load_out.start()
    greet([cross, near, ahead, behind, sibling])
    color = lax.rem(x + 2 * zl, 4)
    started = []

    def color_at(shift):
        return lax.rem(color + shift, 4)

    def block_of(shift):
        return 2 * color_at(shift) + c

    def copy(flow, block, chunk, peer, source=None):
        src = weight_view(*(source or (oin, oout)), block, chunk)
        dst = weight_view(oin, oout, block, chunk)
        return remote(src, dst, send.at[flow, chunk], recv.at[flow, chunk], peer)

    def start(*args):
        op = copy(*args)
        op.start()
        started.append(op)

    def first_hop(chunk):
        mine = block_of(0)
        copy(0, mine, chunk, cross).wait_recv()
        start(1, mine, chunk, ahead)
        start(2, mine, chunk, behind)
        start(3, mine, chunk, near)
        start(4, mine, chunk, sibling)

    def second_hop(chunk):
        for flow, shift in ((1, 3), (2, 1), (3, 2)):
            block = block_of(shift)
            copy(flow, block, chunk, near).wait_recv()
            start(4 + shift, block, chunk, sibling)

    def from_sibling(shift, chunks):
        block = 2 * color_at(shift) + (1 - c)
        for chunk in chunks:
            copy(4 + shift, block, chunk, sibling).wait_recv()

    stored = []

    def store(src, dst):
        op = pltpu.make_async_copy(src, dst, stores.at[len(stored)])
        op.start()
        stored.append(op)

    tile = 2 * WBLK

    def activate(block):
        def strip(i, _):
            at = pl.ds(pl.multiple_of(i * STRIP, STRIP), STRIP)
            h, s = gelu_both(pre[at, :])
            hid[block, at, :] = h.astype(jnp.bfloat16)
            slope[block, at, :] = s.astype(jnp.bfloat16)
            return 0

        lax.fori_loop(0, 2 * rows // STRIP, strip, 0)
        there = (block // 2, slice(None), pl.ds(pl.multiple_of((block % 2) * tile, tile), tile))
        store(hid.at[block], hid_hbm.at[there])
        store(slope.at[block], slope_hbm.at[there])

    def up_own(t):
        pre[...] = nn(normed[...], win[:, t * tile : (t + 1) * tile])
        activate(t)

    def down_own(t):
        step = nn(hid[t], wout[t * tile : (t + 1) * tile, :])
        acc[...] = step if t == 0 else acc[...] + step

    def up_other(shift):
        from_sibling(shift, range(W_CHUNKS // 2))
        at = pl.ds(pl.multiple_of(color_at(shift) * tile, tile), tile)
        pre[...] = nn(normed[...], oin[:, at])
        activate(half // tile + color_at(shift))
        store(oin.at[:, at], oin_hbm.at[:, at])

    def down_other(shift):
        from_sibling(shift, range(W_CHUNKS // 2, W_CHUNKS))
        at = pl.ds(pl.multiple_of(color_at(shift) * tile, tile), tile)
        acc[...] += nn(hid[half // tile + color_at(shift)], oout[at, :])
        store(oout.at[at, :], oout_hbm.at[at, :])

    for chunk in range(W_CHUNKS):
        start(0, block_of(2), chunk, cross, (win_hbm, wout_hbm))
    for k, ref in enumerate((q_in, d_in)):
        values = ref[...].astype(jnp.float32)
        inv_rms = lax.rsqrt(jnp.mean(values * values, axis=1, keepdims=True) + EPSILON)
        normed[k * rows : (k + 1) * rows, :] = ((values * inv_rms) * gain_ref[...]).astype(
            jnp.bfloat16
        )
    load_in.wait()
    up_own(0)
    first_hop(0)
    up_own(1)
    first_hop(1)
    second_hop(0)
    up_own(2)
    first_hop(2)
    second_hop(1)
    up_own(3)
    first_hop(3)
    second_hop(2)
    load_out.wait()
    down_own(0)
    down_own(1)
    first_hop(4)
    second_hop(3)
    up_other(0)
    first_hop(5)
    second_hop(4)
    up_other(1)
    first_hop(6)
    second_hop(5)
    up_other(2)
    first_hop(7)
    second_hop(6)
    up_other(3)
    second_hop(7)
    down_own(2)
    down_own(3)
    for shift in (0, 3, 1, 2):
        down_other(shift)
    for k, (ref, emb) in enumerate(((q_in, q_emb), (d_in, d_emb))):
        emb[...] = (ref[...].astype(jnp.float32) + acc[k * rows : (k + 1) * rows, :]).astype(
            jnp.bfloat16
        )
    for op in started:
        op.wait_send()
    for op in stored:
        op.wait()


def forward(q_in, d_in, gain, w_in, w_out):
    rows, width = q_in.shape
    half = w_in.shape[1]
    bf, f32 = jnp.bfloat16, jnp.float32
    tile = 2 * WBLK
    vmem = pl.BlockSpec(memory_space=pltpu.VMEM)
    hbm = pl.BlockSpec(memory_space=pl.ANY)
    per_chunk = jax.ShapeDtypeStruct((CHUNKS, 2 * rows, 2 * half // CHUNKS), bf)
    return pl.pallas_call(
        forward_kernel,
        out_shape=(
            jax.ShapeDtypeStruct(q_in.shape, bf),
            jax.ShapeDtypeStruct(d_in.shape, bf),
            per_chunk,
            per_chunk,
            jax.ShapeDtypeStruct(w_in.shape, bf),
            jax.ShapeDtypeStruct(w_out.shape, bf),
        ),
        in_specs=[vmem] * 3 + [hbm] * 2,
        out_specs=[vmem] * 2 + [hbm] * 4,
        scratch_shapes=[
            pltpu.VMEM(w_in.shape, bf),
            pltpu.VMEM(w_out.shape, bf),
            pltpu.VMEM(w_in.shape, bf),
            pltpu.VMEM(w_out.shape, bf),
            pltpu.VMEM((2 * rows, width), bf),
            pltpu.VMEM((2 * half // tile, 2 * rows, tile), bf),
            pltpu.VMEM((2 * half // tile, 2 * rows, tile), bf),
            pltpu.VMEM((2 * rows, tile), f32),
            pltpu.VMEM((2 * rows, width), f32),
            pltpu.SemaphoreType.DMA((2,)),
            pltpu.SemaphoreType.DMA((2 * 2 * half // tile + 8,)),
            pltpu.SemaphoreType.DMA((8, W_CHUNKS)),
            pltpu.SemaphoreType.DMA((8, W_CHUNKS)),
        ],
        compiler_params=pltpu.CompilerParams(
            collective_id=0, has_side_effects=True, vmem_limit_bytes=56 * MIB
        ),
        name="forward",
    )(q_in, d_in, gain.reshape(1, width), w_in, w_out)


PIECES = (
    (0, 0, 64, 0, 0),
    (1, 0, 16, 0, 0),
    (0, 64, 64, 1, 0),
    (0, 128, 80, 0, 0),
    (0, 208, 48, 1, 1),
    (2, 0, 64, 0, 0),
    (2, 64, 64, 1, 0),
    (2, 128, 80, 0, 0),
    (2, 208, 48, 1, 1),
)
DOC_PIECES = (0, 1, 2, 3, 4)
QUERY_PIECES = (5, 6, 7, 8)
DETOUR_ROWS = 48


def band_kernel(
    docs,
    tags,
    queries,
    column_tag,
    up,
    upt,
    loss,
    gd,
    gx,
    gq,
    transit,
    s,
    w,
    lt,
    mine,
    acc,
    up_v,
    upt_v,
    local,
    send,
    recv,
    tsem,
):
    x, y, zl, c, r = coords()
    b = lax.axis_index("blk")
    rows, width = docs.shape
    inv_root = 1.0 / math.sqrt(width)
    cross = device(x, y, 1 - zl, c, 1 - r)
    near = device(x, y, 1 - zl, c, r)
    sibling = device(x, y, zl, 1 - c, r)
    step = NZ * NC * (1 - 2 * zl)
    onward = {"blk": wrap(b + step, NBLK), "rep": r}
    source = {"blk": wrap(b - step, NBLK), "rep": r}
    peers = []
    for offset in range(-2, 3):
        for other in range(2):
            if offset or other:
                rep = 1 - r if other else r
                peers.append((offset, other, {"blk": wrap(b + offset, NBLK), "rep": rep}))
    own_docs = pltpu.make_async_copy(docs, gd.at[OWN], local.at[0])
    own_queries = pltpu.make_async_copy(queries, gq.at[OWN], local.at[1])
    own_docs.start()
    own_queries.start()
    greet([peer for _, _, peer in peers] + [onward, source])

    def view(slot, p):
        kind, first, count = PIECES[p][:3]
        return (gd, gx, gq)[kind].at[slot, pl.ds(first, count)]

    def own(p):
        kind, first, count = PIECES[p][:3]
        return (docs, tags, queries)[kind].at[pl.ds(first, count)]

    z_slot = 8 - 8 * zl
    far_slot = 8 * zl
    theirs = 8 * zl
    started = []

    def make(flow, p, src, dst, peer):
        return remote(src, dst, send.at[flow, p], recv.at[flow, p], peer)

    def start(*args):
        op = make(*args)
        op.start()
        started.append(op)

    def arrived(flow, p, slot):
        make(flow, p, view(slot, p), view(slot, p), near).wait_recv()

    def band_to_sibling(p):
        return [
            make(7 + k, p, view(8 - 8 * c + k, p), view(6 - 4 * c + k, p), sibling)
            for k in range(2)
        ]

    def through(p):
        return transit.at[p // 5]

    def send_own(p):
        start(0, p, own(p), view(theirs, p), near)
        start(1, p, own(p), view(theirs + 1, p), cross)
        if PIECES[p][4]:
            start(9, p, own(p), through(p), source)
        start(5, p, own(p), view(2 + 4 * c, p), sibling)

    def from_z(p):
        by_near, detour = PIECES[p][3:]
        arrived(0, p, z_slot)
        if not detour:
            start(3, p, view(z_slot, p), view(far_slot, p), onward)
        if not by_near:
            start(2, p, view(z_slot, p), view(OWN + 1, p), cross)
        arrived(1, p, z_slot + 1)
        if not detour:
            start(4, p, view(z_slot + 1, p), view(far_slot + 1, p), onward)
        if by_near:
            start(2, p, view(z_slot + 1, p), view(OWN + 1, p), near)

        @pl.when(c == zl)
        def _():
            for op in band_to_sibling(p):
                op.start()

    def from_transit(p):
        if PIECES[p][4]:
            make(9, p, own(p), through(p), source).wait_recv()
            start(10, p, through(p), view(8 - 8 * zl, p), near)
            start(11, p, through(p), view(8 - 8 * zl + 1, p), cross)

    def from_rep(p):
        arrived(2, p, OWN + 1)
        start(6, p, view(OWN + 1, p), view(3 + 4 * c, p), sibling)

    def from_far(p):
        detour = PIECES[p][4]
        arrived(10 if detour else 3, p, far_slot)
        arrived(11 if detour else 4, p, far_slot + 1)

        @pl.when(c != zl)
        def _():
            for op in band_to_sibling(p):
                op.start()

    def from_sibling(p):
        arrived(5, p, 6 - 4 * c)
        arrived(6, p, 7 - 4 * c)

    def band_from_sibling(p):
        arrived(7, p, 2 + 4 * c)
        arrived(8, p, 3 + 4 * c)

    def hand_out(k, value):
        up_v[k] = value
        turned = jnp.transpose(value).reshape(width // (NC * GROUP), NC, GROUP, rows)
        for core in range(NC):
            upt_v[k, core] = turned[:, core].reshape(width // NC, rows)
        ops = [
            pltpu.make_async_copy(up_v.at[k], up.at[pl.ds(k * rows, rows)], local.at[2 + 2 * k]),
            pltpu.make_async_copy(upt_v.at[k], upt.at[k], local.at[3 + 2 * k]),
        ]
        for op in ops:
            op.start()
        return ops

    row = lax.broadcasted_iota(jnp.int32, (rows, rows), 0)
    col = lax.broadcasted_iota(jnp.int32, (rows, rows), 1)
    diagonal = row == col

    def masked(a, g, slot):
        scores = nt(a[OWN], g[slot]) * inv_root
        tag_row = gx[slot].astype(jnp.float32)[0:1, :]
        allowed = tag_row != column_tag[...]
        if isinstance(slot, int) and slot == OWN:
            allowed = allowed | diagonal
        return scores, jnp.where(allowed, scores, -jnp.inf)

    def score(slot):
        s[slot] = masked(gq, gd, slot)[1]

    def backward_of(slot):
        m = masked(gd, gq, slot)[1]
        wt = jnp.exp(m - lt[slot, 0:1, :])
        if isinstance(slot, int) and slot == OWN:
            wt = wt - diagonal.astype(jnp.float32)
        acc[...] += nn(wt.astype(jnp.bfloat16), gq[slot])

    for p in DOC_PIECES:
        send_own(p)
    gx[OWN] = tags[...]
    own_docs.wait()
    own_queries.wait()
    for p in DOC_PIECES:
        from_z(p)
    for p in QUERY_PIECES:
        send_own(p)
    for p in DOC_PIECES:
        from_transit(p)
    score(OWN)
    positive = jnp.sum(jnp.where(diagonal, s[OWN], 0.0), axis=1, keepdims=True)
    score(z_slot)
    score(z_slot + 1)
    for p in DOC_PIECES:
        from_rep(p)
    for p in DOC_PIECES[:3]:
        from_far(p)
    from_z(QUERY_PIECES[0])
    for p in DOC_PIECES[3:]:
        from_far(p)
    for p in DOC_PIECES:
        from_sibling(p)
    from_z(QUERY_PIECES[1])
    score(OWN + 1)
    score(6 - 4 * c)
    score(7 - 4 * c)
    score(far_slot)
    score(far_slot + 1)
    from_z(QUERY_PIECES[2])
    for p in DOC_PIECES:
        band_from_sibling(p)
    score(2 + 4 * c)
    score(3 + 4 * c)
    top = s[0]
    for slot in range(1, SLOTS):
        top = jnp.maximum(top, s[slot])
    row_max = jnp.max(top, axis=1, keepdims=True)
    total = jnp.exp(s[0] - row_max)
    for slot in range(1, SLOTS):
        total = total + jnp.exp(s[slot] - row_max)
    log_total = row_max + jnp.log(jnp.sum(total, axis=1, keepdims=True))
    loss[...] = jnp.broadcast_to(
        jnp.sum(log_total - positive, axis=0, keepdims=True), loss.shape
    )
    mine[...] = jnp.transpose(jnp.broadcast_to(log_total, (rows, 128)))[0:8, :]
    lt[OWN] = mine[...]
    tops = []
    for i, (offset, other, peer) in enumerate(peers):
        slot = (2 - offset) * 2 + other
        op = remote(mine, lt.at[slot], tsem.at[0, i], tsem.at[1, slot], peer)
        op.start()
        tops.append(op)
    from_z(QUERY_PIECES[3])
    for p in QUERY_PIECES:
        from_transit(p)
    for slot in range(SLOTS):
        wt = jnp.exp(s[slot] - log_total)
        if slot == OWN:
            wt = wt - diagonal.astype(jnp.float32)
        w[:, slot * rows : (slot + 1) * rows] = wt.astype(jnp.bfloat16)
    query_grad = nn(w[...], gd[...].reshape(SLOTS * rows, width))
    outs = hand_out(0, (query_grad * inv_root).astype(jnp.bfloat16))

    for slot in range(SLOTS):
        if slot != OWN:
            remote(mine, lt.at[slot], tsem.at[0, 0], tsem.at[1, slot], near).wait_recv()
    for p in QUERY_PIECES:
        from_rep(p)
    acc[...] = jnp.zeros_like(acc)
    backward_of(OWN)
    backward_of(z_slot)
    backward_of(z_slot + 1)
    backward_of(OWN + 1)
    for p in QUERY_PIECES:
        from_sibling(p)
    backward_of(6 - 4 * c)
    backward_of(7 - 4 * c)
    for p in QUERY_PIECES:
        from_far(p)
    backward_of(far_slot)
    backward_of(far_slot + 1)
    for p in QUERY_PIECES:
        band_from_sibling(p)
    backward_of(2 + 4 * c)
    backward_of(3 + 4 * c)
    outs += hand_out(1, (acc[...] * inv_root).astype(jnp.bfloat16))

    for p in range(len(PIECES)):
        for op in band_to_sibling(p):
            op.wait_send()
    for op in started + tops:
        op.wait_send()
    for op in outs:
        op.wait()


def band(docs, tags, queries, column_tag):
    rows, width = docs.shape
    bf, f32 = jnp.bfloat16, jnp.float32
    vmem = pl.BlockSpec(memory_space=pltpu.VMEM)
    hbm = pl.BlockSpec(memory_space=pl.ANY)
    return pl.pallas_call(
        band_kernel,
        out_shape=(
            jax.ShapeDtypeStruct((2 * rows, width), bf),
            jax.ShapeDtypeStruct((2, NC, width // NC, rows), bf),
            jax.ShapeDtypeStruct((8, 128), f32),
        ),
        in_specs=[hbm, vmem, hbm, vmem],
        out_specs=[hbm, hbm, vmem],
        scratch_shapes=[
            pltpu.VMEM((SLOTS, rows, width), bf),
            pltpu.VMEM((SLOTS,) + tags.shape, bf),
            pltpu.VMEM((SLOTS, rows, width), bf),
            pltpu.VMEM((2, DETOUR_ROWS, width), bf),
            pltpu.VMEM((SLOTS, rows, rows), f32),
            pltpu.VMEM((rows, SLOTS * rows), bf),
            pltpu.VMEM((SLOTS, 8, rows), f32),
            pltpu.VMEM((8, rows), f32),
            pltpu.VMEM((rows, width), f32),
            pltpu.VMEM((2, rows, width), bf),
            pltpu.VMEM((2, NC, width // NC, rows), bf),
            pltpu.SemaphoreType.DMA((6,)),
            pltpu.SemaphoreType.DMA((12, len(PIECES))),
            pltpu.SemaphoreType.DMA((12, len(PIECES))),
            pltpu.SemaphoreType.DMA((2, SLOTS)),
        ],
        compiler_params=pltpu.CompilerParams(
            collective_id=1, has_side_effects=True, vmem_limit_bytes=60 * MIB
        ),
        name="band",
    )(docs, tags, queries, column_tag)


PARTS = (
    (0, 0, 768, "x"),
    (0, 768, 768, "y"),
    (0, 1536, 512, "z"),
    (1, 0, 768, "x"),
    (1, 768, 768, "y"),
    (1, 1536, 512, "z"),
)
WIDE, NARROW = 768, 512
CHUNKS = 4


def backward_kernel(
    q_hbm,
    d_hbm,
    up_hbm,
    upt_hbm,
    gain_ref,
    loss_ref,
    hid_hbm,
    slope_hbm,
    win_hbm,
    oin_hbm,
    wout_hbm,
    oout_hbm,
    out,
    total,
    grads,
    in_v,
    up_ref,
    upt_ref,
    hid,
    slope,
    win,
    wout,
    s1,
    r1,
    a1,
    r2,
    a2,
    r3,
    a3,
    r4,
    r2z,
    a2z,
    r3z,
    a3z,
    r4z,
    acc,
    s_buf,
    local,
    sems,
):
    x, y, zl, c, r = coords()
    rows, width = q_hbm.shape
    half = win_hbm.shape[1]
    cols = 2 * half // CHUNKS
    per_half = CHUNKS // 2
    sibling = device(x, y, zl, 1 - c, r)
    xs = [device(wrap(x + k, NX), y, zl, c, r) for k in range(1, RING)]
    ys = [device(x, wrap(y + k, NY), zl, c, r) for k in range(1, RING)]
    zs = [device(x, y, 1 - zl, c, r), device(x, y, zl, c, 1 - r), device(x, y, 1 - zl, c, 1 - r)]

    loads = []
    n_loads = [0]

    def load(src, dst):
        nonlocal loads
        op = pltpu.make_async_copy(src, dst, local.at[n_loads[0]])
        op.start()
        n_loads[0] += 1
        loads.append(op)
        return op

    first_loads = [load(upt_hbm.at[k], upt_ref.at[k]) for k in range(2)]
    loads = []
    for j in range(CHUNKS):
        load(hid_hbm.at[j], hid.at[j // per_half, :, pl.ds(j % per_half * cols, cols)])
    for j in range(CHUNKS):
        load(slope_hbm.at[j], slope.at[j])
    for k, (inner, outer) in enumerate(((win_hbm, wout_hbm), (oin_hbm, oout_hbm))):
        load(inner, win.at[k])
        load(outer, wout.at[k])
    late_loads = [
        load(up_hbm, up_ref),
        load(q_hbm, in_v.at[pl.ds(0, rows)]),
        load(d_hbm, in_v.at[pl.ds(rows, rows)]),
    ]

    greet([sibling] + xs + ys + zs)
    state = {"n": 0}
    ops = []

    def send(src, dst, peer):
        n = state["n"]
        state["n"] = n + 1
        op = remote(src, dst, sems.at[0, n], sems.at[1, n], peer)
        op.start()
        ops.append(op)
        return op

    def down_part(core, k, at):
        return nn(upt_ref[0, core], hid[k, 0:rows, at]) + nn(upt_ref[1, core], hid[k, rows:, at])

    wait1 = []
    for op in first_loads:
        op.wait()
    n_loaded = 0
    for k, first, count, _ in PARTS:
        at = slice(first, first + count)
        while n_loaded * cols < k * half + first + count:
            loads[n_loaded].wait()
            n_loaded += 1
        s1[k, :, at] = down_part(1 - c, k, at).astype(jnp.bfloat16)
        view = (k, slice(None), pl.ds(first, count))
        wait1.append(send(s1.at[view], r1.at[view], sibling))

    wait2 = []
    waitz = []
    for p, (k, first, count, axis) in enumerate(PARTS):
        at = slice(first, first + count)
        mine = down_part(c, k, at)
        wait1[p].wait_recv()
        mine = mine + r1[k, :, at].astype(jnp.float32)
        a1[k, :, :, :, :, at] = mine.astype(jnp.bfloat16).reshape(NX, NY, NZ, GROUP, count)
        part = pl.ds(first, count)
        waits = []
        if axis == "z":
            if k == 0:
                waitz.append(send(a1.at[k, :, :, 1 - zl, :, part], r2z.at[0], zs[0]))
            else:
                waitz.append(send(a1.at[k, :, :, zl, :, part], r2z.at[1], zs[1]))
                waitz.append(send(a1.at[k, :, :, 1 - zl, :, part], r2z.at[2], zs[2]))
        for n in range(1, RING):
            slot = RING - 1 - n
            if axis == "x":
                src = a1.at[k, wrap(x + n, NX), :, :, :, part]
                waits.append(send(src, r2.at[k, 0, slot], xs[n - 1]))
            elif axis == "y":
                src = a1.at[k, :, wrap(y + n, NY), :, :, part]
                waits.append(send(src, r2.at[k, 1, slot], ys[n - 1]))
        wait2.append(waits)

    for j in range(CHUNKS):
        loads[CHUNKS + j].wait()
    for k in range(2):
        loads[2 * CHUNKS + 2 * k].wait()
        loads[2 * CHUNKS + 2 * k + 1].wait()
    for op in late_loads:
        op.wait()
    tile = 512
    for j in range(CHUNKS):
        k = j // per_half

        def tile_step(t, _, j=j, k=k):
            first = pl.multiple_of(t * tile, tile)
            there = pl.multiple_of((j % per_half) * cols + t * tile, tile)
            g_act = nt(up_ref[...], wout[k, pl.ds(there, tile), :])
            g_pre = (g_act * slope[j, :, pl.ds(first, tile)].astype(jnp.float32)).astype(
                jnp.bfloat16
            )
            step = nt(g_pre, win[k, :, pl.ds(there, tile)])
            if j == 0:
                before = jnp.where(t == 0, 0.0, acc[...])
            else:
                before = acc[...]
            acc[...] = before + step
            return 0

        if j == 0:
            acc[...] = jnp.zeros_like(acc)
        lax.fori_loop(0, cols // tile, tile_step, 0)

    values = in_v[...].astype(jnp.float32)
    inv_rms = lax.rsqrt(jnp.mean(values * values, axis=1, keepdims=True) + EPSILON)
    unit_rows = values * inv_rms
    g_norm = acc[...]
    weighted = g_norm * unit_rows
    gain_term = jnp.sum(weighted, axis=0, keepdims=True)
    gain = gain_ref[...]
    mean = jnp.mean(weighted * gain, axis=1, keepdims=True)
    d_values = inv_rms * (g_norm * gain - unit_rows * mean)
    grads[...] = (up_ref[...].astype(jnp.float32) + d_values).astype(jnp.bfloat16)

    row = lax.broadcasted_iota(jnp.int32, (8, width), 0)
    s_buf[12] = jnp.where(
        row == 0,
        jnp.broadcast_to(gain_term, (8, width)),
        jnp.broadcast_to(loss_ref[0:1, 0:1], (8, width)),
    )
    small = send(s_buf.at[12], s_buf.at[13], sibling)
    small.wait_recv()
    s_buf[x] = s_buf[12] + s_buf[13]
    small = [send(s_buf.at[x], s_buf.at[x], peer) for peer in xs]

    wait3 = {}

    def second(p):
        k, first, count, axis = PARTS[p]
        at = slice(first, first + count)
        i = 0 if axis == "x" else 1
        for op in wait2[p]:
            op.wait_recv()
        tot = (a1[k, x, :, :, :, at] if i == 0 else a1[k, :, y, :, :, at]).astype(jnp.float32)
        for n in range(RING - 1):
            tot = tot + r2[k, i, n].astype(jnp.float32)
        a2[k, i] = tot.astype(jnp.bfloat16)
        wait3[p] = []
        for n in range(1, RING):
            slot = RING - 1 - n
            if i == 0:
                op = send(a2.at[k, i, wrap(y + n, NY)], r3.at[k, i, slot], ys[n - 1])
            else:
                op = send(a2.at[k, i, wrap(x + n, NX)], r3.at[k, i, slot], xs[n - 1])
            wait3[p].append(op)

    def second_z():
        k, first, count, _ = PARTS[2]
        for op in waitz:
            op.wait_recv()
        tot = a1[k, :, :, zl, :, first : first + count].astype(jnp.float32)
        for n in range(RING - 1):
            tot = tot + r2z[n].astype(jnp.float32)
        a2z[...] = tot.astype(jnp.bfloat16)
        return [
            send(a2z.at[wrap(x + n, NX)], r3z.at[RING - 1 - n], xs[n - 1]) for n in range(1, RING)
        ]

    def third_z(waits):
        for op in waits:
            op.wait_recv()
        tot = a2z[x].astype(jnp.float32)
        for n in range(RING - 1):
            tot = tot + r3z[n].astype(jnp.float32)
        a3z[...] = tot.astype(jnp.bfloat16)
        return [
            send(a3z.at[wrap(y + n, NY)], r4z.at[RING - 1 - n], ys[n - 1]) for n in range(1, RING)
        ]

    second(0)
    second(1)
    for op in small:
        op.wait_recv()
    s_buf[4 + y] = ((s_buf[0] + s_buf[1]) + s_buf[2]) + s_buf[3]
    small = [send(s_buf.at[4 + y], s_buf.at[4 + y], peer) for peer in ys]
    waitz = second_z()
    second(3)
    second(4)
    waitz = third_z(waitz)

    for op in small:
        op.wait_recv()
    here = s_buf.at[8 + 2 * r + zl]
    here[...] = ((s_buf[4] + s_buf[5]) + s_buf[6]) + s_buf[7]
    small = [send(here, here, peer) for peer in zs]

    wait4 = [[], []]
    for p in (0, 1, 3, 4):
        k, first, count, axis = PARTS[p]
        i = 0 if axis == "x" else 1
        for op in wait3[p]:
            op.wait_recv()
        tot = (a2[k, i, y] if i == 0 else a2[k, i, x]).astype(jnp.float32)
        for n in range(RING - 1):
            tot = tot + r3[k, i, n].astype(jnp.float32)
        a3[k, i] = tot.astype(jnp.bfloat16)
        if k == 0:
            wait4[i].append(send(a3.at[k, i, 1 - zl], r4.at[i, 0], zs[0]))
        else:
            wait4[i].append(send(a3.at[k, i, zl], r4.at[i, 1], zs[1]))
            wait4[i].append(send(a3.at[k, i, 1 - zl], r4.at[i, 2], zs[2]))
    for op in waitz:
        op.wait_recv()
    first = PARTS[2][1]
    tot = a3z[y].astype(jnp.float32)
    for n in range(RING - 1):
        tot = tot + r4z[n].astype(jnp.float32)
    out[:, first : first + NARROW] = tot
    for i in range(2):
        for op in wait4[i]:
            op.wait_recv()
        out[:, i * WIDE : (i + 1) * WIDE] = (
            a3[0, i, zl].astype(jnp.float32) + r4[i, 0].astype(jnp.float32)
        ) + (r4[i, 1].astype(jnp.float32) + r4[i, 2].astype(jnp.float32))
    for op in small:
        op.wait_recv()
    total[...] = (s_buf[8] + s_buf[9]) + (s_buf[10] + s_buf[11])
    for op in ops:
        op.wait_send()


def backward(q_in, d_in, up, upt, gain, loss_part, hidden, slope, w_in, o_in, w_out, o_out):
    rows, width = 2 * q_in.shape[0], q_in.shape[1]
    half = w_in.shape[1]
    cols = 2 * half // CHUNKS
    groups = NX * NY * NZ
    bf, f32 = jnp.bfloat16, jnp.float32
    vmem = pl.BlockSpec(memory_space=pltpu.VMEM)
    hbm = pl.BlockSpec(memory_space=pl.ANY)
    return pl.pallas_call(
        backward_kernel,
        out_shape=(
            jax.ShapeDtypeStruct((GROUP, half), f32),
            jax.ShapeDtypeStruct((8, width), f32),
            jax.ShapeDtypeStruct((rows, width), bf),
        ),
        in_specs=[hbm] * 4 + [vmem] * 2 + [hbm] * 6,
        out_specs=[vmem] * 3,
        scratch_shapes=[
            pltpu.VMEM((rows, width), bf),
            pltpu.VMEM((rows, width), bf),
            pltpu.VMEM(upt.shape, bf),
            pltpu.VMEM((2, rows, half), bf),
            pltpu.VMEM((CHUNKS, rows, cols), bf),
            pltpu.VMEM((2,) + w_in.shape, bf),
            pltpu.VMEM((2,) + w_out.shape, bf),
            pltpu.VMEM((2, groups * GROUP, half), bf),
            pltpu.VMEM((2, groups * GROUP, half), bf),
            pltpu.VMEM((2, NX, NY, NZ, GROUP, half), bf),
            pltpu.VMEM((2, 2, RING - 1, RING, NZ, GROUP, WIDE), bf),
            pltpu.VMEM((2, 2, RING, NZ, GROUP, WIDE), bf),
            pltpu.VMEM((2, 2, RING - 1, NZ, GROUP, WIDE), bf),
            pltpu.VMEM((2, 2, NZ, GROUP, WIDE), bf),
            pltpu.VMEM((2, RING - 1, GROUP, WIDE), bf),
            pltpu.VMEM((RING - 1, NX, NY, GROUP, NARROW), bf),
            pltpu.VMEM((NX, NY, GROUP, NARROW), bf),
            pltpu.VMEM((RING - 1, NY, GROUP, NARROW), bf),
            pltpu.VMEM((NY, GROUP, NARROW), bf),
            pltpu.VMEM((RING - 1, GROUP, NARROW), bf),
            pltpu.VMEM((rows, width), f32),
            pltpu.VMEM((14, 8, width), f32),
            pltpu.SemaphoreType.DMA((2 * CHUNKS + 9,)),
            pltpu.SemaphoreType.DMA((2, 64)),
        ],
        compiler_params=pltpu.CompilerParams(
            collective_id=3, has_side_effects=True, vmem_limit_bytes=60 * MIB
        ),
        name="backward",
    )(
        q_in,
        d_in,
        up,
        upt,
        gain.reshape(1, width),
        loss_part,
        hidden,
        slope,
        w_in,
        o_in,
        w_out,
        o_out,
    )


def finish_kernel(down, total, grads, down_out, gain_out, loss_out, q_out, d_out):
    rows = q_out.shape[0]
    down_out[...] = down[...]
    gain_out[...] = total[0:1, :]
    loss_out[...] = total[1:2, 0:1] * (1.0 / (rows * 2 * NBLK))
    q_out[...] = grads[0:rows, :]
    d_out[...] = grads[rows : 2 * rows, :]


def finish(down, total, grads):
    rows, width = grads.shape[0] // 2, grads.shape[1]
    f32 = jnp.float32
    row_grads = jax.ShapeDtypeStruct((rows, width), grads.dtype)
    return pl.pallas_call(
        finish_kernel,
        out_shape=(
            jax.ShapeDtypeStruct(down.shape, f32),
            jax.ShapeDtypeStruct((1, width), f32),
            jax.ShapeDtypeStruct((1, 1), f32),
            row_grads,
            row_grads,
        ),
        name="finish",
    )(down, total, grads)


def on_device(query_in, doc_in, cluster, gain, w_in, w_out):
    rows, width = query_in.shape
    queries, docs, hidden, slope, o_in, o_out = forward(query_in, doc_in, gain, w_in, w_out)

    tags = jnp.broadcast_to(cluster.astype(jnp.bfloat16)[None, :], (16, rows))
    column_tag = cluster.astype(jnp.float32)[:, None]
    up, upt, loss_part = band(docs, tags, queries, column_tag)
    sums = backward(
        query_in, doc_in, up, upt, gain, loss_part, hidden, slope, w_in, o_in, w_out, o_out
    )
    down_t, gain_total, loss, q_grads, d_grads = finish(*sums)
    return (loss.reshape(()), down_t.T, gain_total.reshape(width), q_grads, d_grads)


def solution(mesh):
    in_specs = (
        P(("blk", "rep"), None),
        P(("blk", "rep"), None),
        P(("blk", "rep")),
        P(),
        P(None, "rep"),
        P("rep", None),
    )
    out_specs = (P(), P("rep", "blk"), P(), P(("blk", "rep"), None), P(("blk", "rep"), None))
    return jax.shard_map(
        on_device, mesh=mesh, in_specs=in_specs, out_specs=out_specs, check_vma=False
    )
```

```python
import math

import jax
import jax.numpy as jnp
from jax import lax
from jax.experimental import pallas as pl
from jax.experimental.pallas import tpu as pltpu
from jax.sharding import PartitionSpec as P

MESH = pl.DeviceIdType.MESH
MIB = 2**20
NX, NY, NZ, NC = 4, 4, 2, 2
NBLK = NX * NY * NZ * NC
RING = NX
EPSILON = 1e-06
SLOTS = 10
OWN = 4
GROUP = 16


def coords():
    b = lax.axis_index("blk")
    r = lax.axis_index("rep")
    return b // (NY * NZ * NC), (b // (NZ * NC)) % NY, (b // NC) % NZ, b % NC, r


def device(x, y, zl, c, r):
    return {"blk": ((x * NY + y) * NZ + zl) * NC + c, "rep": r}


def wrap(v, n):
    return lax.rem(v + n, n)


def greet(peers):
    barrier = pltpu.get_barrier_semaphore()
    for peer in peers:
        pl.semaphore_signal(barrier, inc=1, device_id=peer, device_id_type=MESH)
    pl.semaphore_wait(barrier, len(peers))


def remote(src, dst, send, recv, peer):
    return pltpu.make_async_remote_copy(
        src_ref=src,
        dst_ref=dst,
        send_sem=send,
        recv_sem=recv,
        device_id=peer,
        device_id_type=MESH,
    )


WBLK = 256
W_CHUNKS = 8
STRIP = 64


def nt(a, b):
    return lax.dot_general(a, b, (((1,), (1,)), ((), ())), preferred_element_type=jnp.float32)


def nn(a, b):
    return lax.dot_general(a, b, (((1,), (0,)), ((), ())), preferred_element_type=jnp.float32)


def gelu_both(p):
    k = math.sqrt(2.0 / math.pi)
    square = p * p
    t = jnp.tanh(p * (k + (k * 0.044715) * square))
    up = 0.5 + 0.5 * t
    slope = up + (0.5 * p) * ((1.0 - t * t) * (k + (3 * k * 0.044715) * square))
    return p * up, slope


def weight_view(in_ref, out_ref, block, chunk):
    if chunk < W_CHUNKS // 2:
        rows = in_ref.shape[0] // (W_CHUNKS // 2)
        return in_ref.at[
            pl.ds(chunk * rows, rows), pl.ds(pl.multiple_of(block * WBLK, WBLK), WBLK)
        ]
    rows = WBLK // (W_CHUNKS // 2)
    first = block * WBLK + (chunk - W_CHUNKS // 2) * rows
    return out_ref.at[pl.ds(pl.multiple_of(first, rows), rows)]


def forward_part(
    q_in,
    d_in,
    gain_ref,
    win_hbm,
    wout_hbm,
    hid_hbm,
    slope_hbm,
    oin_hbm,
    oout_hbm,
    win,
    wout,
    oin,
    oout,
    normed,
    hid,
    slope,
    pre,
    acc,
    local,
    stores,
    send,
    recv,
    meet,
):
    x, y, zl, c, r = coords()
    cross = device(x, y, 1 - zl, c, 1 - r)
    near = device(x, y, 1 - zl, c, r)
    ahead = device(wrap(x + 1, NX), y, zl, c, r)
    behind = device(wrap(x - 1, NX), y, zl, c, r)
    sibling = device(x, y, zl, 1 - c, r)
    half = win_hbm.shape[1]
    rows = q_in.shape[0]
    load_in = pltpu.make_async_copy(win_hbm, win, local.at[0])
    load_out = pltpu.make_async_copy(wout_hbm, wout, local.at[1])
    load_in.start()
    load_out.start()
    meet([ahead, behind])
    color = lax.rem(x + 2 * zl, 4)
    started = []

    def color_at(shift):
        return lax.rem(color + shift, 4)

    def block_of(shift):
        return 2 * color_at(shift) + c

    def copy(flow, block, chunk, peer, source=None):
        src = weight_view(*(source or (oin, oout)), block, chunk)
        dst = weight_view(oin, oout, block, chunk)
        return remote(src, dst, send.at[flow, chunk], recv.at[flow, chunk], peer)

    def start(*args):
        op = copy(*args)
        op.start()
        started.append(op)

    def first_hop(chunk):
        mine = block_of(0)
        copy(0, mine, chunk, cross).wait_recv()
        start(1, mine, chunk, ahead)
        start(2, mine, chunk, behind)
        start(3, mine, chunk, near)
        start(4, mine, chunk, sibling)

    def second_hop(chunk):
        for flow, shift in ((1, 3), (2, 1), (3, 2)):
            block = block_of(shift)
            copy(flow, block, chunk, near).wait_recv()
            start(4 + shift, block, chunk, sibling)

    def from_sibling(shift, chunks):
        block = 2 * color_at(shift) + (1 - c)
        for chunk in chunks:
            copy(4 + shift, block, chunk, sibling).wait_recv()

    stored = []

    def store(src, dst):
        op = pltpu.make_async_copy(src, dst, stores.at[len(stored)])
        op.start()
        stored.append(op)

    tile = 2 * WBLK

    def activate(block):
        def strip(i, _):
            at = pl.ds(pl.multiple_of(i * STRIP, STRIP), STRIP)
            h, s = gelu_both(pre[at, :])
            hid[block, at, :] = h.astype(jnp.bfloat16)
            slope[block, at, :] = s.astype(jnp.bfloat16)
            return 0

        lax.fori_loop(0, 2 * rows // STRIP, strip, 0)
        there = (block // 2, slice(None), pl.ds(pl.multiple_of((block % 2) * tile, tile), tile))
        store(hid.at[block], hid_hbm.at[there])
        store(slope.at[block], slope_hbm.at[there])

    def up_own(t):
        pre[...] = nn(normed[...], win[:, t * tile : (t + 1) * tile])
        activate(t)

    def down_own(t):
        step = nn(hid[t], wout[t * tile : (t + 1) * tile, :])
        acc[...] = step if t == 0 else acc[...] + step

    def up_other(shift):
        from_sibling(shift, range(W_CHUNKS // 2))
        at = pl.ds(pl.multiple_of(color_at(shift) * tile, tile), tile)
        pre[...] = nn(normed[...], oin[:, at])
        activate(half // tile + color_at(shift))
        store(oin.at[:, at], oin_hbm.at[:, at])

    def down_other(shift):
        from_sibling(shift, range(W_CHUNKS // 2, W_CHUNKS))
        at = pl.ds(pl.multiple_of(color_at(shift) * tile, tile), tile)
        acc[...] += nn(hid[half // tile + color_at(shift)], oout[at, :])
        store(oout.at[at, :], oout_hbm.at[at, :])

    for chunk in range(W_CHUNKS):
        start(0, block_of(2), chunk, cross, (win_hbm, wout_hbm))
    for k, ref in enumerate((q_in, d_in)):
        values = ref[...].astype(jnp.float32)
        inv_rms = lax.rsqrt(jnp.mean(values * values, axis=1, keepdims=True) + EPSILON)
        normed[k * rows : (k + 1) * rows, :] = ((values * inv_rms) * gain_ref[...]).astype(
            jnp.bfloat16
        )
    load_in.wait()
    up_own(0)
    first_hop(0)
    up_own(1)
    first_hop(1)
    second_hop(0)
    up_own(2)
    first_hop(2)
    second_hop(1)
    up_own(3)
    first_hop(3)
    second_hop(2)
    load_out.wait()
    down_own(0)
    down_own(1)
    first_hop(4)
    second_hop(3)
    up_other(0)
    first_hop(5)
    second_hop(4)
    up_other(1)
    first_hop(6)
    second_hop(5)
    up_other(2)
    first_hop(7)
    second_hop(6)
    up_other(3)
    second_hop(7)
    down_own(2)
    down_own(3)
    for shift in (0, 3, 1):
        down_other(shift)
    from_sibling(2, range(W_CHUNKS // 2, W_CHUNKS))
    last = pl.ds(pl.multiple_of(color_at(2) * tile, tile), tile)
    store(oout.at[last, :], oout_hbm.at[last, :])

    def embed(k):
        at = slice(k * rows, (k + 1) * rows)
        mixed = acc[at, :] + nn(hid[half // tile + color_at(2), at, :], oout[last, :])
        return ((q_in, d_in)[k][...].astype(jnp.float32) + mixed).astype(jnp.bfloat16)

    return embed, started, stored


PIECES = (
    (0, 0, 64, 0, 0),
    (1, 0, 16, 0, 0),
    (0, 64, 64, 1, 0),
    (0, 128, 80, 0, 0),
    (0, 208, 48, 1, 1),
    (2, 0, 64, 0, 0),
    (2, 64, 64, 1, 0),
    (2, 128, 80, 0, 0),
    (2, 208, 48, 1, 1),
)
DOC_PIECES = (0, 1, 2, 3, 4)
QUERY_PIECES = (5, 6, 7, 8)
DETOUR_ROWS = 48


def layer_kernel(*refs):
    ins, outs, scratch = refs[:7], refs[7:14], refs[14:]
    q_in, d_in, gain_ref, tags, column_tag, win_hbm, wout_hbm = ins
    up, upt, loss, hid_hbm, slope_hbm, oin_hbm, oout_hbm = outs
    forward_scratch, band_scratch = scratch[:13], scratch[13:]
    b = lax.axis_index("blk")
    zl = coords()[2]
    r = lax.axis_index("rep")
    step = NZ * NC * (1 - 2 * zl)
    onward = {"blk": wrap(b + step, NBLK), "rep": r}
    source = {"blk": wrap(b - step, NBLK), "rep": r}
    peers = []
    for offset in range(-2, 3):
        for other in range(2):
            if offset or other:
                rep = 1 - r if other else r
                peers.append((offset, other, {"blk": wrap(b + offset, NBLK), "rep": rep}))

    def meet(more):
        greet([peer for _, _, peer in peers] + [onward, source] + more)

    embed, started, stored = forward_part(
        q_in,
        d_in,
        gain_ref,
        win_hbm,
        wout_hbm,
        hid_hbm,
        slope_hbm,
        oin_hbm,
        oout_hbm,
        *forward_scratch,
        meet,
    )
    band_part(tags, column_tag, up, upt, loss, *band_scratch, embed, peers, onward, source)
    for op in started:
        op.wait_send()
    for op in stored:
        op.wait()


def band_part(
    tags,
    column_tag,
    up,
    upt,
    loss,
    gd,
    gx,
    gq,
    transit,
    s,
    w,
    lt,
    mine,
    acc,
    up_v,
    upt_v,
    local,
    send,
    recv,
    tsem,
    embed,
    peers,
    onward,
    source,
):
    x, y, zl, c, r = coords()
    rows, width = gd.shape[1:]
    inv_root = 1.0 / math.sqrt(width)
    cross = device(x, y, 1 - zl, c, 1 - r)
    near = device(x, y, 1 - zl, c, r)
    sibling = device(x, y, zl, 1 - c, r)

    def view(slot, p):
        kind, first, count = PIECES[p][:3]
        return (gd, gx, gq)[kind].at[slot, pl.ds(first, count)]

    def own(p):
        return view(OWN, p)

    z_slot = 8 - 8 * zl
    far_slot = 8 * zl
    theirs = 8 * zl
    started = []

    def make(flow, p, src, dst, peer):
        return remote(src, dst, send.at[flow, p], recv.at[flow, p], peer)

    def start(*args):
        op = make(*args)
        op.start()
        started.append(op)

    def arrived(flow, p, slot):
        make(flow, p, view(slot, p), view(slot, p), near).wait_recv()

    def band_to_sibling(p):
        return [
            make(7 + k, p, view(8 - 8 * c + k, p), view(6 - 4 * c + k, p), sibling)
            for k in range(2)
        ]

    def through(p):
        return transit.at[p // 5]

    def send_own(p):
        start(0, p, own(p), view(theirs, p), near)
        start(1, p, own(p), view(theirs + 1, p), cross)
        if PIECES[p][4]:
            start(9, p, own(p), through(p), source)
        start(5, p, own(p), view(2 + 4 * c, p), sibling)

    def from_z(p):
        by_near, detour = PIECES[p][3:]
        arrived(0, p, z_slot)
        if not detour:
            start(3, p, view(z_slot, p), view(far_slot, p), onward)
        if not by_near:
            start(2, p, view(z_slot, p), view(OWN + 1, p), cross)
        arrived(1, p, z_slot + 1)
        if not detour:
            start(4, p, view(z_slot + 1, p), view(far_slot + 1, p), onward)
        if by_near:
            start(2, p, view(z_slot + 1, p), view(OWN + 1, p), near)

        @pl.when(c == zl)
        def _():
            for op in band_to_sibling(p):
                op.start()

    def from_transit(p):
        if PIECES[p][4]:
            make(9, p, own(p), through(p), source).wait_recv()
            start(10, p, through(p), view(8 - 8 * zl, p), near)
            start(11, p, through(p), view(8 - 8 * zl + 1, p), cross)

    def from_rep(p):
        arrived(2, p, OWN + 1)
        start(6, p, view(OWN + 1, p), view(3 + 4 * c, p), sibling)

    def from_far(p):
        detour = PIECES[p][4]
        arrived(10 if detour else 3, p, far_slot)
        arrived(11 if detour else 4, p, far_slot + 1)

        @pl.when(c != zl)
        def _():
            for op in band_to_sibling(p):
                op.start()

    def from_sibling(p):
        arrived(5, p, 6 - 4 * c)
        arrived(6, p, 7 - 4 * c)

    def band_from_sibling(p):
        arrived(7, p, 2 + 4 * c)
        arrived(8, p, 3 + 4 * c)

    def hand_out(k, value):
        up_v[k] = value
        turned = jnp.transpose(value).reshape(width // (NC * GROUP), NC, GROUP, rows)
        for core in range(NC):
            upt_v[k, core] = turned[:, core].reshape(width // NC, rows)
        ops = [
            pltpu.make_async_copy(up_v.at[k], up.at[pl.ds(k * rows, rows)], local.at[2 * k]),
            pltpu.make_async_copy(upt_v.at[k], upt.at[k], local.at[1 + 2 * k]),
        ]
        for op in ops:
            op.start()
        return ops

    row = lax.broadcasted_iota(jnp.int32, (rows, rows), 0)
    col = lax.broadcasted_iota(jnp.int32, (rows, rows), 1)
    diagonal = row == col

    def masked(a, g, slot):
        scores = nt(a[OWN], g[slot]) * inv_root
        tag_row = gx[slot].astype(jnp.float32)[0:1, :]
        allowed = tag_row != column_tag[...]
        if isinstance(slot, int) and slot == OWN:
            allowed = allowed | diagonal
        return scores, jnp.where(allowed, scores, -jnp.inf)

    def score(slot):
        s[slot] = masked(gq, gd, slot)[1]

    def backward_of(slot):
        m = masked(gd, gq, slot)[1]
        wt = jnp.exp(m - lt[slot, 0:1, :])
        if isinstance(slot, int) and slot == OWN:
            wt = wt - diagonal.astype(jnp.float32)
        acc[...] += nn(wt.astype(jnp.bfloat16), gq[slot])

    gx[OWN] = tags[...]
    gd[OWN] = embed(1)
    for p in DOC_PIECES:
        send_own(p)
    gq[OWN] = embed(0)
    for p in DOC_PIECES:
        from_z(p)
    for p in QUERY_PIECES:
        send_own(p)
    for p in DOC_PIECES:
        from_transit(p)
    score(OWN)
    positive = jnp.sum(jnp.where(diagonal, s[OWN], 0.0), axis=1, keepdims=True)
    score(z_slot)
    score(z_slot + 1)
    for p in DOC_PIECES:
        from_rep(p)
    for p in DOC_PIECES[:3]:
        from_far(p)
    from_z(QUERY_PIECES[0])
    for p in DOC_PIECES[3:]:
        from_far(p)
    for p in DOC_PIECES:
        from_sibling(p)
    from_z(QUERY_PIECES[1])
    score(OWN + 1)
    score(6 - 4 * c)
    score(7 - 4 * c)
    score(far_slot)
    score(far_slot + 1)
    from_z(QUERY_PIECES[2])
    for p in DOC_PIECES:
        band_from_sibling(p)
    score(2 + 4 * c)
    score(3 + 4 * c)
    top = s[0]
    for slot in range(1, SLOTS):
        top = jnp.maximum(top, s[slot])
    row_max = jnp.max(top, axis=1, keepdims=True)
    total = jnp.exp(s[0] - row_max)
    for slot in range(1, SLOTS):
        total = total + jnp.exp(s[slot] - row_max)
    log_total = row_max + jnp.log(jnp.sum(total, axis=1, keepdims=True))
    loss[...] = jnp.broadcast_to(
        jnp.sum(log_total - positive, axis=0, keepdims=True), loss.shape
    )
    mine[...] = jnp.transpose(jnp.broadcast_to(log_total, (rows, 128)))[0:8, :]
    lt[OWN] = mine[...]
    tops = []
    for i, (offset, other, peer) in enumerate(peers):
        slot = (2 - offset) * 2 + other
        op = remote(mine, lt.at[slot], tsem.at[0, i], tsem.at[1, slot], peer)
        op.start()
        tops.append(op)
    from_z(QUERY_PIECES[3])
    for p in QUERY_PIECES:
        from_transit(p)
    for slot in range(SLOTS):
        wt = jnp.exp(s[slot] - log_total)
        if slot == OWN:
            wt = wt - diagonal.astype(jnp.float32)
        w[:, slot * rows : (slot + 1) * rows] = wt.astype(jnp.bfloat16)
    query_grad = nn(w[...], gd[...].reshape(SLOTS * rows, width))
    outs = hand_out(0, (query_grad * inv_root).astype(jnp.bfloat16))

    for slot in range(SLOTS):
        if slot != OWN:
            remote(mine, lt.at[slot], tsem.at[0, 0], tsem.at[1, slot], near).wait_recv()
    for p in QUERY_PIECES:
        from_rep(p)
    acc[...] = jnp.zeros_like(acc)
    backward_of(OWN)
    backward_of(z_slot)
    backward_of(z_slot + 1)
    backward_of(OWN + 1)
    for p in QUERY_PIECES:
        from_sibling(p)
    backward_of(6 - 4 * c)
    backward_of(7 - 4 * c)
    for p in QUERY_PIECES:
        from_far(p)
    backward_of(far_slot)
    backward_of(far_slot + 1)
    for p in QUERY_PIECES:
        band_from_sibling(p)
    backward_of(2 + 4 * c)
    backward_of(3 + 4 * c)
    outs += hand_out(1, (acc[...] * inv_root).astype(jnp.bfloat16))

    for p in range(len(PIECES)):
        for op in band_to_sibling(p):
            op.wait_send()
    for op in started + tops:
        op.wait_send()
    for op in outs:
        op.wait()


def layer(q_in, d_in, gain, tags, column_tag, w_in, w_out):
    rows, width = q_in.shape
    half = w_in.shape[1]
    bf, f32 = jnp.bfloat16, jnp.float32
    tile = 2 * WBLK
    vmem = pl.BlockSpec(memory_space=pltpu.VMEM)
    hbm = pl.BlockSpec(memory_space=pl.ANY)
    per_chunk = jax.ShapeDtypeStruct((CHUNKS, 2 * rows, 2 * half // CHUNKS), bf)
    return pl.pallas_call(
        layer_kernel,
        out_shape=(
            jax.ShapeDtypeStruct((2 * rows, width), bf),
            jax.ShapeDtypeStruct((2, NC, width // NC, rows), bf),
            jax.ShapeDtypeStruct((8, 128), f32),
            per_chunk,
            per_chunk,
            jax.ShapeDtypeStruct(w_in.shape, bf),
            jax.ShapeDtypeStruct(w_out.shape, bf),
        ),
        in_specs=[vmem] * 5 + [hbm] * 2,
        out_specs=[hbm, hbm, vmem] + [hbm] * 4,
        scratch_shapes=[
            pltpu.VMEM(w_in.shape, bf),
            pltpu.VMEM(w_out.shape, bf),
            pltpu.VMEM(w_in.shape, bf),
            pltpu.VMEM(w_out.shape, bf),
            pltpu.VMEM((2 * rows, width), bf),
            pltpu.VMEM((2 * half // tile, 2 * rows, tile), bf),
            pltpu.VMEM((2 * half // tile, 2 * rows, tile), bf),
            pltpu.VMEM((2 * rows, tile), f32),
            pltpu.VMEM((2 * rows, width), f32),
            pltpu.SemaphoreType.DMA((2,)),
            pltpu.SemaphoreType.DMA((2 * 2 * half // tile + 8,)),
            pltpu.SemaphoreType.DMA((8, W_CHUNKS)),
            pltpu.SemaphoreType.DMA((8, W_CHUNKS)),
            pltpu.VMEM((SLOTS, rows, width), bf),
            pltpu.VMEM((SLOTS,) + tags.shape, bf),
            pltpu.VMEM((SLOTS, rows, width), bf),
            pltpu.VMEM((2, DETOUR_ROWS, width), bf),
            pltpu.VMEM((SLOTS, rows, rows), f32),
            pltpu.VMEM((rows, SLOTS * rows), bf),
            pltpu.VMEM((SLOTS, 8, rows), f32),
            pltpu.VMEM((8, rows), f32),
            pltpu.VMEM((rows, width), f32),
            pltpu.VMEM((2, rows, width), bf),
            pltpu.VMEM((2, NC, width // NC, rows), bf),
            pltpu.SemaphoreType.DMA((4,)),
            pltpu.SemaphoreType.DMA((12, len(PIECES))),
            pltpu.SemaphoreType.DMA((12, len(PIECES))),
            pltpu.SemaphoreType.DMA((2, SLOTS)),
        ],
        compiler_params=pltpu.CompilerParams(
            collective_id=0, has_side_effects=True, vmem_limit_bytes=60 * MIB
        ),
        name="layer",
    )(q_in, d_in, gain.reshape(1, width), tags, column_tag, w_in, w_out)


PARTS = (
    (0, 0, 768, "x"),
    (0, 768, 768, "y"),
    (0, 1536, 512, "z"),
    (1, 0, 768, "x"),
    (1, 768, 768, "y"),
    (1, 1536, 512, "z"),
)
WIDE, NARROW = 768, 512
CHUNKS = 4


def backward_kernel(
    q_hbm,
    d_hbm,
    up_hbm,
    upt_hbm,
    gain_ref,
    loss_ref,
    hid_hbm,
    slope_hbm,
    win_hbm,
    oin_hbm,
    wout_hbm,
    oout_hbm,
    out,
    total,
    grads,
    in_v,
    up_ref,
    upt_ref,
    hid,
    slope,
    win,
    wout,
    s1,
    r1,
    a1,
    r2,
    a2,
    r3,
    a3,
    r4,
    r2z,
    a2z,
    r3z,
    a3z,
    r4z,
    acc,
    s_buf,
    local,
    sems,
):
    x, y, zl, c, r = coords()
    rows, width = q_hbm.shape
    half = win_hbm.shape[1]
    cols = 2 * half // CHUNKS
    per_half = CHUNKS // 2
    sibling = device(x, y, zl, 1 - c, r)
    xs = [device(wrap(x + k, NX), y, zl, c, r) for k in range(1, RING)]
    ys = [device(x, wrap(y + k, NY), zl, c, r) for k in range(1, RING)]
    zs = [device(x, y, 1 - zl, c, r), device(x, y, zl, c, 1 - r), device(x, y, 1 - zl, c, 1 - r)]

    loads = []
    n_loads = [0]

    def load(src, dst):
        nonlocal loads
        op = pltpu.make_async_copy(src, dst, local.at[n_loads[0]])
        op.start()
        n_loads[0] += 1
        loads.append(op)
        return op

    first_loads = [load(upt_hbm.at[k], upt_ref.at[k]) for k in range(2)]
    loads = []
    for j in range(CHUNKS):
        load(hid_hbm.at[j], hid.at[j // per_half, :, pl.ds(j % per_half * cols, cols)])
    for j in range(CHUNKS):
        load(slope_hbm.at[j], slope.at[j])
    for k, (inner, outer) in enumerate(((win_hbm, wout_hbm), (oin_hbm, oout_hbm))):
        load(inner, win.at[k])
        load(outer, wout.at[k])
    late_loads = [
        load(up_hbm, up_ref),
        load(q_hbm, in_v.at[pl.ds(0, rows)]),
        load(d_hbm, in_v.at[pl.ds(rows, rows)]),
    ]

    greet([sibling] + xs + ys + zs)
    state = {"n": 0}
    ops = []

    def send(src, dst, peer):
        n = state["n"]
        state["n"] = n + 1
        op = remote(src, dst, sems.at[0, n], sems.at[1, n], peer)
        op.start()
        ops.append(op)
        return op

    def down_part(core, k, at):
        return nn(upt_ref[0, core], hid[k, 0:rows, at]) + nn(upt_ref[1, core], hid[k, rows:, at])

    wait1 = []
    for op in first_loads:
        op.wait()
    n_loaded = 0
    for k, first, count, _ in PARTS:
        at = slice(first, first + count)
        while n_loaded * cols < k * half + first + count:
            loads[n_loaded].wait()
            n_loaded += 1
        s1[k, :, at] = down_part(1 - c, k, at).astype(jnp.bfloat16)
        view = (k, slice(None), pl.ds(first, count))
        wait1.append(send(s1.at[view], r1.at[view], sibling))

    wait2 = []
    waitz = []
    for p, (k, first, count, axis) in enumerate(PARTS):
        at = slice(first, first + count)
        mine = down_part(c, k, at)
        wait1[p].wait_recv()
        mine = mine + r1[k, :, at].astype(jnp.float32)
        a1[k, :, :, :, :, at] = mine.astype(jnp.bfloat16).reshape(NX, NY, NZ, GROUP, count)
        part = pl.ds(first, count)
        waits = []
        if axis == "z":
            if k == 0:
                waitz.append(send(a1.at[k, :, :, 1 - zl, :, part], r2z.at[0], zs[0]))
            else:
                waitz.append(send(a1.at[k, :, :, zl, :, part], r2z.at[1], zs[1]))
                waitz.append(send(a1.at[k, :, :, 1 - zl, :, part], r2z.at[2], zs[2]))
        for n in range(1, RING):
            slot = RING - 1 - n
            if axis == "x":
                src = a1.at[k, wrap(x + n, NX), :, :, :, part]
                waits.append(send(src, r2.at[k, 0, slot], xs[n - 1]))
            elif axis == "y":
                src = a1.at[k, :, wrap(y + n, NY), :, :, part]
                waits.append(send(src, r2.at[k, 1, slot], ys[n - 1]))
        wait2.append(waits)

    for j in range(CHUNKS):
        loads[CHUNKS + j].wait()
    for k in range(2):
        loads[2 * CHUNKS + 2 * k].wait()
        loads[2 * CHUNKS + 2 * k + 1].wait()
    for op in late_loads:
        op.wait()
    tile = 512
    for j in range(CHUNKS):
        k = j // per_half

        def tile_step(t, _, j=j, k=k):
            first = pl.multiple_of(t * tile, tile)
            there = pl.multiple_of((j % per_half) * cols + t * tile, tile)
            g_act = nt(up_ref[...], wout[k, pl.ds(there, tile), :])
            g_pre = (g_act * slope[j, :, pl.ds(first, tile)].astype(jnp.float32)).astype(
                jnp.bfloat16
            )
            step = nt(g_pre, win[k, :, pl.ds(there, tile)])
            if j == 0:
                before = jnp.where(t == 0, 0.0, acc[...])
            else:
                before = acc[...]
            acc[...] = before + step
            return 0

        if j == 0:
            acc[...] = jnp.zeros_like(acc)
        lax.fori_loop(0, cols // tile, tile_step, 0)

    values = in_v[...].astype(jnp.float32)
    inv_rms = lax.rsqrt(jnp.mean(values * values, axis=1, keepdims=True) + EPSILON)
    unit_rows = values * inv_rms
    g_norm = acc[...]
    weighted = g_norm * unit_rows
    gain_term = jnp.sum(weighted, axis=0, keepdims=True)
    gain = gain_ref[...]
    mean = jnp.mean(weighted * gain, axis=1, keepdims=True)
    d_values = inv_rms * (g_norm * gain - unit_rows * mean)
    grads[...] = (up_ref[...].astype(jnp.float32) + d_values).astype(jnp.bfloat16)

    row = lax.broadcasted_iota(jnp.int32, (8, width), 0)
    s_buf[12] = jnp.where(
        row == 0,
        jnp.broadcast_to(gain_term, (8, width)),
        jnp.broadcast_to(loss_ref[0:1, 0:1], (8, width)),
    )
    small = send(s_buf.at[12], s_buf.at[13], sibling)
    small.wait_recv()
    s_buf[x] = s_buf[12] + s_buf[13]
    small = [send(s_buf.at[x], s_buf.at[x], peer) for peer in xs]

    wait3 = {}

    def second(p):
        k, first, count, axis = PARTS[p]
        at = slice(first, first + count)
        i = 0 if axis == "x" else 1
        for op in wait2[p]:
            op.wait_recv()
        tot = (a1[k, x, :, :, :, at] if i == 0 else a1[k, :, y, :, :, at]).astype(jnp.float32)
        for n in range(RING - 1):
            tot = tot + r2[k, i, n].astype(jnp.float32)
        a2[k, i] = tot.astype(jnp.bfloat16)
        wait3[p] = []
        for n in range(1, RING):
            slot = RING - 1 - n
            if i == 0:
                op = send(a2.at[k, i, wrap(y + n, NY)], r3.at[k, i, slot], ys[n - 1])
            else:
                op = send(a2.at[k, i, wrap(x + n, NX)], r3.at[k, i, slot], xs[n - 1])
            wait3[p].append(op)

    def second_z():
        k, first, count, _ = PARTS[2]
        for op in waitz:
            op.wait_recv()
        tot = a1[k, :, :, zl, :, first : first + count].astype(jnp.float32)
        for n in range(RING - 1):
            tot = tot + r2z[n].astype(jnp.float32)
        a2z[...] = tot.astype(jnp.bfloat16)
        return [
            send(a2z.at[wrap(x + n, NX)], r3z.at[RING - 1 - n], xs[n - 1]) for n in range(1, RING)
        ]

    def third_z(waits):
        for op in waits:
            op.wait_recv()
        tot = a2z[x].astype(jnp.float32)
        for n in range(RING - 1):
            tot = tot + r3z[n].astype(jnp.float32)
        a3z[...] = tot.astype(jnp.bfloat16)
        return [
            send(a3z.at[wrap(y + n, NY)], r4z.at[RING - 1 - n], ys[n - 1]) for n in range(1, RING)
        ]

    second(0)
    second(1)
    for op in small:
        op.wait_recv()
    s_buf[4 + y] = ((s_buf[0] + s_buf[1]) + s_buf[2]) + s_buf[3]
    small = [send(s_buf.at[4 + y], s_buf.at[4 + y], peer) for peer in ys]
    waitz = second_z()
    second(3)
    second(4)
    waitz = third_z(waitz)

    for op in small:
        op.wait_recv()
    here = s_buf.at[8 + 2 * r + zl]
    here[...] = ((s_buf[4] + s_buf[5]) + s_buf[6]) + s_buf[7]
    small = [send(here, here, peer) for peer in zs]

    wait4 = [[], []]
    for p in (0, 1, 3, 4):
        k, first, count, axis = PARTS[p]
        i = 0 if axis == "x" else 1
        for op in wait3[p]:
            op.wait_recv()
        tot = (a2[k, i, y] if i == 0 else a2[k, i, x]).astype(jnp.float32)
        for n in range(RING - 1):
            tot = tot + r3[k, i, n].astype(jnp.float32)
        a3[k, i] = tot.astype(jnp.bfloat16)
        if k == 0:
            wait4[i].append(send(a3.at[k, i, 1 - zl], r4.at[i, 0], zs[0]))
        else:
            wait4[i].append(send(a3.at[k, i, zl], r4.at[i, 1], zs[1]))
            wait4[i].append(send(a3.at[k, i, 1 - zl], r4.at[i, 2], zs[2]))
    for op in waitz:
        op.wait_recv()
    first = PARTS[2][1]
    tot = a3z[y].astype(jnp.float32)
    for n in range(RING - 1):
        tot = tot + r4z[n].astype(jnp.float32)
    out[:, first : first + NARROW] = tot
    for i in range(2):
        for op in wait4[i]:
            op.wait_recv()
        out[:, i * WIDE : (i + 1) * WIDE] = (
            a3[0, i, zl].astype(jnp.float32) + r4[i, 0].astype(jnp.float32)
        ) + (r4[i, 1].astype(jnp.float32) + r4[i, 2].astype(jnp.float32))
    for op in small:
        op.wait_recv()
    total[...] = (s_buf[8] + s_buf[9]) + (s_buf[10] + s_buf[11])
    for op in ops:
        op.wait_send()


def backward(q_in, d_in, up, upt, gain, loss_part, hidden, slope, w_in, o_in, w_out, o_out):
    rows, width = 2 * q_in.shape[0], q_in.shape[1]
    half = w_in.shape[1]
    cols = 2 * half // CHUNKS
    groups = NX * NY * NZ
    bf, f32 = jnp.bfloat16, jnp.float32
    vmem = pl.BlockSpec(memory_space=pltpu.VMEM)
    hbm = pl.BlockSpec(memory_space=pl.ANY)
    return pl.pallas_call(
        backward_kernel,
        out_shape=(
            jax.ShapeDtypeStruct((GROUP, half), f32),
            jax.ShapeDtypeStruct((8, width), f32),
            jax.ShapeDtypeStruct((rows, width), bf),
        ),
        in_specs=[hbm] * 4 + [vmem] * 2 + [hbm] * 6,
        out_specs=[vmem] * 3,
        scratch_shapes=[
            pltpu.VMEM((rows, width), bf),
            pltpu.VMEM((rows, width), bf),
            pltpu.VMEM(upt.shape, bf),
            pltpu.VMEM((2, rows, half), bf),
            pltpu.VMEM((CHUNKS, rows, cols), bf),
            pltpu.VMEM((2,) + w_in.shape, bf),
            pltpu.VMEM((2,) + w_out.shape, bf),
            pltpu.VMEM((2, groups * GROUP, half), bf),
            pltpu.VMEM((2, groups * GROUP, half), bf),
            pltpu.VMEM((2, NX, NY, NZ, GROUP, half), bf),
            pltpu.VMEM((2, 2, RING - 1, RING, NZ, GROUP, WIDE), bf),
            pltpu.VMEM((2, 2, RING, NZ, GROUP, WIDE), bf),
            pltpu.VMEM((2, 2, RING - 1, NZ, GROUP, WIDE), bf),
            pltpu.VMEM((2, 2, NZ, GROUP, WIDE), bf),
            pltpu.VMEM((2, RING - 1, GROUP, WIDE), bf),
            pltpu.VMEM((RING - 1, NX, NY, GROUP, NARROW), bf),
            pltpu.VMEM((NX, NY, GROUP, NARROW), bf),
            pltpu.VMEM((RING - 1, NY, GROUP, NARROW), bf),
            pltpu.VMEM((NY, GROUP, NARROW), bf),
            pltpu.VMEM((RING - 1, GROUP, NARROW), bf),
            pltpu.VMEM((rows, width), f32),
            pltpu.VMEM((14, 8, width), f32),
            pltpu.SemaphoreType.DMA((2 * CHUNKS + 9,)),
            pltpu.SemaphoreType.DMA((2, 64)),
        ],
        compiler_params=pltpu.CompilerParams(
            collective_id=3, has_side_effects=True, vmem_limit_bytes=60 * MIB
        ),
        name="backward",
    )(
        q_in,
        d_in,
        up,
        upt,
        gain.reshape(1, width),
        loss_part,
        hidden,
        slope,
        w_in,
        o_in,
        w_out,
        o_out,
    )


def finish_kernel(down, total, grads, down_out, gain_out, loss_out, q_out, d_out):
    rows = q_out.shape[0]
    down_out[...] = down[...]
    gain_out[...] = total[0:1, :]
    loss_out[...] = total[1:2, 0:1] * (1.0 / (rows * 2 * NBLK))
    q_out[...] = grads[0:rows, :]
    d_out[...] = grads[rows : 2 * rows, :]


def finish(down, total, grads):
    rows, width = grads.shape[0] // 2, grads.shape[1]
    f32 = jnp.float32
    row_grads = jax.ShapeDtypeStruct((rows, width), grads.dtype)
    return pl.pallas_call(
        finish_kernel,
        out_shape=(
            jax.ShapeDtypeStruct(down.shape, f32),
            jax.ShapeDtypeStruct((1, width), f32),
            jax.ShapeDtypeStruct((1, 1), f32),
            row_grads,
            row_grads,
        ),
        name="finish",
    )(down, total, grads)


def on_device(query_in, doc_in, cluster, gain, w_in, w_out):
    rows, width = query_in.shape
    tags = jnp.broadcast_to(cluster.astype(jnp.bfloat16)[None, :], (16, rows))
    column_tag = cluster.astype(jnp.float32)[:, None]
    up, upt, loss_part, hidden, slope, o_in, o_out = layer(
        query_in, doc_in, gain, tags, column_tag, w_in, w_out
    )
    sums = backward(
        query_in, doc_in, up, upt, gain, loss_part, hidden, slope, w_in, o_in, w_out, o_out
    )
    down_t, gain_total, loss, q_grads, d_grads = finish(*sums)
    return (loss.reshape(()), down_t.T, gain_total.reshape(width), q_grads, d_grads)


def solution(mesh):
    in_specs = (
        P(("blk", "rep"), None),
        P(("blk", "rep"), None),
        P(("blk", "rep")),
        P(),
        P(None, "rep"),
        P("rep", None),
    )
    out_specs = (P(), P("rep", "blk"), P(), P(("blk", "rep"), None), P(("blk", "rep"), None))
    return jax.shard_map(
        on_device, mesh=mesh, in_specs=in_specs, out_specs=out_specs, check_vma=False
    )
```

```python
import math

import jax
import jax.numpy as jnp
from jax import lax
from jax.experimental import pallas as pl
from jax.experimental.pallas import tpu as pltpu
from jax.sharding import PartitionSpec as P

MESH = pl.DeviceIdType.MESH
MIB = 2**20
NX, NY, NZ, NC = 4, 4, 2, 2
NBLK = NX * NY * NZ * NC
RING = NX
EPSILON = 1e-06
SLOTS = 10
OWN = 4
GROUP = 16


def coords():
    b = lax.axis_index("blk")
    r = lax.axis_index("rep")
    return b // (NY * NZ * NC), (b // (NZ * NC)) % NY, (b // NC) % NZ, b % NC, r


def device(x, y, zl, c, r):
    return {"blk": ((x * NY + y) * NZ + zl) * NC + c, "rep": r}


def wrap(v, n):
    return lax.rem(v + n, n)


def greet(peers):
    barrier = pltpu.get_barrier_semaphore()
    for peer in peers:
        pl.semaphore_signal(barrier, inc=1, device_id=peer, device_id_type=MESH)
    pl.semaphore_wait(barrier, len(peers))


def remote(src, dst, send, recv, peer):
    return pltpu.make_async_remote_copy(
        src_ref=src,
        dst_ref=dst,
        send_sem=send,
        recv_sem=recv,
        device_id=peer,
        device_id_type=MESH,
    )


WBLK = 256
W_CHUNKS = 8
STRIP = 64


def nt(a, b):
    return lax.dot_general(a, b, (((1,), (1,)), ((), ())), preferred_element_type=jnp.float32)


def nn(a, b):
    return lax.dot_general(a, b, (((1,), (0,)), ((), ())), preferred_element_type=jnp.float32)


def gelu_both(p):
    k = math.sqrt(2.0 / math.pi)
    square = p * p
    t = jnp.tanh(p * (k + (k * 0.044715) * square))
    up = 0.5 + 0.5 * t
    slope = up + (0.5 * p) * ((1.0 - t * t) * (k + (3 * k * 0.044715) * square))
    return p * up, slope


def weight_view(in_ref, out_ref, block, chunk):
    if chunk < W_CHUNKS // 2:
        rows = in_ref.shape[0] // (W_CHUNKS // 2)
        return in_ref.at[
            pl.ds(chunk * rows, rows), pl.ds(pl.multiple_of(block * WBLK, WBLK), WBLK)
        ]
    rows = WBLK // (W_CHUNKS // 2)
    first = block * WBLK + (chunk - W_CHUNKS // 2) * rows
    return out_ref.at[pl.ds(pl.multiple_of(first, rows), rows)]


def forward_part(
    q_in,
    d_in,
    gain_ref,
    win_hbm,
    wout_hbm,
    hid_hbm,
    slope_hbm,
    oin_hbm,
    oout_hbm,
    win,
    wout,
    oin,
    oout,
    normed,
    hid,
    slope,
    pre,
    acc,
    local,
    stores,
    send,
    recv,
    meet,
):
    x, y, zl, c, r = coords()
    cross = device(x, y, 1 - zl, c, 1 - r)
    near = device(x, y, 1 - zl, c, r)
    ahead = device(wrap(x + 1, NX), y, zl, c, r)
    behind = device(wrap(x - 1, NX), y, zl, c, r)
    sibling = device(x, y, zl, 1 - c, r)
    half = win_hbm.shape[1]
    rows = q_in.shape[0]
    load_in = pltpu.make_async_copy(win_hbm, win, local.at[0])
    load_out = pltpu.make_async_copy(wout_hbm, wout, local.at[1])
    load_in.start()
    load_out.start()
    meet([ahead, behind])
    color = lax.rem(x + 2 * zl, 4)
    started = []

    def color_at(shift):
        return lax.rem(color + shift, 4)

    def block_of(shift):
        return 2 * color_at(shift) + c

    def copy(flow, block, chunk, peer, source=None):
        src = weight_view(*(source or (oin, oout)), block, chunk)
        dst = weight_view(oin, oout, block, chunk)
        return remote(src, dst, send.at[flow, chunk], recv.at[flow, chunk], peer)

    def start(*args):
        op = copy(*args)
        op.start()
        started.append(op)

    def first_hop(chunk):
        mine = block_of(0)
        copy(0, mine, chunk, cross).wait_recv()
        start(1, mine, chunk, ahead)
        start(2, mine, chunk, behind)
        start(3, mine, chunk, near)
        start(4, mine, chunk, sibling)

    def second_hop(chunk):
        for flow, shift in ((1, 3), (2, 1), (3, 2)):
            block = block_of(shift)
            copy(flow, block, chunk, near).wait_recv()
            start(4 + shift, block, chunk, sibling)

    def from_sibling(shift, chunks):
        block = 2 * color_at(shift) + (1 - c)
        for chunk in chunks:
            copy(4 + shift, block, chunk, sibling).wait_recv()

    stored = []

    def store(src, dst):
        op = pltpu.make_async_copy(src, dst, stores.at[len(stored)])
        op.start()
        stored.append(op)

    tile = 2 * WBLK

    def activate(block):
        def strip(i, _):
            at = pl.ds(pl.multiple_of(i * STRIP, STRIP), STRIP)
            h, s = gelu_both(pre[at, :])
            hid[block, at, :] = h.astype(jnp.bfloat16)
            slope[block, at, :] = s.astype(jnp.bfloat16)
            return 0

        lax.fori_loop(0, 2 * rows // STRIP, strip, 0)
        there = (block // 2, slice(None), pl.ds(pl.multiple_of((block % 2) * tile, tile), tile))
        store(hid.at[block], hid_hbm.at[there])
        store(slope.at[block], slope_hbm.at[there])

    def up_own(t):
        pre[...] = nn(normed[...], win[:, t * tile : (t + 1) * tile])
        activate(t)

    def down_own(t):
        step = nn(hid[t], wout[t * tile : (t + 1) * tile, :])
        acc[...] = step if t == 0 else acc[...] + step

    def up_other(shift):
        from_sibling(shift, range(W_CHUNKS // 2))
        at = pl.ds(pl.multiple_of(color_at(shift) * tile, tile), tile)
        pre[...] = nn(normed[...], oin[:, at])
        activate(half // tile + color_at(shift))
        store(oin.at[:, at], oin_hbm.at[:, at])

    def down_other(shift):
        from_sibling(shift, range(W_CHUNKS // 2, W_CHUNKS))
        at = pl.ds(pl.multiple_of(color_at(shift) * tile, tile), tile)
        acc[...] += nn(hid[half // tile + color_at(shift)], oout[at, :])
        store(oout.at[at, :], oout_hbm.at[at, :])

    for chunk in range(W_CHUNKS):
        start(0, block_of(2), chunk, cross, (win_hbm, wout_hbm))
    for k, ref in enumerate((q_in, d_in)):
        values = ref[...].astype(jnp.float32)
        inv_rms = lax.rsqrt(jnp.mean(values * values, axis=1, keepdims=True) + EPSILON)
        normed[k * rows : (k + 1) * rows, :] = ((values * inv_rms) * gain_ref[...]).astype(
            jnp.bfloat16
        )
    load_in.wait()
    up_own(0)
    first_hop(0)
    up_own(1)
    first_hop(1)
    second_hop(0)
    up_own(2)
    first_hop(2)
    second_hop(1)
    up_own(3)
    first_hop(3)
    second_hop(2)
    load_out.wait()
    down_own(0)
    down_own(1)
    first_hop(4)
    second_hop(3)
    up_other(0)
    first_hop(5)
    second_hop(4)
    up_other(1)
    first_hop(6)
    second_hop(5)
    up_other(2)
    first_hop(7)
    second_hop(6)
    up_other(3)
    second_hop(7)
    down_own(2)
    down_own(3)
    for shift in (0, 3, 1):
        down_other(shift)
    from_sibling(2, range(W_CHUNKS // 2, W_CHUNKS))
    last = pl.ds(pl.multiple_of(color_at(2) * tile, tile), tile)
    store(oout.at[last, :], oout_hbm.at[last, :])

    def embed(k):
        at = slice(k * rows, (k + 1) * rows)
        mixed = acc[at, :] + nn(hid[half // tile + color_at(2), at, :], oout[last, :])
        return ((q_in, d_in)[k][...].astype(jnp.float32) + mixed).astype(jnp.bfloat16)

    return embed, started, stored


PIECES = (
    (0, 0, 64, 0, 0),
    (1, 0, 16, 0, 0),
    (0, 64, 64, 1, 0),
    (0, 128, 80, 0, 0),
    (0, 208, 48, 1, 1),
    (2, 0, 64, 0, 0),
    (2, 64, 64, 1, 0),
    (2, 128, 80, 0, 0),
    (2, 208, 48, 1, 1),
)
DOC_PIECES = (0, 1, 2, 3, 4)
QUERY_PIECES = (5, 6, 7, 8)
DETOUR_ROWS = 48


def layer_kernel(*refs):
    ins, outs, scratch = refs[:6], refs[6:13], refs[13:]
    q_in, d_in, gain_ref, cluster, win_hbm, wout_hbm = ins
    up, upt, loss, hid_hbm, slope_hbm, oin_hbm, oout_hbm = outs
    forward_scratch, band_scratch = scratch[:13], scratch[13:]
    b = lax.axis_index("blk")
    zl = coords()[2]
    r = lax.axis_index("rep")
    step = NZ * NC * (1 - 2 * zl)
    onward = {"blk": wrap(b + step, NBLK), "rep": r}
    source = {"blk": wrap(b - step, NBLK), "rep": r}
    peers = []
    for offset in range(-2, 3):
        for other in range(2):
            if offset or other:
                rep = 1 - r if other else r
                peers.append((offset, other, {"blk": wrap(b + offset, NBLK), "rep": rep}))

    def meet(more):
        greet([peer for _, _, peer in peers] + [onward, source] + more)

    embed, started, stored = forward_part(
        q_in,
        d_in,
        gain_ref,
        win_hbm,
        wout_hbm,
        hid_hbm,
        slope_hbm,
        oin_hbm,
        oout_hbm,
        *forward_scratch,
        meet,
    )
    band_part(cluster, up, upt, loss, *band_scratch, embed, peers, onward, source)
    for op in started:
        op.wait_send()
    for op in stored:
        op.wait()


def band_part(
    cluster,
    up,
    upt,
    loss,
    gd,
    gx,
    gq,
    transit,
    s,
    w,
    lt,
    mine,
    acc,
    column_tag,
    up_v,
    upt_v,
    local,
    send,
    recv,
    tsem,
    embed,
    peers,
    onward,
    source,
):
    x, y, zl, c, r = coords()
    rows, width = gd.shape[1:]
    tag = cluster[...].astype(jnp.float32)
    column_tag[...] = jnp.transpose(jnp.broadcast_to(tag, (128, rows)))
    inv_root = 1.0 / math.sqrt(width)
    cross = device(x, y, 1 - zl, c, 1 - r)
    near = device(x, y, 1 - zl, c, r)
    sibling = device(x, y, zl, 1 - c, r)

    def view(slot, p):
        kind, first, count = PIECES[p][:3]
        return (gd, gx, gq)[kind].at[slot, pl.ds(first, count)]

    def own(p):
        return view(OWN, p)

    z_slot = 8 - 8 * zl
    far_slot = 8 * zl
    theirs = 8 * zl
    started = []

    def make(flow, p, src, dst, peer):
        return remote(src, dst, send.at[flow, p], recv.at[flow, p], peer)

    def start(*args):
        op = make(*args)
        op.start()
        started.append(op)

    def arrived(flow, p, slot):
        make(flow, p, view(slot, p), view(slot, p), near).wait_recv()

    def band_to_sibling(p):
        return [
            make(7 + k, p, view(8 - 8 * c + k, p), view(6 - 4 * c + k, p), sibling)
            for k in range(2)
        ]

    def through(p):
        return transit.at[p // 5]

    def send_own(p):
        start(0, p, own(p), view(theirs, p), near)
        start(1, p, own(p), view(theirs + 1, p), cross)
        if PIECES[p][4]:
            start(9, p, own(p), through(p), source)
        start(5, p, own(p), view(2 + 4 * c, p), sibling)

    def from_z(p):
        by_near, detour = PIECES[p][3:]
        arrived(0, p, z_slot)
        if not detour:
            start(3, p, view(z_slot, p), view(far_slot, p), onward)
        if not by_near:
            start(2, p, view(z_slot, p), view(OWN + 1, p), cross)
        arrived(1, p, z_slot + 1)
        if not detour:
            start(4, p, view(z_slot + 1, p), view(far_slot + 1, p), onward)
        if by_near:
            start(2, p, view(z_slot + 1, p), view(OWN + 1, p), near)

        @pl.when(c == zl)
        def _():
            for op in band_to_sibling(p):
                op.start()

    def from_transit(p):
        if PIECES[p][4]:
            make(9, p, own(p), through(p), source).wait_recv()
            start(10, p, through(p), view(8 - 8 * zl, p), near)
            start(11, p, through(p), view(8 - 8 * zl + 1, p), cross)

    def from_rep(p):
        arrived(2, p, OWN + 1)
        start(6, p, view(OWN + 1, p), view(3 + 4 * c, p), sibling)

    def from_far(p):
        detour = PIECES[p][4]
        arrived(10 if detour else 3, p, far_slot)
        arrived(11 if detour else 4, p, far_slot + 1)

        @pl.when(c != zl)
        def _():
            for op in band_to_sibling(p):
                op.start()

    def from_sibling(p):
        arrived(5, p, 6 - 4 * c)
        arrived(6, p, 7 - 4 * c)

    def band_from_sibling(p):
        arrived(7, p, 2 + 4 * c)
        arrived(8, p, 3 + 4 * c)

    def hand_out(k, value):
        up_v[k] = value
        turned = jnp.transpose(value).reshape(width // (NC * GROUP), NC, GROUP, rows)
        for core in range(NC):
            upt_v[k, core] = turned[:, core].reshape(width // NC, rows)
        ops = [
            pltpu.make_async_copy(up_v.at[k], up.at[pl.ds(k * rows, rows)], local.at[2 * k]),
            pltpu.make_async_copy(upt_v.at[k], upt.at[k], local.at[1 + 2 * k]),
        ]
        for op in ops:
            op.start()
        return ops

    row = lax.broadcasted_iota(jnp.int32, (rows, rows), 0)
    col = lax.broadcasted_iota(jnp.int32, (rows, rows), 1)
    diagonal = row == col

    def masked(a, g, slot):
        scores = nt(a[OWN], g[slot]) * inv_root
        tag_row = gx[slot].astype(jnp.float32)[0:1, :]
        allowed = tag_row != column_tag[:, 0:1]
        if isinstance(slot, int) and slot == OWN:
            allowed = allowed | diagonal
        return scores, jnp.where(allowed, scores, -jnp.inf)

    def score(slot):
        s[slot] = masked(gq, gd, slot)[1]

    def backward_of(slot):
        m = masked(gd, gq, slot)[1]
        wt = jnp.exp(m - lt[slot, 0:1, :])
        if isinstance(slot, int) and slot == OWN:
            wt = wt - diagonal.astype(jnp.float32)
        acc[...] += nn(wt.astype(jnp.bfloat16), gq[slot])

    gx[OWN] = jnp.broadcast_to(tag, gx.shape[1:]).astype(jnp.bfloat16)
    gd[OWN] = embed(1)
    for p in DOC_PIECES:
        send_own(p)
    gq[OWN] = embed(0)
    for p in DOC_PIECES:
        from_z(p)
    for p in QUERY_PIECES:
        send_own(p)
    for p in DOC_PIECES:
        from_transit(p)
    score(OWN)
    positive = jnp.sum(jnp.where(diagonal, s[OWN], 0.0), axis=1, keepdims=True)
    score(z_slot)
    score(z_slot + 1)
    for p in DOC_PIECES:
        from_rep(p)
    for p in DOC_PIECES[:3]:
        from_far(p)
    from_z(QUERY_PIECES[0])
    for p in DOC_PIECES[3:]:
        from_far(p)
    for p in DOC_PIECES:
        from_sibling(p)
    from_z(QUERY_PIECES[1])
    score(OWN + 1)
    score(6 - 4 * c)
    score(7 - 4 * c)
    score(far_slot)
    score(far_slot + 1)
    from_z(QUERY_PIECES[2])
    for p in DOC_PIECES:
        band_from_sibling(p)
    score(2 + 4 * c)
    score(3 + 4 * c)
    top = s[0]
    for slot in range(1, SLOTS):
        top = jnp.maximum(top, s[slot])
    row_max = jnp.max(top, axis=1, keepdims=True)
    total = jnp.exp(s[0] - row_max)
    for slot in range(1, SLOTS):
        total = total + jnp.exp(s[slot] - row_max)
    log_total = row_max + jnp.log(jnp.sum(total, axis=1, keepdims=True))
    loss[...] = jnp.broadcast_to(
        jnp.sum(log_total - positive, axis=0, keepdims=True), loss.shape
    )
    mine[...] = jnp.transpose(jnp.broadcast_to(log_total, (rows, 128)))[0:8, :]
    lt[OWN] = mine[...]
    tops = []
    for i, (offset, other, peer) in enumerate(peers):
        slot = (2 - offset) * 2 + other
        op = remote(mine, lt.at[slot], tsem.at[0, i], tsem.at[1, slot], peer)
        op.start()
        tops.append(op)
    from_z(QUERY_PIECES[3])
    for p in QUERY_PIECES:
        from_transit(p)
    for slot in range(SLOTS):
        wt = jnp.exp(s[slot] - log_total)
        if slot == OWN:
            wt = wt - diagonal.astype(jnp.float32)
        w[:, slot * rows : (slot + 1) * rows] = wt.astype(jnp.bfloat16)
    query_grad = nn(w[...], gd[...].reshape(SLOTS * rows, width))
    outs = hand_out(0, (query_grad * inv_root).astype(jnp.bfloat16))

    for slot in range(SLOTS):
        if slot != OWN:
            remote(mine, lt.at[slot], tsem.at[0, 0], tsem.at[1, slot], near).wait_recv()
    for p in QUERY_PIECES:
        from_rep(p)
    acc[...] = jnp.zeros_like(acc)
    backward_of(OWN)
    backward_of(z_slot)
    backward_of(z_slot + 1)
    backward_of(OWN + 1)
    for p in QUERY_PIECES:
        from_sibling(p)
    backward_of(6 - 4 * c)
    backward_of(7 - 4 * c)
    for p in QUERY_PIECES:
        from_far(p)
    backward_of(far_slot)
    backward_of(far_slot + 1)
    for p in QUERY_PIECES:
        band_from_sibling(p)
    backward_of(2 + 4 * c)
    backward_of(3 + 4 * c)
    outs += hand_out(1, (acc[...] * inv_root).astype(jnp.bfloat16))

    for p in range(len(PIECES)):
        for op in band_to_sibling(p):
            op.wait_send()
    for op in started + tops:
        op.wait_send()
    for op in outs:
        op.wait()


def layer(q_in, d_in, gain, cluster, w_in, w_out):
    rows, width = q_in.shape
    half = w_in.shape[1]
    bf, f32 = jnp.bfloat16, jnp.float32
    tile = 2 * WBLK
    vmem = pl.BlockSpec(memory_space=pltpu.VMEM)
    hbm = pl.BlockSpec(memory_space=pl.ANY)
    per_chunk = jax.ShapeDtypeStruct((CHUNKS, 2 * rows, 2 * half // CHUNKS), bf)
    return pl.pallas_call(
        layer_kernel,
        out_shape=(
            jax.ShapeDtypeStruct((2 * rows, width), bf),
            jax.ShapeDtypeStruct((2, NC, width // NC, rows), bf),
            jax.ShapeDtypeStruct((8, 128), f32),
            per_chunk,
            per_chunk,
            jax.ShapeDtypeStruct(w_in.shape, bf),
            jax.ShapeDtypeStruct(w_out.shape, bf),
        ),
        in_specs=[vmem] * 4 + [hbm] * 2,
        out_specs=[hbm, hbm, vmem] + [hbm] * 4,
        scratch_shapes=[
            pltpu.VMEM(w_in.shape, bf),
            pltpu.VMEM(w_out.shape, bf),
            pltpu.VMEM(w_in.shape, bf),
            pltpu.VMEM(w_out.shape, bf),
            pltpu.VMEM((2 * rows, width), bf),
            pltpu.VMEM((2 * half // tile, 2 * rows, tile), bf),
            pltpu.VMEM((2 * half // tile, 2 * rows, tile), bf),
            pltpu.VMEM((2 * rows, tile), f32),
            pltpu.VMEM((2 * rows, width), f32),
            pltpu.SemaphoreType.DMA((2,)),
            pltpu.SemaphoreType.DMA((2 * 2 * half // tile + 8,)),
            pltpu.SemaphoreType.DMA((8, W_CHUNKS)),
            pltpu.SemaphoreType.DMA((8, W_CHUNKS)),
            pltpu.VMEM((SLOTS, rows, width), bf),
            pltpu.VMEM((SLOTS, 16, rows), bf),
            pltpu.VMEM((SLOTS, rows, width), bf),
            pltpu.VMEM((2, DETOUR_ROWS, width), bf),
            pltpu.VMEM((SLOTS, rows, rows), f32),
            pltpu.VMEM((rows, SLOTS * rows), bf),
            pltpu.VMEM((SLOTS, 8, rows), f32),
            pltpu.VMEM((8, rows), f32),
            pltpu.VMEM((rows, width), f32),
            pltpu.VMEM((rows, 128), f32),
            pltpu.VMEM((2, rows, width), bf),
            pltpu.VMEM((2, NC, width // NC, rows), bf),
            pltpu.SemaphoreType.DMA((4,)),
            pltpu.SemaphoreType.DMA((12, len(PIECES))),
            pltpu.SemaphoreType.DMA((12, len(PIECES))),
            pltpu.SemaphoreType.DMA((2, SLOTS)),
        ],
        compiler_params=pltpu.CompilerParams(
            collective_id=0, has_side_effects=True, vmem_limit_bytes=60 * MIB
        ),
        name="layer",
    )(q_in, d_in, gain.reshape(1, width), cluster.reshape(1, rows), w_in, w_out)


PARTS = (
    (0, 0, 768, "x"),
    (0, 768, 768, "y"),
    (0, 1536, 512, "z"),
    (1, 0, 768, "x"),
    (1, 768, 768, "y"),
    (1, 1536, 512, "z"),
)
WIDE, NARROW = 768, 512
CHUNKS = 4


def backward_kernel(
    q_hbm,
    d_hbm,
    up_hbm,
    upt_hbm,
    gain_ref,
    loss_ref,
    hid_hbm,
    slope_hbm,
    win_hbm,
    oin_hbm,
    wout_hbm,
    oout_hbm,
    out,
    total,
    grads,
    in_v,
    up_ref,
    upt_ref,
    hid,
    slope,
    win,
    wout,
    s1,
    r1,
    a1,
    r2,
    a2,
    r3,
    a3,
    r4,
    r2z,
    a2z,
    r3z,
    a3z,
    r4z,
    acc,
    s_buf,
    local,
    sems,
):
    x, y, zl, c, r = coords()
    rows, width = q_hbm.shape
    half = win_hbm.shape[1]
    cols = 2 * half // CHUNKS
    per_half = CHUNKS // 2
    sibling = device(x, y, zl, 1 - c, r)
    xs = [device(wrap(x + k, NX), y, zl, c, r) for k in range(1, RING)]
    ys = [device(x, wrap(y + k, NY), zl, c, r) for k in range(1, RING)]
    zs = [device(x, y, 1 - zl, c, r), device(x, y, zl, c, 1 - r), device(x, y, 1 - zl, c, 1 - r)]

    loads = []
    n_loads = [0]

    def load(src, dst):
        nonlocal loads
        op = pltpu.make_async_copy(src, dst, local.at[n_loads[0]])
        op.start()
        n_loads[0] += 1
        loads.append(op)
        return op

    first_loads = [load(upt_hbm.at[k], upt_ref.at[k]) for k in range(2)]
    loads = []
    for j in range(CHUNKS):
        load(hid_hbm.at[j], hid.at[j // per_half, :, pl.ds(j % per_half * cols, cols)])
    for j in range(CHUNKS):
        load(slope_hbm.at[j], slope.at[j])
    for k, (inner, outer) in enumerate(((win_hbm, wout_hbm), (oin_hbm, oout_hbm))):
        load(inner, win.at[k])
        load(outer, wout.at[k])
    late_loads = [
        load(up_hbm, up_ref),
        load(q_hbm, in_v.at[pl.ds(0, rows)]),
        load(d_hbm, in_v.at[pl.ds(rows, rows)]),
    ]

    greet([sibling] + xs + ys + zs)
    state = {"n": 0}
    ops = []

    def send(src, dst, peer):
        n = state["n"]
        state["n"] = n + 1
        op = remote(src, dst, sems.at[0, n], sems.at[1, n], peer)
        op.start()
        ops.append(op)
        return op

    def down_part(core, k, at):
        return nn(upt_ref[0, core], hid[k, 0:rows, at]) + nn(upt_ref[1, core], hid[k, rows:, at])

    wait1 = []
    for op in first_loads:
        op.wait()
    n_loaded = 0
    for k, first, count, _ in PARTS:
        at = slice(first, first + count)
        while n_loaded * cols < k * half + first + count:
            loads[n_loaded].wait()
            n_loaded += 1
        s1[k, :, at] = down_part(1 - c, k, at).astype(jnp.bfloat16)
        view = (k, slice(None), pl.ds(first, count))
        wait1.append(send(s1.at[view], r1.at[view], sibling))

    wait2 = []
    waitz = []
    for p, (k, first, count, axis) in enumerate(PARTS):
        at = slice(first, first + count)
        mine = down_part(c, k, at)
        wait1[p].wait_recv()
        mine = mine + r1[k, :, at].astype(jnp.float32)
        a1[k, :, :, :, :, at] = mine.astype(jnp.bfloat16).reshape(NX, NY, NZ, GROUP, count)
        part = pl.ds(first, count)
        waits = []
        if axis == "z":
            if k == 0:
                waitz.append(send(a1.at[k, :, :, 1 - zl, :, part], r2z.at[0], zs[0]))
            else:
                waitz.append(send(a1.at[k, :, :, zl, :, part], r2z.at[1], zs[1]))
                waitz.append(send(a1.at[k, :, :, 1 - zl, :, part], r2z.at[2], zs[2]))
        for n in range(1, RING):
            slot = RING - 1 - n
            if axis == "x":
                src = a1.at[k, wrap(x + n, NX), :, :, :, part]
                waits.append(send(src, r2.at[k, 0, slot], xs[n - 1]))
            elif axis == "y":
                src = a1.at[k, :, wrap(y + n, NY), :, :, part]
                waits.append(send(src, r2.at[k, 1, slot], ys[n - 1]))
        wait2.append(waits)

    for j in range(CHUNKS):
        loads[CHUNKS + j].wait()
    for k in range(2):
        loads[2 * CHUNKS + 2 * k].wait()
        loads[2 * CHUNKS + 2 * k + 1].wait()
    for op in late_loads:
        op.wait()
    tile = 512
    for j in range(CHUNKS):
        k = j // per_half

        def tile_step(t, _, j=j, k=k):
            first = pl.multiple_of(t * tile, tile)
            there = pl.multiple_of((j % per_half) * cols + t * tile, tile)
            g_act = nt(up_ref[...], wout[k, pl.ds(there, tile), :])
            g_pre = (g_act * slope[j, :, pl.ds(first, tile)].astype(jnp.float32)).astype(
                jnp.bfloat16
            )
            step = nt(g_pre, win[k, :, pl.ds(there, tile)])
            if j == 0:
                before = jnp.where(t == 0, 0.0, acc[...])
            else:
                before = acc[...]
            acc[...] = before + step
            return 0

        if j == 0:
            acc[...] = jnp.zeros_like(acc)
        lax.fori_loop(0, cols // tile, tile_step, 0)

    values = in_v[...].astype(jnp.float32)
    inv_rms = lax.rsqrt(jnp.mean(values * values, axis=1, keepdims=True) + EPSILON)
    unit_rows = values * inv_rms
    g_norm = acc[...]
    weighted = g_norm * unit_rows
    gain_term = jnp.sum(weighted, axis=0, keepdims=True)
    gain = gain_ref[...]
    mean = jnp.mean(weighted * gain, axis=1, keepdims=True)
    d_values = inv_rms * (g_norm * gain - unit_rows * mean)
    grads[...] = (up_ref[...].astype(jnp.float32) + d_values).astype(jnp.bfloat16)

    row = lax.broadcasted_iota(jnp.int32, (8, width), 0)
    s_buf[12] = jnp.where(
        row == 0,
        jnp.broadcast_to(gain_term, (8, width)),
        jnp.broadcast_to(loss_ref[0:1, 0:1], (8, width)),
    )
    small = send(s_buf.at[12], s_buf.at[13], sibling)
    small.wait_recv()
    s_buf[x] = s_buf[12] + s_buf[13]
    small = [send(s_buf.at[x], s_buf.at[x], peer) for peer in xs]

    wait3 = {}

    def second(p):
        k, first, count, axis = PARTS[p]
        at = slice(first, first + count)
        i = 0 if axis == "x" else 1
        for op in wait2[p]:
            op.wait_recv()
        tot = (a1[k, x, :, :, :, at] if i == 0 else a1[k, :, y, :, :, at]).astype(jnp.float32)
        for n in range(RING - 1):
            tot = tot + r2[k, i, n].astype(jnp.float32)
        a2[k, i] = tot.astype(jnp.bfloat16)
        wait3[p] = []
        for n in range(1, RING):
            slot = RING - 1 - n
            if i == 0:
                op = send(a2.at[k, i, wrap(y + n, NY)], r3.at[k, i, slot], ys[n - 1])
            else:
                op = send(a2.at[k, i, wrap(x + n, NX)], r3.at[k, i, slot], xs[n - 1])
            wait3[p].append(op)

    def second_z():
        k, first, count, _ = PARTS[2]
        for op in waitz:
            op.wait_recv()
        tot = a1[k, :, :, zl, :, first : first + count].astype(jnp.float32)
        for n in range(RING - 1):
            tot = tot + r2z[n].astype(jnp.float32)
        a2z[...] = tot.astype(jnp.bfloat16)
        return [
            send(a2z.at[wrap(x + n, NX)], r3z.at[RING - 1 - n], xs[n - 1]) for n in range(1, RING)
        ]

    def third_z(waits):
        for op in waits:
            op.wait_recv()
        tot = a2z[x].astype(jnp.float32)
        for n in range(RING - 1):
            tot = tot + r3z[n].astype(jnp.float32)
        a3z[...] = tot.astype(jnp.bfloat16)
        return [
            send(a3z.at[wrap(y + n, NY)], r4z.at[RING - 1 - n], ys[n - 1]) for n in range(1, RING)
        ]

    second(0)
    second(1)
    for op in small:
        op.wait_recv()
    s_buf[4 + y] = ((s_buf[0] + s_buf[1]) + s_buf[2]) + s_buf[3]
    small = [send(s_buf.at[4 + y], s_buf.at[4 + y], peer) for peer in ys]
    waitz = second_z()
    second(3)
    second(4)
    waitz = third_z(waitz)

    for op in small:
        op.wait_recv()
    here = s_buf.at[8 + 2 * r + zl]
    here[...] = ((s_buf[4] + s_buf[5]) + s_buf[6]) + s_buf[7]
    small = [send(here, here, peer) for peer in zs]

    wait4 = [[], []]
    for p in (0, 1, 3, 4):
        k, first, count, axis = PARTS[p]
        i = 0 if axis == "x" else 1
        for op in wait3[p]:
            op.wait_recv()
        tot = (a2[k, i, y] if i == 0 else a2[k, i, x]).astype(jnp.float32)
        for n in range(RING - 1):
            tot = tot + r3[k, i, n].astype(jnp.float32)
        a3[k, i] = tot.astype(jnp.bfloat16)
        if k == 0:
            wait4[i].append(send(a3.at[k, i, 1 - zl], r4.at[i, 0], zs[0]))
        else:
            wait4[i].append(send(a3.at[k, i, zl], r4.at[i, 1], zs[1]))
            wait4[i].append(send(a3.at[k, i, 1 - zl], r4.at[i, 2], zs[2]))
    for op in waitz:
        op.wait_recv()
    first = PARTS[2][1]
    tot = a3z[y].astype(jnp.float32)
    for n in range(RING - 1):
        tot = tot + r4z[n].astype(jnp.float32)
    out[:, first : first + NARROW] = tot
    for i in range(2):
        for op in wait4[i]:
            op.wait_recv()
        out[:, i * WIDE : (i + 1) * WIDE] = (
            a3[0, i, zl].astype(jnp.float32) + r4[i, 0].astype(jnp.float32)
        ) + (r4[i, 1].astype(jnp.float32) + r4[i, 2].astype(jnp.float32))
    for op in small:
        op.wait_recv()
    total[...] = (s_buf[8] + s_buf[9]) + (s_buf[10] + s_buf[11])
    for op in ops:
        op.wait_send()


def backward(q_in, d_in, up, upt, gain, loss_part, hidden, slope, w_in, o_in, w_out, o_out):
    rows, width = 2 * q_in.shape[0], q_in.shape[1]
    half = w_in.shape[1]
    cols = 2 * half // CHUNKS
    groups = NX * NY * NZ
    bf, f32 = jnp.bfloat16, jnp.float32
    vmem = pl.BlockSpec(memory_space=pltpu.VMEM)
    hbm = pl.BlockSpec(memory_space=pl.ANY)
    return pl.pallas_call(
        backward_kernel,
        out_shape=(
            jax.ShapeDtypeStruct((GROUP, half), f32),
            jax.ShapeDtypeStruct((8, width), f32),
            jax.ShapeDtypeStruct((rows, width), bf),
        ),
        in_specs=[hbm] * 4 + [vmem] * 2 + [hbm] * 6,
        out_specs=[vmem] * 3,
        scratch_shapes=[
            pltpu.VMEM((rows, width), bf),
            pltpu.VMEM((rows, width), bf),
            pltpu.VMEM(upt.shape, bf),
            pltpu.VMEM((2, rows, half), bf),
            pltpu.VMEM((CHUNKS, rows, cols), bf),
            pltpu.VMEM((2,) + w_in.shape, bf),
            pltpu.VMEM((2,) + w_out.shape, bf),
            pltpu.VMEM((2, groups * GROUP, half), bf),
            pltpu.VMEM((2, groups * GROUP, half), bf),
            pltpu.VMEM((2, NX, NY, NZ, GROUP, half), bf),
            pltpu.VMEM((2, 2, RING - 1, RING, NZ, GROUP, WIDE), bf),
            pltpu.VMEM((2, 2, RING, NZ, GROUP, WIDE), bf),
            pltpu.VMEM((2, 2, RING - 1, NZ, GROUP, WIDE), bf),
            pltpu.VMEM((2, 2, NZ, GROUP, WIDE), bf),
            pltpu.VMEM((2, RING - 1, GROUP, WIDE), bf),
            pltpu.VMEM((RING - 1, NX, NY, GROUP, NARROW), bf),
            pltpu.VMEM((NX, NY, GROUP, NARROW), bf),
            pltpu.VMEM((RING - 1, NY, GROUP, NARROW), bf),
            pltpu.VMEM((NY, GROUP, NARROW), bf),
            pltpu.VMEM((RING - 1, GROUP, NARROW), bf),
            pltpu.VMEM((rows, width), f32),
            pltpu.VMEM((14, 8, width), f32),
            pltpu.SemaphoreType.DMA((2 * CHUNKS + 9,)),
            pltpu.SemaphoreType.DMA((2, 64)),
        ],
        compiler_params=pltpu.CompilerParams(
            collective_id=3, has_side_effects=True, vmem_limit_bytes=60 * MIB
        ),
        name="backward",
    )(
        q_in,
        d_in,
        up,
        upt,
        gain.reshape(1, width),
        loss_part,
        hidden,
        slope,
        w_in,
        o_in,
        w_out,
        o_out,
    )


def finish_kernel(down, total, grads, down_out, gain_out, loss_out, q_out, d_out):
    rows = q_out.shape[0]
    down_out[...] = down[...]
    gain_out[...] = total[0:1, :]
    loss_out[...] = total[1:2, 0:1] * (1.0 / (rows * 2 * NBLK))
    q_out[...] = grads[0:rows, :]
    d_out[...] = grads[rows : 2 * rows, :]


def finish(down, total, grads):
    rows, width = grads.shape[0] // 2, grads.shape[1]
    f32 = jnp.float32
    row_grads = jax.ShapeDtypeStruct((rows, width), grads.dtype)
    return pl.pallas_call(
        finish_kernel,
        out_shape=(
            jax.ShapeDtypeStruct(down.shape, f32),
            jax.ShapeDtypeStruct((1, width), f32),
            jax.ShapeDtypeStruct((1, 1), f32),
            row_grads,
            row_grads,
        ),
        name="finish",
    )(down, total, grads)


def on_device(query_in, doc_in, cluster, gain, w_in, w_out):
    width = query_in.shape[1]
    up, upt, loss_part, hidden, slope, o_in, o_out = layer(
        query_in, doc_in, gain, cluster, w_in, w_out
    )
    sums = backward(
        query_in, doc_in, up, upt, gain, loss_part, hidden, slope, w_in, o_in, w_out, o_out
    )
    down_t, gain_total, loss, q_grads, d_grads = finish(*sums)
    return (loss.reshape(()), down_t.T, gain_total.reshape(width), q_grads, d_grads)


def solution(mesh):
    in_specs = (
        P(("blk", "rep"), None),
        P(("blk", "rep"), None),
        P(("blk", "rep")),
        P(),
        P(None, "rep"),
        P("rep", None),
    )
    out_specs = (P(), P("rep", "blk"), P(), P(("blk", "rep"), None), P(("blk", "rep"), None))
    return jax.shard_map(
        on_device, mesh=mesh, in_specs=in_specs, out_specs=out_specs, check_vma=False
    )
```

```python
import math

import jax
import jax.numpy as jnp
from jax import lax
from jax.experimental import pallas as pl
from jax.experimental.pallas import tpu as pltpu
from jax.sharding import PartitionSpec as P

MESH = pl.DeviceIdType.MESH
MIB = 2**20
NX, NY, NZ, NC = 4, 4, 2, 2
NBLK = NX * NY * NZ * NC
RING = NX
EPSILON = 1e-06
SLOTS = 10
OWN = 4
GROUP = 16


def coords():
    b = lax.axis_index("blk")
    r = lax.axis_index("rep")
    return b // (NY * NZ * NC), (b // (NZ * NC)) % NY, (b // NC) % NZ, b % NC, r


def device(x, y, zl, c, r):
    return {"blk": ((x * NY + y) * NZ + zl) * NC + c, "rep": r}


def wrap(v, n):
    return lax.rem(v + n, n)


def greet(peers):
    barrier = pltpu.get_barrier_semaphore()
    for peer in peers:
        pl.semaphore_signal(barrier, inc=1, device_id=peer, device_id_type=MESH)
    pl.semaphore_wait(barrier, len(peers))


def remote(src, dst, send, recv, peer):
    return pltpu.make_async_remote_copy(
        src_ref=src,
        dst_ref=dst,
        send_sem=send,
        recv_sem=recv,
        device_id=peer,
        device_id_type=MESH,
    )


WBLK = 256
W_CHUNKS = 8
STRIP = 64


def nt(a, b):
    return lax.dot_general(a, b, (((1,), (1,)), ((), ())), preferred_element_type=jnp.float32)


def nn(a, b):
    return lax.dot_general(a, b, (((1,), (0,)), ((), ())), preferred_element_type=jnp.float32)


def gelu_both(p):
    k = math.sqrt(2.0 / math.pi)
    square = p * p
    t = jnp.tanh(p * (k + (k * 0.044715) * square))
    up = 0.5 + 0.5 * t
    slope = up + (0.5 * p) * ((1.0 - t * t) * (k + (3 * k * 0.044715) * square))
    return p * up, slope


def weight_view(in_ref, out_ref, block, chunk):
    if chunk < W_CHUNKS // 2:
        rows = in_ref.shape[0] // (W_CHUNKS // 2)
        return in_ref.at[
            pl.ds(chunk * rows, rows), pl.ds(pl.multiple_of(block * WBLK, WBLK), WBLK)
        ]
    rows = WBLK // (W_CHUNKS // 2)
    first = block * WBLK + (chunk - W_CHUNKS // 2) * rows
    return out_ref.at[pl.ds(pl.multiple_of(first, rows), rows)]


def forward_part(
    q_in,
    d_in,
    gain_ref,
    win_hbm,
    wout_hbm,
    hid_hbm,
    slope_hbm,
    oin_hbm,
    oout_hbm,
    win,
    wout,
    oin,
    oout,
    normed,
    hid,
    slope,
    pre,
    acc,
    local,
    stores,
    send,
    recv,
    meet,
):
    x, y, zl, c, r = coords()
    cross = device(x, y, 1 - zl, c, 1 - r)
    near = device(x, y, 1 - zl, c, r)
    ahead = device(wrap(x + 1, NX), y, zl, c, r)
    behind = device(wrap(x - 1, NX), y, zl, c, r)
    sibling = device(x, y, zl, 1 - c, r)
    half = win_hbm.shape[1]
    rows = q_in.shape[0]
    load_in = pltpu.make_async_copy(win_hbm, win, local.at[0])
    load_out = pltpu.make_async_copy(wout_hbm, wout, local.at[1])
    load_in.start()
    load_out.start()
    meet([ahead, behind])
    color = lax.rem(x + 2 * zl, 4)
    started = []

    def color_at(shift):
        return lax.rem(color + shift, 4)

    def block_of(shift):
        return 2 * color_at(shift) + c

    def copy(flow, block, chunk, peer, source=None):
        src = weight_view(*(source or (oin, oout)), block, chunk)
        dst = weight_view(oin, oout, block, chunk)
        return remote(src, dst, send.at[flow, chunk], recv.at[flow, chunk], peer)

    def start(*args):
        op = copy(*args)
        op.start()
        started.append(op)

    def first_hop(chunk):
        mine = block_of(0)
        copy(0, mine, chunk, cross).wait_recv()
        start(1, mine, chunk, ahead)
        start(2, mine, chunk, behind)
        start(3, mine, chunk, near)
        start(4, mine, chunk, sibling)

    def second_hop(chunk):
        for flow, shift in ((1, 3), (2, 1), (3, 2)):
            block = block_of(shift)
            copy(flow, block, chunk, near).wait_recv()
            start(4 + shift, block, chunk, sibling)

    def from_sibling(shift, chunks):
        block = 2 * color_at(shift) + (1 - c)
        for chunk in chunks:
            copy(4 + shift, block, chunk, sibling).wait_recv()

    stored = []

    def store(src, dst):
        op = pltpu.make_async_copy(src, dst, stores.at[len(stored)])
        op.start()
        stored.append(op)

    tile = 2 * WBLK

    def activate(block):
        def strip(i, _):
            at = pl.ds(pl.multiple_of(i * STRIP, STRIP), STRIP)
            h, s = gelu_both(pre[at, :])
            hid[block, at, :] = h.astype(jnp.bfloat16)
            slope[block, at, :] = s.astype(jnp.bfloat16)
            return 0

        lax.fori_loop(0, 2 * rows // STRIP, strip, 0)
        there = (block // 2, slice(None), pl.ds(pl.multiple_of((block % 2) * tile, tile), tile))
        store(hid.at[block], hid_hbm.at[there])
        store(slope.at[block], slope_hbm.at[there])

    def up_own(t):
        pre[...] = nn(normed[...], win[:, t * tile : (t + 1) * tile])
        activate(t)

    def down_own(t):
        step = nn(hid[t], wout[t * tile : (t + 1) * tile, :])
        acc[...] = step if t == 0 else acc[...] + step

    def up_other(shift):
        from_sibling(shift, range(W_CHUNKS // 2))
        at = pl.ds(pl.multiple_of(color_at(shift) * tile, tile), tile)
        pre[...] = nn(normed[...], oin[:, at])
        activate(half // tile + color_at(shift))
        store(oin.at[:, at], oin_hbm.at[:, at])

    def down_other(shift):
        from_sibling(shift, range(W_CHUNKS // 2, W_CHUNKS))
        at = pl.ds(pl.multiple_of(color_at(shift) * tile, tile), tile)
        acc[...] += nn(hid[half // tile + color_at(shift)], oout[at, :])
        store(oout.at[at, :], oout_hbm.at[at, :])

    for chunk in range(W_CHUNKS):
        start(0, block_of(2), chunk, cross, (win_hbm, wout_hbm))
    for k, ref in enumerate((q_in, d_in)):
        values = ref[...].astype(jnp.float32)
        inv_rms = lax.rsqrt(jnp.mean(values * values, axis=1, keepdims=True) + EPSILON)
        normed[k * rows : (k + 1) * rows, :] = ((values * inv_rms) * gain_ref[...]).astype(
            jnp.bfloat16
        )
    load_in.wait()
    up_own(0)
    first_hop(0)
    up_own(1)
    first_hop(1)
    second_hop(0)
    up_own(2)
    first_hop(2)
    second_hop(1)
    up_own(3)
    first_hop(3)
    second_hop(2)
    load_out.wait()
    down_own(0)
    down_own(1)
    first_hop(4)
    second_hop(3)
    up_other(0)
    first_hop(5)
    second_hop(4)
    up_other(1)
    first_hop(6)
    second_hop(5)
    up_other(2)
    first_hop(7)
    second_hop(6)
    up_other(3)
    second_hop(7)
    down_own(2)
    down_own(3)
    for shift in (0, 3, 1):
        down_other(shift)
    from_sibling(2, range(W_CHUNKS // 2, W_CHUNKS))
    last = pl.ds(pl.multiple_of(color_at(2) * tile, tile), tile)
    store(oout.at[last, :], oout_hbm.at[last, :])

    def embed(k):
        at = slice(k * rows, (k + 1) * rows)
        mixed = acc[at, :] + nn(hid[half // tile + color_at(2), at, :], oout[last, :])
        return ((q_in, d_in)[k][...].astype(jnp.float32) + mixed).astype(jnp.bfloat16)

    return embed, started, stored


PIECES = (
    (0, 0, 64, 0, 0),
    (1, 0, 16, 0, 0),
    (0, 64, 64, 1, 0),
    (0, 128, 80, 0, 0),
    (0, 208, 48, 1, 1),
    (2, 0, 64, 0, 0),
    (2, 64, 64, 1, 0),
    (2, 128, 80, 0, 0),
    (2, 208, 48, 1, 1),
)
DOC_PIECES = (0, 1, 2, 3, 4)
QUERY_PIECES = (5, 6, 7, 8)
DETOUR_ROWS = 48


def layer_kernel(*refs):
    ins, outs, scratch = refs[:6], refs[6:13], refs[13:]
    q_in, d_in, gain_ref, cluster, win_hbm, wout_hbm = ins
    up, upt, loss, hid_hbm, slope_hbm, oin_hbm, oout_hbm = outs
    forward_scratch, band_scratch = scratch[:13], scratch[13:]
    b = lax.axis_index("blk")
    zl = coords()[2]
    r = lax.axis_index("rep")
    step = NZ * NC * (1 - 2 * zl)
    onward = {"blk": wrap(b + step, NBLK), "rep": r}
    source = {"blk": wrap(b - step, NBLK), "rep": r}
    peers = []
    for offset in range(-2, 3):
        for other in range(2):
            if offset or other:
                rep = 1 - r if other else r
                peers.append((offset, other, {"blk": wrap(b + offset, NBLK), "rep": rep}))

    def meet(more):
        greet([peer for _, _, peer in peers] + [onward, source] + more)

    embed, started, stored = forward_part(
        q_in,
        d_in,
        gain_ref,
        win_hbm,
        wout_hbm,
        hid_hbm,
        slope_hbm,
        oin_hbm,
        oout_hbm,
        *forward_scratch,
        meet,
    )
    band_part(cluster, up, upt, loss, *band_scratch, embed, peers, onward, source)
    for op in started:
        op.wait_send()
    for op in stored:
        op.wait()


def band_part(
    cluster,
    up,
    upt,
    loss,
    gd,
    gx,
    gq,
    transit,
    s,
    w,
    lt,
    mine,
    acc,
    column_tag,
    up_v,
    upt_v,
    local,
    send,
    recv,
    tsem,
    embed,
    peers,
    onward,
    source,
):
    x, y, zl, c, r = coords()
    rows, width = gd.shape[1:]
    tag = cluster[...].astype(jnp.float32)
    column_tag[...] = jnp.transpose(jnp.broadcast_to(tag, (128, rows)))
    inv_root = 1.0 / math.sqrt(width)
    cross = device(x, y, 1 - zl, c, 1 - r)
    near = device(x, y, 1 - zl, c, r)
    sibling = device(x, y, zl, 1 - c, r)

    def view(slot, p):
        kind, first, count = PIECES[p][:3]
        return (gd, gx, gq)[kind].at[slot, pl.ds(first, count)]

    def own(p):
        return view(OWN, p)

    z_slot = 8 - 8 * zl
    far_slot = 8 * zl
    theirs = 8 * zl
    started = []

    def make(flow, p, src, dst, peer):
        return remote(src, dst, send.at[flow, p], recv.at[flow, p], peer)

    def start(*args):
        op = make(*args)
        op.start()
        started.append(op)

    def arrived(flow, p, slot):
        make(flow, p, view(slot, p), view(slot, p), near).wait_recv()

    def band_to_sibling(p):
        return [
            make(7 + k, p, view(8 - 8 * c + k, p), view(6 - 4 * c + k, p), sibling)
            for k in range(2)
        ]

    def through(p):
        return transit.at[p // 5]

    def send_own(p):
        start(0, p, own(p), view(theirs, p), near)
        start(1, p, own(p), view(theirs + 1, p), cross)
        if PIECES[p][4]:
            start(9, p, own(p), through(p), source)
        start(5, p, own(p), view(2 + 4 * c, p), sibling)

    def from_z(p):
        by_near, detour = PIECES[p][3:]
        arrived(0, p, z_slot)
        if not detour:
            start(3, p, view(z_slot, p), view(far_slot, p), onward)
        if not by_near:
            start(2, p, view(z_slot, p), view(OWN + 1, p), cross)
        arrived(1, p, z_slot + 1)
        if not detour:
            start(4, p, view(z_slot + 1, p), view(far_slot + 1, p), onward)
        if by_near:
            start(2, p, view(z_slot + 1, p), view(OWN + 1, p), near)

        @pl.when(c == zl)
        def _():
            for op in band_to_sibling(p):
                op.start()

    def from_transit(p):
        if PIECES[p][4]:
            make(9, p, own(p), through(p), source).wait_recv()
            start(10, p, through(p), view(8 - 8 * zl, p), near)
            start(11, p, through(p), view(8 - 8 * zl + 1, p), cross)

    def from_rep(p):
        arrived(2, p, OWN + 1)
        start(6, p, view(OWN + 1, p), view(3 + 4 * c, p), sibling)

    def from_far(p):
        detour = PIECES[p][4]
        arrived(10 if detour else 3, p, far_slot)
        arrived(11 if detour else 4, p, far_slot + 1)

        @pl.when(c != zl)
        def _():
            for op in band_to_sibling(p):
                op.start()

    def from_sibling(p):
        arrived(5, p, 6 - 4 * c)
        arrived(6, p, 7 - 4 * c)

    def band_from_sibling(p):
        arrived(7, p, 2 + 4 * c)
        arrived(8, p, 3 + 4 * c)

    def hand_out(k, value):
        up_v[k] = value
        turned = jnp.transpose(value).reshape(width // (NC * GROUP), NC, GROUP, rows)
        for core in range(NC):
            upt_v[k, core] = turned[:, core].reshape(width // NC, rows)
        ops = [
            pltpu.make_async_copy(up_v.at[k], up.at[pl.ds(k * rows, rows)], local.at[2 * k]),
            pltpu.make_async_copy(upt_v.at[k], upt.at[k], local.at[1 + 2 * k]),
        ]
        for op in ops:
            op.start()
        return ops

    row = lax.broadcasted_iota(jnp.int32, (rows, rows), 0)
    col = lax.broadcasted_iota(jnp.int32, (rows, rows), 1)
    diagonal = row == col

    def masked(a, g, slot):
        scores = nt(a[OWN], g[slot]) * inv_root
        tag_row = gx[slot].astype(jnp.float32)[0:1, :]
        allowed = tag_row != column_tag[:, 0:1]
        if isinstance(slot, int) and slot == OWN:
            allowed = allowed | diagonal
        return scores, jnp.where(allowed, scores, -jnp.inf)

    def score(slot):
        s[slot] = masked(gq, gd, slot)[1]

    def backward_of(slot):
        m = masked(gd, gq, slot)[1]
        wt = jnp.exp(m - lt[slot, 0:1, :])
        if isinstance(slot, int) and slot == OWN:
            wt = wt - diagonal.astype(jnp.float32)
        acc[...] += nn(wt.astype(jnp.bfloat16), gq[slot])

    gx[OWN] = jnp.broadcast_to(tag, gx.shape[1:]).astype(jnp.bfloat16)
    gd[OWN] = embed(1)
    for p in DOC_PIECES:
        send_own(p)
    gq[OWN] = embed(0)
    for p in DOC_PIECES:
        from_z(p)
    for p in QUERY_PIECES:
        send_own(p)
    for p in DOC_PIECES:
        from_transit(p)
    score(OWN)
    positive = jnp.sum(jnp.where(diagonal, s[OWN], 0.0), axis=1, keepdims=True)
    score(z_slot)
    score(z_slot + 1)
    for p in DOC_PIECES:
        from_rep(p)
    for p in DOC_PIECES[:3]:
        from_far(p)
    from_z(QUERY_PIECES[0])
    for p in DOC_PIECES[3:]:
        from_far(p)
    for p in DOC_PIECES:
        from_sibling(p)
    from_z(QUERY_PIECES[1])
    score(OWN + 1)
    score(6 - 4 * c)
    score(7 - 4 * c)
    score(far_slot)
    score(far_slot + 1)
    from_z(QUERY_PIECES[2])
    for p in DOC_PIECES:
        band_from_sibling(p)
    score(2 + 4 * c)
    score(3 + 4 * c)
    top = s[0]
    for slot in range(1, SLOTS):
        top = jnp.maximum(top, s[slot])
    row_max = jnp.max(top, axis=1, keepdims=True)
    total = jnp.exp(s[0] - row_max)
    for slot in range(1, SLOTS):
        total = total + jnp.exp(s[slot] - row_max)
    log_total = row_max + jnp.log(jnp.sum(total, axis=1, keepdims=True))
    loss[...] = jnp.broadcast_to(
        jnp.sum(log_total - positive, axis=0, keepdims=True), loss.shape
    )
    mine[...] = jnp.transpose(jnp.broadcast_to(log_total, (rows, 128)))[0:8, :]
    lt[OWN] = mine[...]
    tops = []
    for i, (offset, other, peer) in enumerate(peers):
        slot = (2 - offset) * 2 + other
        op = remote(mine, lt.at[slot], tsem.at[0, i], tsem.at[1, slot], peer)
        op.start()
        tops.append(op)
    from_z(QUERY_PIECES[3])
    for p in QUERY_PIECES:
        from_transit(p)
    for slot in range(SLOTS):
        wt = jnp.exp(s[slot] - log_total)
        if slot == OWN:
            wt = wt - diagonal.astype(jnp.float32)
        w[:, slot * rows : (slot + 1) * rows] = wt.astype(jnp.bfloat16)
    query_grad = nn(w[...], gd[...].reshape(SLOTS * rows, width))
    outs = hand_out(0, (query_grad * inv_root).astype(jnp.bfloat16))

    for slot in range(SLOTS):
        if slot != OWN:
            remote(mine, lt.at[slot], tsem.at[0, 0], tsem.at[1, slot], near).wait_recv()
    for p in QUERY_PIECES:
        from_rep(p)
    acc[...] = jnp.zeros_like(acc)
    backward_of(OWN)
    backward_of(z_slot)
    backward_of(z_slot + 1)
    backward_of(OWN + 1)
    for p in QUERY_PIECES:
        from_sibling(p)
    backward_of(6 - 4 * c)
    backward_of(7 - 4 * c)
    for p in QUERY_PIECES:
        from_far(p)
    backward_of(far_slot)
    backward_of(far_slot + 1)
    for p in QUERY_PIECES:
        band_from_sibling(p)
    backward_of(2 + 4 * c)
    backward_of(3 + 4 * c)
    outs += hand_out(1, (acc[...] * inv_root).astype(jnp.bfloat16))

    for p in range(len(PIECES)):
        for op in band_to_sibling(p):
            op.wait_send()
    for op in started + tops:
        op.wait_send()
    for op in outs:
        op.wait()


def layer(q_in, d_in, gain, cluster, w_in, w_out):
    rows, width = q_in.shape
    half = w_in.shape[1]
    bf, f32 = jnp.bfloat16, jnp.float32
    tile = 2 * WBLK
    vmem = pl.BlockSpec(memory_space=pltpu.VMEM)
    hbm = pl.BlockSpec(memory_space=pl.ANY)
    per_chunk = jax.ShapeDtypeStruct((CHUNKS, 2 * rows, 2 * half // CHUNKS), bf)
    return pl.pallas_call(
        layer_kernel,
        out_shape=(
            jax.ShapeDtypeStruct((2 * rows, width), bf),
            jax.ShapeDtypeStruct((2, NC, width // NC, rows), bf),
            jax.ShapeDtypeStruct((8, 128), f32),
            per_chunk,
            per_chunk,
            jax.ShapeDtypeStruct(w_in.shape, bf),
            jax.ShapeDtypeStruct(w_out.shape, bf),
        ),
        in_specs=[vmem] * 4 + [hbm] * 2,
        out_specs=[hbm, hbm, vmem] + [hbm] * 4,
        scratch_shapes=[
            pltpu.VMEM(w_in.shape, bf),
            pltpu.VMEM(w_out.shape, bf),
            pltpu.VMEM(w_in.shape, bf),
            pltpu.VMEM(w_out.shape, bf),
            pltpu.VMEM((2 * rows, width), bf),
            pltpu.VMEM((2 * half // tile, 2 * rows, tile), bf),
            pltpu.VMEM((2 * half // tile, 2 * rows, tile), bf),
            pltpu.VMEM((2 * rows, tile), f32),
            pltpu.VMEM((2 * rows, width), f32),
            pltpu.SemaphoreType.DMA((2,)),
            pltpu.SemaphoreType.DMA((2 * 2 * half // tile + 8,)),
            pltpu.SemaphoreType.DMA((8, W_CHUNKS)),
            pltpu.SemaphoreType.DMA((8, W_CHUNKS)),
            pltpu.VMEM((SLOTS, rows, width), bf),
            pltpu.VMEM((SLOTS, 16, rows), bf),
            pltpu.VMEM((SLOTS, rows, width), bf),
            pltpu.VMEM((2, DETOUR_ROWS, width), bf),
            pltpu.VMEM((SLOTS, rows, rows), f32),
            pltpu.VMEM((rows, SLOTS * rows), bf),
            pltpu.VMEM((SLOTS, 8, rows), f32),
            pltpu.VMEM((8, rows), f32),
            pltpu.VMEM((rows, width), f32),
            pltpu.VMEM((rows, 128), f32),
            pltpu.VMEM((2, rows, width), bf),
            pltpu.VMEM((2, NC, width // NC, rows), bf),
            pltpu.SemaphoreType.DMA((4,)),
            pltpu.SemaphoreType.DMA((12, len(PIECES))),
            pltpu.SemaphoreType.DMA((12, len(PIECES))),
            pltpu.SemaphoreType.DMA((2, SLOTS)),
        ],
        compiler_params=pltpu.CompilerParams(
            collective_id=0, has_side_effects=True, vmem_limit_bytes=60 * MIB
        ),
        name="layer",
    )(q_in, d_in, gain.reshape(1, width), cluster.reshape(1, rows), w_in, w_out)


PARTS = (
    (0, 0, 768, "x"),
    (0, 768, 768, "y"),
    (0, 1536, 512, "z"),
    (1, 0, 768, "x"),
    (1, 768, 768, "y"),
    (1, 1536, 512, "z"),
)
WIDE, NARROW = 768, 512
CHUNKS = 4


def backward_kernel(
    q_hbm,
    d_hbm,
    up_hbm,
    upt_hbm,
    gain_ref,
    loss_ref,
    hid_hbm,
    slope_hbm,
    win_hbm,
    oin_hbm,
    wout_hbm,
    oout_hbm,
    out,
    total,
    grads,
    in_v,
    up_ref,
    upt_ref,
    hid,
    slope,
    win,
    wout,
    s1,
    r1,
    a1,
    r2,
    a2,
    r3,
    a3,
    r4,
    r2z,
    a2z,
    r3z,
    a3z,
    r4z,
    acc,
    s_buf,
    local,
    sems,
):
    x, y, zl, c, r = coords()
    rows, width = q_hbm.shape
    half = win_hbm.shape[1]
    cols = 2 * half // CHUNKS
    per_half = CHUNKS // 2
    sibling = device(x, y, zl, 1 - c, r)
    xs = [device(wrap(x + k, NX), y, zl, c, r) for k in range(1, RING)]
    ys = [device(x, wrap(y + k, NY), zl, c, r) for k in range(1, RING)]
    zs = [device(x, y, 1 - zl, c, r), device(x, y, zl, c, 1 - r), device(x, y, 1 - zl, c, 1 - r)]

    loads = []
    n_loads = [0]

    def load(src, dst):
        nonlocal loads
        op = pltpu.make_async_copy(src, dst, local.at[n_loads[0]])
        op.start()
        n_loads[0] += 1
        loads.append(op)
        return op

    first_loads = [load(upt_hbm.at[k], upt_ref.at[k]) for k in range(2)]
    loads = []
    for j in range(CHUNKS):
        load(hid_hbm.at[j], hid.at[j // per_half, :, pl.ds(j % per_half * cols, cols)])
    for j in range(CHUNKS):
        load(slope_hbm.at[j], slope.at[j])
    for k, (inner, outer) in enumerate(((win_hbm, wout_hbm), (oin_hbm, oout_hbm))):
        load(inner, win.at[k])
        load(outer, wout.at[k])
    late_loads = [
        load(up_hbm, up_ref),
        load(q_hbm, in_v.at[pl.ds(0, rows)]),
        load(d_hbm, in_v.at[pl.ds(rows, rows)]),
    ]

    greet([sibling] + xs + ys + zs)
    state = {"n": 0}
    ops = []

    def send(src, dst, peer):
        n = state["n"]
        state["n"] = n + 1
        op = remote(src, dst, sems.at[0, n], sems.at[1, n], peer)
        op.start()
        ops.append(op)
        return op

    def down_part(core, k, at):
        return nn(upt_ref[0, core], hid[k, 0:rows, at]) + nn(upt_ref[1, core], hid[k, rows:, at])

    wait1 = []
    for op in first_loads:
        op.wait()
    loaded = []

    def for_sibling(p):
        k, first, count, _ = PARTS[p]
        at = slice(first, first + count)
        while len(loaded) * cols < k * half + first + count:
            loads[len(loaded)].wait()
            loaded.append(1)
        s1[k, :, at] = down_part(1 - c, k, at).astype(jnp.bfloat16)
        view = (k, slice(None), pl.ds(first, count))
        wait1.append(send(s1.at[view], r1.at[view], sibling))

    wait2 = []
    waitz = []

    def for_links(p):
        k, first, count, axis = PARTS[p]
        at = slice(first, first + count)
        mine = down_part(c, k, at)
        wait1[p].wait_recv()
        mine = mine + r1[k, :, at].astype(jnp.float32)
        a1[k, :, :, :, :, at] = mine.astype(jnp.bfloat16).reshape(NX, NY, NZ, GROUP, count)
        part = pl.ds(first, count)
        waits = []
        if axis == "z":
            if k == 0:
                waitz.append(send(a1.at[k, :, :, 1 - zl, :, part], r2z.at[0], zs[0]))
            else:
                waitz.append(send(a1.at[k, :, :, zl, :, part], r2z.at[1], zs[1]))
                waitz.append(send(a1.at[k, :, :, 1 - zl, :, part], r2z.at[2], zs[2]))
        for n in range(1, RING):
            slot = RING - 1 - n
            if axis == "x":
                src = a1.at[k, wrap(x + n, NX), :, :, :, part]
                waits.append(send(src, r2.at[k, 0, slot], xs[n - 1]))
            elif axis == "y":
                src = a1.at[k, :, wrap(y + n, NY), :, :, part]
                waits.append(send(src, r2.at[k, 1, slot], ys[n - 1]))
        wait2.append(waits)

    ahead = 3
    for p in range(len(PARTS) + ahead):
        if p < len(PARTS):
            for_sibling(p)
        if p >= ahead:
            for_links(p - ahead)

    for j in range(CHUNKS):
        loads[CHUNKS + j].wait()
    for k in range(2):
        loads[2 * CHUNKS + 2 * k].wait()
        loads[2 * CHUNKS + 2 * k + 1].wait()
    for op in late_loads:
        op.wait()
    tile = 512
    for j in range(CHUNKS):
        k = j // per_half

        def tile_step(t, _, j=j, k=k):
            first = pl.multiple_of(t * tile, tile)
            there = pl.multiple_of((j % per_half) * cols + t * tile, tile)
            g_act = nt(up_ref[...], wout[k, pl.ds(there, tile), :])
            g_pre = (g_act * slope[j, :, pl.ds(first, tile)].astype(jnp.float32)).astype(
                jnp.bfloat16
            )
            step = nt(g_pre, win[k, :, pl.ds(there, tile)])
            if j == 0:
                before = jnp.where(t == 0, 0.0, acc[...])
            else:
                before = acc[...]
            acc[...] = before + step
            return 0

        if j == 0:
            acc[...] = jnp.zeros_like(acc)
        lax.fori_loop(0, cols // tile, tile_step, 0)

    values = in_v[...].astype(jnp.float32)
    inv_rms = lax.rsqrt(jnp.mean(values * values, axis=1, keepdims=True) + EPSILON)
    unit_rows = values * inv_rms
    g_norm = acc[...]
    weighted = g_norm * unit_rows
    gain_term = jnp.sum(weighted, axis=0, keepdims=True)
    gain = gain_ref[...]
    mean = jnp.mean(weighted * gain, axis=1, keepdims=True)
    d_values = inv_rms * (g_norm * gain - unit_rows * mean)
    grads[...] = (up_ref[...].astype(jnp.float32) + d_values).astype(jnp.bfloat16)

    row = lax.broadcasted_iota(jnp.int32, (8, width), 0)
    s_buf[12] = jnp.where(
        row == 0,
        jnp.broadcast_to(gain_term, (8, width)),
        jnp.broadcast_to(loss_ref[0:1, 0:1], (8, width)),
    )
    small = send(s_buf.at[12], s_buf.at[13], sibling)
    small.wait_recv()
    s_buf[x] = s_buf[12] + s_buf[13]
    small = [send(s_buf.at[x], s_buf.at[x], peer) for peer in xs]

    wait3 = {}

    def second(p):
        k, first, count, axis = PARTS[p]
        at = slice(first, first + count)
        i = 0 if axis == "x" else 1
        for op in wait2[p]:
            op.wait_recv()
        tot = (a1[k, x, :, :, :, at] if i == 0 else a1[k, :, y, :, :, at]).astype(jnp.float32)
        for n in range(RING - 1):
            tot = tot + r2[k, i, n].astype(jnp.float32)
        a2[k, i] = tot.astype(jnp.bfloat16)
        wait3[p] = []
        for n in range(1, RING):
            slot = RING - 1 - n
            if i == 0:
                op = send(a2.at[k, i, wrap(y + n, NY)], r3.at[k, i, slot], ys[n - 1])
            else:
                op = send(a2.at[k, i, wrap(x + n, NX)], r3.at[k, i, slot], xs[n - 1])
            wait3[p].append(op)

    def second_z():
        k, first, count, _ = PARTS[2]
        for op in waitz:
            op.wait_recv()
        tot = a1[k, :, :, zl, :, first : first + count].astype(jnp.float32)
        for n in range(RING - 1):
            tot = tot + r2z[n].astype(jnp.float32)
        a2z[...] = tot.astype(jnp.bfloat16)
        return [
            send(a2z.at[wrap(x + n, NX)], r3z.at[RING - 1 - n], xs[n - 1]) for n in range(1, RING)
        ]

    def third_z(waits):
        for op in waits:
            op.wait_recv()
        tot = a2z[x].astype(jnp.float32)
        for n in range(RING - 1):
            tot = tot + r3z[n].astype(jnp.float32)
        a3z[...] = tot.astype(jnp.bfloat16)
        return [
            send(a3z.at[wrap(y + n, NY)], r4z.at[RING - 1 - n], ys[n - 1]) for n in range(1, RING)
        ]

    second(0)
    second(1)
    for op in small:
        op.wait_recv()
    s_buf[4 + y] = ((s_buf[0] + s_buf[1]) + s_buf[2]) + s_buf[3]
    small = [send(s_buf.at[4 + y], s_buf.at[4 + y], peer) for peer in ys]
    waitz = second_z()
    second(3)
    second(4)
    waitz = third_z(waitz)

    for op in small:
        op.wait_recv()
    here = s_buf.at[8 + 2 * r + zl]
    here[...] = ((s_buf[4] + s_buf[5]) + s_buf[6]) + s_buf[7]
    small = [send(here, here, peer) for peer in zs]

    wait4 = [[], []]
    for p in (0, 1, 3, 4):
        k, first, count, axis = PARTS[p]
        i = 0 if axis == "x" else 1
        for op in wait3[p]:
            op.wait_recv()
        tot = (a2[k, i, y] if i == 0 else a2[k, i, x]).astype(jnp.float32)
        for n in range(RING - 1):
            tot = tot + r3[k, i, n].astype(jnp.float32)
        a3[k, i] = tot.astype(jnp.bfloat16)
        if k == 0:
            wait4[i].append(send(a3.at[k, i, 1 - zl], r4.at[i, 0], zs[0]))
        else:
            wait4[i].append(send(a3.at[k, i, zl], r4.at[i, 1], zs[1]))
            wait4[i].append(send(a3.at[k, i, 1 - zl], r4.at[i, 2], zs[2]))
    for op in waitz:
        op.wait_recv()
    first = PARTS[2][1]
    tot = a3z[y].astype(jnp.float32)
    for n in range(RING - 1):
        tot = tot + r4z[n].astype(jnp.float32)
    out[:, first : first + NARROW] = tot
    for i in range(2):
        for op in wait4[i]:
            op.wait_recv()
        out[:, i * WIDE : (i + 1) * WIDE] = (
            a3[0, i, zl].astype(jnp.float32) + r4[i, 0].astype(jnp.float32)
        ) + (r4[i, 1].astype(jnp.float32) + r4[i, 2].astype(jnp.float32))
    for op in small:
        op.wait_recv()
    total[...] = (s_buf[8] + s_buf[9]) + (s_buf[10] + s_buf[11])
    for op in ops:
        op.wait_send()


def backward(q_in, d_in, up, upt, gain, loss_part, hidden, slope, w_in, o_in, w_out, o_out):
    rows, width = 2 * q_in.shape[0], q_in.shape[1]
    half = w_in.shape[1]
    cols = 2 * half // CHUNKS
    groups = NX * NY * NZ
    bf, f32 = jnp.bfloat16, jnp.float32
    vmem = pl.BlockSpec(memory_space=pltpu.VMEM)
    hbm = pl.BlockSpec(memory_space=pl.ANY)
    return pl.pallas_call(
        backward_kernel,
        out_shape=(
            jax.ShapeDtypeStruct((GROUP, half), f32),
            jax.ShapeDtypeStruct((8, width), f32),
            jax.ShapeDtypeStruct((rows, width), bf),
        ),
        in_specs=[hbm] * 4 + [vmem] * 2 + [hbm] * 6,
        out_specs=[vmem] * 3,
        scratch_shapes=[
            pltpu.VMEM((rows, width), bf),
            pltpu.VMEM((rows, width), bf),
            pltpu.VMEM(upt.shape, bf),
            pltpu.VMEM((2, rows, half), bf),
            pltpu.VMEM((CHUNKS, rows, cols), bf),
            pltpu.VMEM((2,) + w_in.shape, bf),
            pltpu.VMEM((2,) + w_out.shape, bf),
            pltpu.VMEM((2, groups * GROUP, half), bf),
            pltpu.VMEM((2, groups * GROUP, half), bf),
            pltpu.VMEM((2, NX, NY, NZ, GROUP, half), bf),
            pltpu.VMEM((2, 2, RING - 1, RING, NZ, GROUP, WIDE), bf),
            pltpu.VMEM((2, 2, RING, NZ, GROUP, WIDE), bf),
            pltpu.VMEM((2, 2, RING - 1, NZ, GROUP, WIDE), bf),
            pltpu.VMEM((2, 2, NZ, GROUP, WIDE), bf),
            pltpu.VMEM((2, RING - 1, GROUP, WIDE), bf),
            pltpu.VMEM((RING - 1, NX, NY, GROUP, NARROW), bf),
            pltpu.VMEM((NX, NY, GROUP, NARROW), bf),
            pltpu.VMEM((RING - 1, NY, GROUP, NARROW), bf),
            pltpu.VMEM((NY, GROUP, NARROW), bf),
            pltpu.VMEM((RING - 1, GROUP, NARROW), bf),
            pltpu.VMEM((rows, width), f32),
            pltpu.VMEM((14, 8, width), f32),
            pltpu.SemaphoreType.DMA((2 * CHUNKS + 9,)),
            pltpu.SemaphoreType.DMA((2, 64)),
        ],
        compiler_params=pltpu.CompilerParams(
            collective_id=3, has_side_effects=True, vmem_limit_bytes=60 * MIB
        ),
        name="backward",
    )(
        q_in,
        d_in,
        up,
        upt,
        gain.reshape(1, width),
        loss_part,
        hidden,
        slope,
        w_in,
        o_in,
        w_out,
        o_out,
    )


def finish_kernel(down, total, grads, down_out, gain_out, loss_out, q_out, d_out):
    rows = q_out.shape[0]
    down_out[...] = down[...]
    gain_out[...] = total[0:1, :]
    loss_out[...] = total[1:2, 0:1] * (1.0 / (rows * 2 * NBLK))
    q_out[...] = grads[0:rows, :]
    d_out[...] = grads[rows : 2 * rows, :]


def finish(down, total, grads):
    rows, width = grads.shape[0] // 2, grads.shape[1]
    f32 = jnp.float32
    row_grads = jax.ShapeDtypeStruct((rows, width), grads.dtype)
    return pl.pallas_call(
        finish_kernel,
        out_shape=(
            jax.ShapeDtypeStruct(down.shape, f32),
            jax.ShapeDtypeStruct((1, width), f32),
            jax.ShapeDtypeStruct((1, 1), f32),
            row_grads,
            row_grads,
        ),
        name="finish",
    )(down, total, grads)


def on_device(query_in, doc_in, cluster, gain, w_in, w_out):
    width = query_in.shape[1]
    up, upt, loss_part, hidden, slope, o_in, o_out = layer(
        query_in, doc_in, gain, cluster, w_in, w_out
    )
    sums = backward(
        query_in, doc_in, up, upt, gain, loss_part, hidden, slope, w_in, o_in, w_out, o_out
    )
    down_t, gain_total, loss, q_grads, d_grads = finish(*sums)
    return (loss.reshape(()), down_t.T, gain_total.reshape(width), q_grads, d_grads)


def solution(mesh):
    in_specs = (
        P(("blk", "rep"), None),
        P(("blk", "rep"), None),
        P(("blk", "rep")),
        P(),
        P(None, "rep"),
        P("rep", None),
    )
    out_specs = (P(), P("rep", "blk"), P(), P(("blk", "rep"), None), P(("blk", "rep"), None))
    return jax.shard_map(
        on_device, mesh=mesh, in_specs=in_specs, out_specs=out_specs, check_vma=False
    )
```
